512 devices in a mesh: row: 64 (over z_lo, x, y), col: 8 (over z_hi, core).
Axes of the slice: x: 4, y: 4, z: 16 (z_hi: 4, z_lo: 4; z = z_hi * 4 + z_lo), core: 2. Of those that a mesh axis runs over, the one named last changes fastest.
Arguments:
- features: bfloat16 [64, 32768], P(None, ('row', 'col')), may hold values from -6 to 6
- inv_scale: float32 [64], replicated, may hold values from 0.05 to 0.6
- pivots: int32 [64], replicated, may hold values from 0 to 32767, as said below
- solution: float32 [32, 32768], P(None, ('row', 'col')), may hold values from -6 to 6
- residual: float32 [32, 32768], P(None, ('row', 'col')), may hold values from -16 to 16
- direction: float32 [32, 32768], P(None, ('row', 'col')), may hold values from -16 to 16
Outputs:
- solution_out: float32 [32, 32768], P(None, ('row', 'col'))
- residual_out: float32 [32, 32768], P(None, ('row', 'col'))
- direction_out: float32 [32, 32768], P(None, ('row', 'col'))
- slope_image: float32 [32, 32768], P(None, ('row', 'col'))
The draws below stay inside these ranges and needn't reach their ends.
Inputs may be any that keep to these rules, and one draw needn't show every extreme that they name: `pivots`: distinct; exactly one pivot in each aligned run of 512 samples, in no particular order.
All inputs are finite; a program needn't handle non-finite values.
Results may differ from the reference program's by a relative error of at most 0.019.
Values may be sent and summed in bfloat16 or wider, within the bound.
A program may use at most 64 MiB of HBM per device.

```python
import math
import jax
import jax.numpy as jnp
from jax import lax

D = 64
RHS = 32
RANK = 64
SAMPLES = 32768


def profile(key, reach):
    position = jnp.arange(SAMPLES, dtype=jnp.float32) / (SAMPLES - 1)
    row_scale = 10.0 ** (reach * (2.0 * position - 1.0))
    col_scale = 10.0 ** jax.random.uniform(key, (RHS, 1), jnp.float32, -0.5, 0.5)
    return row_scale[None, :] * col_scale


def draw_pivots(key, part):
    key = jax.random.fold_in(key, 11)
    first, second = jax.random.split(key)
    run = SAMPLES // RANK
    offsets = jax.random.randint(first, (RANK,), 0, run)
    counter = jnp.arange(RANK, dtype=jnp.int32)
    offsets = jnp.where(counter == 0, 0, jnp.where(counter == RANK - 1, run - 1, offsets))
    base = counter * run + offsets
    order = jax.random.permutation(second, RANK)
    return base[order].astype(jnp.int32)


def draw_residual(key, part):
    key = jax.random.fold_in(key, 21)
    first, second = jax.random.split(key, 2)
    values = jax.random.normal(first, (RHS, SAMPLES), jnp.float32) * profile(second, 0.5)
    return jnp.clip(values, -16.0, 16.0)


def draw_direction(key, part):
    key = jax.random.fold_in(key, 31)
    first, second = jax.random.split(key, 2)
    values = jax.random.normal(first, (RHS, SAMPLES), jnp.float32) * profile(second, 0.5)
    return jnp.clip(values, -16.0, 16.0)


def block_levels(key, shape, cuts, smallest, top_value):
    loudness = 1.0
    for axis_at, shards_of in cuts:
        steps = jax.random.uniform(jax.random.fold_in(jax.random.fold_in(key, 6), axis_at), (shards_of,), jnp.float32, smallest / len(cuts), top_value / len(cuts))
        loudness = loudness * jnp.repeat(jnp.exp(steps), shape[axis_at] // shards_of).reshape((-1,) + (1,) * (len(shape) - 1 - axis_at))
    return loudness


def noise(key, shape, deviation, bound, cuts=(), held_as=jnp.bfloat16):
    values = jax.random.normal(key, shape, jnp.float32) * deviation
    if len(cuts) > 0:
        values = block_levels(key, shape, cuts, -0.22, 0.18) * values
    return jnp.clip(values, min=-bound, max=bound).astype(held_as)


def setup_inputs(seed: int = 0) -> dict:
    key_list = jax.random.split(jax.random.key(seed), 7)
    return {
        "features": noise(key_list[0], (D, SAMPLES), 1.0, 6.0, ((1, 512),)),
        "inv_scale": jnp.clip(jnp.exp(jax.random.uniform(key_list[1], (D,), jnp.float32, math.log(0.05), math.log(0.6))), 0.05, 0.6),
        "pivots": draw_pivots(jax.random.fold_in(key_list[6], 71), 0),
        "solution": noise(key_list[3], (RHS, SAMPLES), 1.0, 6.0, ((1, 512),), jnp.float32),
        "residual": draw_residual(jax.random.fold_in(key_list[6], 71), 0),
        "direction": draw_direction(jax.random.fold_in(key_list[6], 71), 0),
    }


noise_var = 1.0
highest = lax.Precision.HIGHEST

def scale_features(features, inv_scale):
    return (features.astype(jnp.float32) * inv_scale[:, None]).astype(jnp.bfloat16)

def square_norms(scaled_wide):
    return jnp.sum(scaled_wide * scaled_wide, axis=0)

def kernel_pairs(left, left_norm, right, right_norm):
    products = jnp.dot(left.T, right, precision=highest)
    distance = left_norm[:, None] + right_norm[None, :] - 2.0 * products
    return (jnp.exp(-0.5 * distance), distance)

def round_half(values):
    return lax.optimization_barrier(values.astype(jnp.bfloat16)).astype(jnp.float32)

def reference(features, inv_scale, pivots, solution, residual, direction):
    scaled = scale_features(features, inv_scale)
    scaled_wide = scaled.astype(jnp.float32)
    sq_norm = square_norms(scaled_wide)
    samples = scaled.shape[1]
    columns = direction.shape[0]
    block = math.gcd(samples, 512)
    dir_wide = round_half(direction)

    def one_block(index):
        row_feat = lax.dynamic_slice_in_dim(scaled_wide, index * block, block, 1)
        row_norm = lax.dynamic_slice_in_dim(sq_norm, index * block, block, 0)
        kernel_tile, distance = kernel_pairs(scaled_wide, sq_norm, row_feat, row_norm)
        kernel_term = jnp.dot(dir_wide, round_half(kernel_tile), precision=highest)
        slope_term = jnp.dot(dir_wide, round_half(kernel_tile * distance), precision=highest)
        return (kernel_term, slope_term)
    indices = jnp.arange(samples // block, dtype=jnp.int32)
    kernel_terms, slope_terms = lax.map(one_block, indices)
    kernel_image = jnp.transpose(kernel_terms, (1, 0, 2)).reshape(columns, samples)
    slope_image = jnp.transpose(slope_terms, (1, 0, 2)).reshape(columns, samples)
    image = kernel_image + noise_var * direction
    pivot_feat = scaled_wide[:, pivots]
    pivot_norm = sq_norm[pivots]
    pivot_kernel, unused_one = kernel_pairs(pivot_feat, pivot_norm, scaled_wide, sq_norm)
    pivot_self, unused_two = kernel_pairs(pivot_feat, pivot_norm, pivot_feat, pivot_norm)
    gram = noise_var * pivot_self + jnp.dot(pivot_kernel, pivot_kernel.T, precision=highest)
    factor = jnp.linalg.cholesky(gram)

    def precondition(values):
        projected = jnp.dot(values, pivot_kernel.T, precision=highest)
        solved = jax.scipy.linalg.cho_solve((factor, True), projected.T)
        return (values - jnp.dot(solved.T, pivot_kernel, precision=highest)) / noise_var
    norm_old = jnp.sum(residual * precondition(residual), axis=1)
    step_size = norm_old / jnp.sum(direction * image, axis=1)
    solution_out = solution + step_size[:, None] * direction
    residual_out = residual - step_size[:, None] * image
    precond_new = precondition(residual_out)
    norm_new = jnp.sum(residual_out * precond_new, axis=1)
    direction_out = precond_new + (norm_new / norm_old)[:, None] * direction
    return (solution_out, residual_out, direction_out, slope_image)
```

```python
import jax
import jax.numpy as jnp
from jax import lax
from jax.experimental import pallas as pl
from jax.experimental.pallas import tpu as pltpu
from jax.sharding import PartitionSpec as P

noise_var = 1.0
MESH = pl.DeviceIdType.MESH
highest = lax.Precision.HIGHEST
f32 = jnp.float32
bf16 = jnp.bfloat16
NT = (((1,), (1,)), ((), ()))
NN = (((1,), (0,)), ((), ()))


def iota(shape, dim):
    return lax.broadcasted_iota(jnp.int32, shape, dim)


def pieces(norm):
    high = norm.astype(bf16).astype(f32)
    rest = norm - high
    mid = rest.astype(bf16).astype(f32)
    low = (rest - mid).astype(bf16).astype(f32)
    return high, mid, low


def with_norms(values, lane):
    norm = jnp.sum(values * values, axis=1, keepdims=True)
    high, mid, low = pieces(norm)
    values = values + jnp.where((lane == 32) | (lane == 35), high, 0.0)
    values = values + jnp.where((lane == 33) | (lane == 36), mid, 0.0)
    return values + jnp.where((lane == 34) | (lane == 37), low, 0.0)


def lane_rows():
    lane = iota((1, 128), 1)
    feat = lane >= 64
    first = (lane >= 32) & (lane < 35)
    second = (lane >= 35) & (lane < 38)
    one = jnp.where(first | feat, 1.0, 0.0)
    col_scale = one.astype(bf16)
    col_shift = jnp.where(second, 1.0, 0.0).astype(bf16)
    row_scale = jnp.where(feat, -2.0, jnp.where(second, 1.0, 0.0)).astype(bf16)
    row_shift = jnp.where(first, 1.0, 0.0).astype(bf16)
    return col_scale, col_shift, row_scale, row_shift


def kernel(
    feat_hbm, inv_hbm, piv_hbm, sol_hbm, res_hbm, dir_hbm,
    sol_out, res_out, dir_out, slope_out,
    feat_in, inv_in, piv_in, sol_in, res_in, dir_in,
    stage_a, stage_b,
    zbuf, xbuf, colm, wmat,
    fold, fold_sib, part, part_xy,
    q_own, q_sib, q_sum, q_xy,
    g_own, g_sib, g_sum, g_xy,
    p_own, p_sib, p_sum, p_xy, p_tot, p_z, p_half, p_other,
    in_sem, zs, zr, xs, xr, ws, wr, fs, fr, ps, pr, qs, qr, qxs, qxr, gs, gr, gxs, gxr, ts, tr, txs, txr, tzs, tzr, us, ur,
):
    row = lax.axis_index("row")
    col = lax.axis_index("col")
    xy = lax.rem(row, 16)
    core = lax.rem(col, 2)
    z = (col // 2) * 4 + row // 16

    def dev(z_at, xy_at, core_at):
        return (lax.rem(z_at, 4) * 16 + xy_at, (z_at // 4) * 2 + core_at)

    def z_peer(k):
        far = 8 - (k + 1) // 2
        return lax.rem(z + jnp.where(lax.rem(k, 2) == 1, far, 16 - far), 16)

    def xy_peer(k):
        return lax.rem(xy + k, 16)

    sibling = dev(z, xy, 1 - core)

    def remote(src, dst, send, recv, where):
        return pltpu.make_async_remote_copy(
            src_ref=src, dst_ref=dst, send_sem=send, recv_sem=recv, device_id=where, device_id_type=MESH
        )

    def loop(low, high, body):
        def step(k, carry):
            body(k)
            return carry

        lax.fori_loop(low, high, step, 0)

    barrier = pltpu.get_barrier_semaphore()

    def greet(where):
        pl.semaphore_signal(barrier, inc=1, device_id=where, device_id_type=MESH)

    loop(0, 15, lambda k: greet(dev(z_peer(k), xy, core)))
    loop(1, 16, lambda k: greet(dev(z, xy_peer(k), core)))
    greet(sibling)

    loads = [
        pltpu.make_async_copy(src, dst, in_sem.at[n])
        for n, (src, dst) in enumerate(
            (
                (feat_hbm, feat_in), (inv_hbm, inv_in), (piv_hbm, piv_in),
                (sol_hbm, sol_in), (res_hbm, res_in), (dir_hbm, dir_in),
            )
        )
    ]
    for load in loads:
        load.start()
    stage_a[...] = jnp.zeros((128, 128), f32)
    stage_b[...] = jnp.zeros((128, 128), f32)
    for load in loads:
        load.wait()

    lane = iota((64, 128), 1)
    line = iota((64, 128), 0)
    stage_a[0:32, 0:64] = dir_in[...]
    stage_a[64:128, 0:64] = feat_in[...].astype(f32)
    stage_b[0:32, 0:64] = res_in[...]
    stage_b[32:64, 0:64] = sol_in[...]
    turned = stage_a[...].T[0:64]
    others = stage_b[...].T[0:64]
    dir_t = jnp.where(lane < 32, turned, 0.0)
    res_t = jnp.where(lane < 32, others, 0.0)
    sol_t = jnp.where(lane < 32, pltpu.roll(others, 96, 1), 0.0)
    stage_a[0:1, 0:64] = inv_in[...]
    stage_a[0:1, 64:128] = jnp.zeros((1, 64), f32)
    inv_row = pltpu.roll(stage_a[0:8, :], 64, 1)[0:1]
    scaled = jnp.where(lane >= 64, (turned * inv_row).astype(bf16).astype(f32), 0.0)

    offset = (row * 8 + col) * 64
    hits = piv_in[...] == iota((64, 64), 0) + offset
    picked = jnp.max(jnp.where(hits, 1.0, 0.0), axis=1, keepdims=True)
    chosen = jnp.broadcast_to(jnp.sum(picked * scaled, axis=0, keepdims=True), (8, 128))
    block = with_norms(scaled, lane) + dir_t
    for k in range(4):
        moved = pltpu.roll(chosen, (38 - 64 - 16 * k) % 128, 1)[0:1]
        block = block + jnp.where((line == k) & (lane >= 38) & (lane < 54), moved, 0.0)
    own = block.astype(bf16)
    zbuf[z] = own
    xbuf[core, xy] = own

    pl.semaphore_wait(barrier, 31)

    def z_copy(k):
        return remote(zbuf.at[z], zbuf.at[z], zs.at[k], zr.at[z], dev(z_peer(k), xy, core))

    def x_copy(k):
        return remote(xbuf.at[core, xy], xbuf.at[core, xy], xs.at[k], xr.at[xy], dev(z, xy_peer(k), core))

    def w_copy(p):
        return remote(xbuf.at[core, p], xbuf.at[core, p], ws.at[p], wr.at[p], sibling)

    loop(0, 15, lambda k: z_copy(k).start())
    loop(1, 16, lambda k: x_copy(k).start())
    w_copy(xy).start()

    def forward(k):
        p = xy_peer(k)
        remote(xbuf.at[core, p], xbuf.at[core, p], xs.at[k], xr.at[p], sibling).wait_recv()
        w_copy(p).start()

    loop(1, 16, forward)

    def z_arrive(k):
        p = z_peer(k)
        remote(zbuf.at[p], zbuf.at[p], zs.at[k], zr.at[p], sibling).wait_recv()

    loop(0, 15, z_arrive)

    lane16 = iota((16, 128), 1)
    line16 = iota((16, 128), 0)
    found = jnp.zeros((16, 128), f32)
    for low in range(4):
        seen = zbuf[low, 0:16, :].astype(f32)
        for high in range(1, 4):
            seen = seen + zbuf[high * 4 + low, 0:16, :].astype(f32)
        seen = jnp.where((lane16 >= 38) & (lane16 < 54), seen, 0.0)[0:8]
        whole = jnp.zeros((1, 128), f32)
        for k in range(4):
            whole = whole + pltpu.roll(seen, 64 + 16 * k - 38, 1)[k : k + 1]
        found = found + jnp.where(line16 == lax.rem(xy, 4) * 4 + low, whole, 0.0)
    q_own[...] = found.astype(bf16)
    q_copy = remote(q_own, q_sib, qs, qr, sibling)
    q_copy.start()

    col_scale, col_shift, row_scale, row_shift = lane_rows()
    lane_w = iota((64, 128), 1)

    def columns(k):
        held = zbuf[k]
        start = pl.multiple_of(k * 64, 64)
        colm[pl.ds(start, 64), :] = held * col_scale + col_shift
        direction = jnp.where(lane_w < 32, held.astype(f32), 0.0)
        wmat[0, pl.ds(start, 64), :] = direction.astype(bf16)
        wmat[1, pl.ds(start, 64), :] = pltpu.roll(direction, 32, 1).astype(bf16)

    loop(0, 16, columns)

    def tile(owner, chunk):
        rows = xbuf[owner, pl.ds(chunk * 4, 4)].reshape(256, 128) * row_scale + row_shift
        total = jnp.zeros((256, 128), f32)
        for part_at in range(4):
            cols = slice(part_at * 256, part_at * 256 + 256)
            distance = lax.dot_general(rows, colm[cols, :], NT, preferred_element_type=f32)
            value = jnp.exp(-0.5 * distance)
            total = total + jnp.dot(value.astype(bf16), wmat[0, cols, :], preferred_element_type=f32)
            total = total + jnp.dot((value * distance).astype(bf16), wmat[1, cols, :], preferred_element_type=f32)
        total = total.reshape(4, 64, 128)
        upper = total[:, 0:32].reshape(128, 128)
        lower = total[:, 32:64].reshape(128, 128)
        fold[owner, pl.ds(chunk * 4, 4)] = (upper + pltpu.roll(lower, 64, 1)).reshape(4, 32, 128)

    def w_arrive(p):
        remote(xbuf.at[1 - core, p], xbuf.at[1 - core, p], ws.at[p], wr.at[p], sibling).wait_recv()

    loop(0, 16, w_arrive)
    loop(0, 4, lambda chunk: tile(1 - core, chunk))
    f_copy = remote(fold.at[1 - core], fold_sib, fs, fr, sibling)
    f_copy.start()

    q_copy.wait()
    q_sum[...] = (q_own[...].astype(f32) + q_sib[...].astype(f32)).astype(bf16)
    q_xy[xy] = q_sum[...]

    def q_send(k):
        return remote(q_sum, q_xy.at[xy], qxs.at[k], qxr.at[xy], dev(z, xy_peer(k), core))

    loop(1, 16, lambda k: q_send(k).start())

    loop(0, 4, lambda chunk: tile(core, chunk))
    f_copy.wait()
    part[...] = fold[core] + fold_sib[...]
    part_xy[xy] = part[xy]

    def s_copy(k):
        p = xy_peer(k)
        return remote(part.at[p], part_xy.at[xy], ps.at[k], pr.at[xy], dev(z, p, core))

    loop(1, 16, lambda k: s_copy(k).start())

    def q_arrive(k):
        p = xy_peer(k)
        remote(q_xy.at[p], q_xy.at[p], qxs.at[k], qxr.at[p], sibling).wait_recv()

    loop(1, 16, q_arrive)
    lots = []
    for x_at in range(4):
        lot = q_xy[x_at * 4].astype(f32)
        for y_at in range(1, 4):
            lot = lot + q_xy[x_at * 4 + y_at].astype(f32)
        lots.append(lot)
    pivot = with_norms(jnp.concatenate(lots, axis=0), lane).astype(bf16)
    pivot_row = pivot * row_scale + row_shift
    pivot_col = pivot * col_scale + col_shift

    def kern(left, right):
        return jnp.exp(-0.5 * lax.dot_general(left, right, NT, preferred_element_type=f32))

    def exact(left, right, numbers):
        return lax.dot_general(left, right, numbers, precision=highest, preferred_element_type=f32)

    line_kernel = kern(pivot_row, colm[...])
    gram_part = exact(line_kernel, line_kernel, NT)
    wide = jnp.concatenate([gram_part, jnp.zeros((64, 64), f32)], axis=1)
    g_own[...] = wide[0:32] + pltpu.roll(wide[32:64], 64, 1)
    g_copy = remote(g_own, g_sib, gs, gr, sibling)
    g_copy.start()
    own_col = own * col_scale + col_shift
    own_row = own * row_scale + row_shift
    own_kernel = kern(pivot_row, own_col)
    own_kernel_t = kern(own_row, pivot_col)
    pivot_self = kern(pivot_row, pivot_col)
    g_copy.wait()
    g_sum[...] = g_own[...] + g_sib[...]
    g_xy[xy] = g_sum[...]

    def g_send(k):
        return remote(g_sum, g_xy.at[xy], gxs.at[k], gxr.at[xy], dev(z, xy_peer(k), core))

    loop(1, 16, lambda k: g_send(k).start())

    def s_arrive(k):
        p = xy_peer(k)
        remote(part.at[p], part_xy.at[p], ps.at[k], pr.at[p], sibling).wait_recv()

    loop(1, 16, s_arrive)
    folded = jnp.sum(part_xy[...], axis=0)
    images = jnp.concatenate([folded, pltpu.roll(folded, 64, 1)], axis=0)
    image = jnp.where(lane < 32, images + noise_var * dir_t, 0.0)
    slope = jnp.where((lane >= 32) & (lane < 64), images, 0.0)
    both = image + pltpu.roll(res_t, 32, 1)
    proj = exact(own_kernel, both, NN)
    p_own[0:32, :] = proj[0:32] + pltpu.roll(proj[32:64], 64, 1)
    line8 = iota((8, 128), 0)
    sums = jnp.zeros((8, 128), f32)
    for n, value in enumerate((dir_t * image, res_t * image, image * image, res_t * res_t)):
        sums = sums + jnp.where(line8 == n, jnp.sum(value, axis=0, keepdims=True), 0.0)
    p_own[32:40, :] = sums
    p_copy = remote(p_own, p_sib, ts, tr, sibling)
    p_copy.start()
    p_copy.wait()
    p_sum[...] = p_own[...] + p_sib[...]
    p_xy[xy] = p_sum[...]

    def p_send(k):
        return remote(p_sum, p_xy.at[xy], txs.at[k], txr.at[xy], dev(z, xy_peer(k), core))

    loop(1, 16, lambda k: p_send(k).start())

    def p_arrive(k):
        p = xy_peer(k)
        remote(p_xy.at[p], p_xy.at[p], txs.at[k], txr.at[p], sibling).wait_recv()

    loop(1, 16, p_arrive)
    p_tot[...] = jnp.sum(p_xy[...], axis=0)
    half = pl.multiple_of(core * 16, 8)
    p_z[z] = p_tot[pl.ds(half, 24), :]

    def t_send(k):
        return remote(p_z.at[z], p_z.at[z], tzs.at[k], tzr.at[z], dev(z_peer(k), xy, core))

    loop(0, 15, lambda k: t_send(k).start())

    def g_arrive(k):
        p = xy_peer(k)
        remote(g_xy.at[p], g_xy.at[p], gxs.at[k], gxr.at[p], sibling).wait_recv()

    loop(1, 16, g_arrive)
    gathered = jnp.sum(g_xy[...], axis=0)
    gram = jnp.concatenate([gathered, pltpu.roll(gathered, 64, 1)], axis=0)
    own_self = jnp.concatenate([noise_var * pivot_self, jnp.zeros((64, 64), f32)], axis=1)
    work = jnp.where(lane < 64, gram + own_self, jnp.where(lane == line + 64, 1.0, 0.0))
    for k in range(64):
        head = work[k : k + 1, :]
        factor = work[:, k : k + 1] * (1.0 / head[:, k : k + 1])
        work = work - jnp.where(line > k, factor, 0.0) * head
    pivots_d = jnp.sum(jnp.where(lane == line, work, 0.0), axis=1, keepdims=True)
    lower_inv = pltpu.roll(work, 64, 1)[:, 0:64] * lax.rsqrt(pivots_d)
    gram_inv = exact(lower_inv.T, lower_inv, NN)
    mapped = exact(own_kernel_t, gram_inv, NN)

    def t_arrive(k):
        p = z_peer(k)
        remote(p_z.at[p], p_z.at[p], tzs.at[k], tzr.at[p], sibling).wait_recv()

    loop(0, 15, t_arrive)
    p_half[...] = jnp.sum(p_z[...], axis=0)
    u_copy = remote(p_half, p_other, us, ur, sibling)
    u_copy.start()
    u_copy.wait()
    mine = p_half[...]
    other = p_other[...]
    top = jnp.where(core == 0, mine, other)
    bottom = jnp.where(core == 0, other, mine)
    packed = jnp.concatenate([top, bottom[8:16]], axis=0)
    scalars = bottom[16:24]

    projs = jnp.concatenate([packed, pltpu.roll(packed, 64, 1)], axis=0)
    solved = exact(gram_inv, projs, NN)
    spread = exact(mapped, projs, NN)

    def old(values):
        return pltpu.roll(values, 96, 1)

    curvature = scalars[0:1]
    cross = scalars[1:2]
    square = scalars[2:3]
    square_old = scalars[3:4]
    proj_old = old(projs)
    solved_old = old(solved)
    norm_old = (square_old - jnp.sum(proj_old * solved_old, axis=0, keepdims=True)) / noise_var
    step = norm_old / curvature
    solution_new = sol_t + step * dir_t
    residual_new = res_t - step * image
    proj_new = proj_old - step * projs
    solved_new = solved_old - step * solved
    square_new = square_old - 2.0 * step * cross + step * step * square
    norm_new = (square_new - jnp.sum(proj_new * solved_new, axis=0, keepdims=True)) / noise_var
    precond_new = (residual_new - (old(spread) - step * spread)) / noise_var
    direction_new = precond_new + (norm_new / norm_old) * dir_t

    result = jnp.where(
        lane < 32,
        solution_new,
        jnp.where(
            lane < 64,
            pltpu.roll(residual_new, 32, 1),
            jnp.where(lane < 96, pltpu.roll(direction_new, 64, 1), pltpu.roll(slope, 64, 1)),
        ),
    )
    stage_b[0:64, :] = result
    turned_back = stage_b[...].T
    sol_out[...] = turned_back[0:32, 0:64]
    res_out[...] = turned_back[32:64, 0:64]
    dir_out[...] = turned_back[64:96, 0:64]
    slope_out[...] = turned_back[96:128, 0:64]

    loop(0, 15, lambda k: z_copy(k).wait_send())
    loop(1, 16, lambda k: x_copy(k).wait_send())
    loop(0, 16, lambda p: w_copy(p).wait_send())
    loop(1, 16, lambda k: q_send(k).wait_send())
    loop(1, 16, lambda k: s_copy(k).wait_send())
    loop(1, 16, lambda k: g_send(k).wait_send())
    loop(1, 16, lambda k: p_send(k).wait_send())
    loop(0, 15, lambda k: t_send(k).wait_send())


def local(features, inv_scale, pivots, solution, residual, direction):
    vmem = pltpu.VMEM
    dma = pltpu.SemaphoreType.DMA
    one = dma(())
    many = dma((16,))
    shape = jax.ShapeDtypeStruct((32, 64), f32)
    scratch = [
        vmem((64, 64), bf16), vmem((1, 64), f32), vmem((1, 64), jnp.int32),
        vmem((32, 64), f32), vmem((32, 64), f32), vmem((32, 64), f32),
        vmem((128, 128), f32), vmem((128, 128), f32),
        vmem((16, 64, 128), bf16), vmem((2, 16, 64, 128), bf16), vmem((1024, 128), bf16), vmem((2, 1024, 128), bf16),
        vmem((2, 16, 32, 128), f32), vmem((16, 32, 128), f32), vmem((16, 32, 128), f32), vmem((16, 32, 128), f32),
        vmem((16, 128), bf16), vmem((16, 128), bf16), vmem((16, 128), bf16), vmem((16, 16, 128), bf16),
        vmem((32, 128), f32), vmem((32, 128), f32), vmem((32, 128), f32), vmem((16, 32, 128), f32),
        vmem((40, 128), f32), vmem((40, 128), f32), vmem((40, 128), f32), vmem((16, 40, 128), f32),
        vmem((40, 128), f32), vmem((16, 24, 128), f32), vmem((24, 128), f32), vmem((24, 128), f32),
        dma((6,)),
        many, many, many, many, many, many, one, one, many, many, one, one, many, many,
        one, one, many, many, one, one, many, many, many, many, one, one,
    ]
    return pl.pallas_call(
        kernel,
        name="cg_step",
        out_shape=(shape,) * 4,
        in_specs=[pl.BlockSpec(memory_space=pl.ANY)] * 6,
        out_specs=(pl.BlockSpec(memory_space=pltpu.VMEM),) * 4,
        scratch_shapes=scratch,
        compiler_params=pltpu.CompilerParams(
            collective_id=0, has_side_effects=True, vmem_limit_bytes=40 * 1024 * 1024
        ),
    )(features, inv_scale[None, :], pivots[None, :], solution, residual, direction)


def solution(mesh):
    placed = (
        P(None, ("row", "col")),
        P(),
        P(),
        P(None, ("row", "col")),
        P(None, ("row", "col")),
        P(None, ("row", "col")),
    )
    return jax.shard_map(
        local,
        mesh=mesh,
        in_specs=placed,
        out_specs=(P(None, ("row", "col")),) * 4,
        check_vma=False,
    )
```

```python
import jax
import jax.numpy as jnp
from jax import lax
from jax.experimental import pallas as pl
from jax.experimental.pallas import tpu as pltpu
from jax.sharding import PartitionSpec as P

noise_var = 1.0
MESH = pl.DeviceIdType.MESH
highest = lax.Precision.HIGHEST
f32 = jnp.float32
bf16 = jnp.bfloat16
NT = (((1,), (1,)), ((), ()))
NN = (((1,), (0,)), ((), ()))


def iota(shape, dim):
    return lax.broadcasted_iota(jnp.int32, shape, dim)


def loop(low, high, body):
    def step(k, carry):
        body(k)
        return carry

    lax.fori_loop(low, high, step, 0)


def exact(left, right, numbers=NN):
    return lax.dot_general(left, right, numbers, precision=highest, preferred_element_type=f32)


def kernel_of(left, right):
    return jnp.exp(lax.dot_general(left, right, NT, preferred_element_type=f32))


def forms(scaled, lane):
    norm = jnp.sum(scaled * scaled, axis=1, keepdims=True)
    high = norm.astype(bf16).astype(f32)
    rest = norm - high
    mid = rest.astype(bf16).astype(f32)
    low = (rest - mid).astype(bf16).astype(f32)
    place = lane - 32
    first = jnp.where(place == 0, high, jnp.where(place == 1, mid, jnp.where(place == 2, low, 0.0)))
    place = lane - 35
    second = jnp.where(place == 0, high, jnp.where(place == 1, mid, jnp.where(place == 2, low, 0.0)))
    in_first = (lane >= 32) & (lane < 35)
    in_second = (lane >= 35) & (lane < 38)
    row_form = scaled + second + jnp.where(in_first, -0.5, 0.0)
    col_form = scaled + first + jnp.where(in_second, -0.5, 0.0)
    return row_form, col_form


def unfold(packed):
    return jnp.concatenate([packed, pltpu.roll(packed, 64, 1)], axis=0)


def step_kernel(
    feat_hbm, inv_hbm, piv_hbm, sol_hbm, res_hbm, dir_hbm,
    result,
    feat_in, inv_in, piv_in, sol_in, res_in, dir_in,
    stage_a, stage_b,
    zbuf, xbuf, weights, acc,
    fold, fold_sib, part, part_xy,
    q_z,
    g_own, g_sib, g_sum, g_xy,
    l_own, l_sib, l_sum, l_xy, l_tot, l_z, l_half, l_other,
    e_own, e_sib, e_sum, e_xy, e_z,
    in_sem, zs, zr, xs, xr, ws, wr, fs, fr, ps, pr, qs, qr,
    gs, gr, gxs, gxr, ls, lr, lxs, lxr, lzs, lzr, us, ur, es, er, exs, exr, ezs, ezr,
):
    row = lax.axis_index("row")
    col = lax.axis_index("col")
    xy = lax.rem(row, 16)
    core = lax.rem(col, 2)
    z = (col // 2) * 4 + row // 16

    def dev(z_at, xy_at, core_at):
        return (lax.rem(z_at, 4) * 16 + xy_at, (z_at // 4) * 2 + core_at)

    def z_shift(k):
        far = 8 - (k + 1) // 2
        return jnp.where(lax.rem(k, 2) == 1, far, 16 - far)

    def z_peer(k):
        return lax.rem(z + z_shift(k), 16)

    def xy_peer(k):
        return lax.rem(xy + k, 16)

    sibling = dev(z, xy, 1 - core)

    def remote(src, dst, send, recv, where=sibling):
        return pltpu.make_async_remote_copy(
            src_ref=src, dst_ref=dst, send_sem=send, recv_sem=recv, device_id=where, device_id_type=MESH
        )

    def along_z(src, buf, send, recv):
        def copy(k):
            return remote(src, buf.at[z], send.at[k], recv.at[z], dev(z_peer(k), xy, core))

        def arrival(k):
            p = z_peer(k)
            return remote(src, buf.at[p], send.at[k], recv.at[p])

        return (
            lambda: loop(0, 15, lambda k: copy(k).start()),
            lambda: loop(0, 15, lambda k: arrival(k).wait_recv()),
            lambda: loop(0, 15, lambda k: copy(k).wait_send()),
        )

    def over_xy(src_of, buf, send, recv):
        def copy(k):
            p = xy_peer(k)
            return remote(src_of(p), buf.at[xy], send.at[k], recv.at[xy], dev(z, p, core))

        def arrival(k):
            p = xy_peer(k)
            return remote(src_of(p), buf.at[p], send.at[k], recv.at[p])

        return (
            lambda: loop(1, 16, lambda k: copy(k).start()),
            lambda: loop(1, 16, lambda k: arrival(k).wait_recv()),
            lambda: loop(1, 16, lambda k: copy(k).wait_send()),
        )

    barrier = pltpu.get_barrier_semaphore()

    def greet(where):
        pl.semaphore_signal(barrier, inc=1, device_id=where, device_id_type=MESH)

    loop(0, 15, lambda k: greet(dev(z_peer(k), xy, core)))
    loop(1, 16, lambda k: greet(dev(z, xy_peer(k), core)))
    greet(sibling)

    loads = [
        pltpu.make_async_copy(src, dst, in_sem.at[n])
        for n, (src, dst) in enumerate(
            (
                (feat_hbm, feat_in), (inv_hbm, inv_in), (piv_hbm, piv_in),
                (sol_hbm, sol_in), (res_hbm, res_in), (dir_hbm, dir_in),
            )
        )
    ]
    for load in loads:
        load.start()
    stage_a[...] = jnp.zeros((128, 128), f32)
    stage_b[...] = jnp.zeros((128, 128), f32)
    for load in loads:
        load.wait()

    lane = iota((64, 128), 1)
    line = iota((64, 128), 0)
    stage_a[0:32, 0:64] = dir_in[...]
    stage_a[64:128, 0:64] = feat_in[...].astype(f32)
    stage_b[0:32, 0:64] = res_in[...]
    stage_b[32:64, 0:64] = sol_in[...]
    turned = stage_a[...].T[0:64]
    others = stage_b[...].T[0:64]
    dir_t = jnp.where(lane < 32, turned, 0.0)
    res_t = jnp.where(lane < 32, others, 0.0)
    sol_t = jnp.where(lane < 32, pltpu.roll(others, 96, 1), 0.0)
    stage_a[0:1, 0:64] = inv_in[...]
    stage_a[0:1, 64:128] = jnp.zeros((1, 64), f32)
    inv_row = pltpu.roll(stage_a[0:8, :], 64, 1)[0:1]
    scaled = jnp.where(lane >= 64, (turned * inv_row).astype(bf16).astype(f32), 0.0)

    offset = (row * 8 + col) * 64
    hits = piv_in[...] == iota((64, 64), 0) + offset
    picked = jnp.max(jnp.where(hits, 1.0, 0.0), axis=1, keepdims=True)
    chosen = jnp.broadcast_to(jnp.sum(picked * scaled, axis=0, keepdims=True), (8, 128))
    row_form, col_form = forms(scaled, lane)
    for k in range(4):
        moved = pltpu.roll(chosen, (38 - 64 - 16 * k) % 128, 1)[0:1]
        row_form = row_form + jnp.where((line == k) & (lane >= 38) & (lane < 54), moved, 0.0)
    own_row = row_form.astype(bf16)
    own_col = (col_form + dir_t).astype(bf16)
    zbuf[0] = own_col
    xbuf[core, xy] = own_row

    pl.semaphore_wait(barrier, 31)

    def z_copy(k):
        return remote(zbuf.at[0], zbuf.at[k + 1], zs.at[k], zr.at[k], dev(z_peer(k), xy, core))

    x_start, x_arrive, x_left = over_xy(lambda p: xbuf.at[core, xy], xbuf.at[core], xs, xr)

    def w_copy(p):
        return remote(xbuf.at[core, p], xbuf.at[core, p], ws.at[p], wr.at[p])

    def w_arrival(p):
        return remote(xbuf.at[1 - core, p], xbuf.at[1 - core, p], ws.at[p], wr.at[p])

    loop(0, 15, lambda k: z_copy(k).start())
    x_start()
    w_copy(xy).start()

    def forward(k):
        p = xy_peer(k)
        remote(xbuf.at[core, p], xbuf.at[core, p], xs.at[k], xr.at[p]).wait_recv()
        w_copy(p).start()

    loop(1, 16, forward)
    loop(0, 16, lambda p: w_arrival(p).wait_recv())

    seen = (xbuf[0, :, 0:16, :].astype(f32) + xbuf[1, :, 0:16, :].astype(f32))[:, 0:8, :]
    at_lane = iota((16, 8, 128), 2)
    at_line = iota((16, 8, 128), 1)
    seen = jnp.where((at_lane >= 38) & (at_lane < 54), seen, 0.0).reshape(128, 128)
    found = jnp.zeros((16, 8, 128), f32)
    for k in range(4):
        found = found + jnp.where(at_line == k, pltpu.roll(seen, 64 + 16 * k - 38, 1).reshape(16, 8, 128), 0.0)
    q_z[z] = jnp.sum(found, axis=1).astype(bf16)
    q_start, q_arrive, q_left = along_z(q_z.at[z], q_z, qs, qr)
    q_start()

    lane_w = iota((256, 128), 1)

    def columns(group):
        held = zbuf[group * 4 : group * 4 + 4].reshape(256, 128)
        direction = jnp.where(lane_w < 32, held.astype(f32), 0.0)
        weights[0:256, :] = direction.astype(bf16)
        weights[256:512, :] = (pltpu.roll(direction, 32, 1) * -2.0).astype(bf16)
        return held

    def tile(rows, cols):
        half = lax.dot_general(rows, cols, NT, preferred_element_type=f32)
        value = jnp.exp(half)
        images = jnp.dot(value.astype(bf16), weights[0:256, :], preferred_element_type=f32)
        return images + jnp.dot((value * half).astype(bf16), weights[256:512, :], preferred_element_type=f32)

    def z_arrival(k):
        remote(zbuf.at[0], zbuf.at[k + 1], zs.at[k], zr.at[k]).wait_recv()

    for group in range(3):
        loop(max(group * 4 - 1, 0), group * 4 + 3, z_arrival)
        cols = columns(group)
        product = tile(xbuf[...].reshape(2048, 128), cols)
        if group == 0:
            acc[...] = product.reshape(2, 1024, 128)
        else:
            acc[...] += product.reshape(2, 1024, 128)
    loop(11, 15, z_arrival)
    cols = columns(3)

    def last(owner):
        total = acc[owner] + tile(xbuf[owner].reshape(1024, 128), cols)
        acc[owner] = total
        total = total.reshape(16, 64, 128)
        upper = total[:, 0:32].reshape(512, 128)
        lower = total[:, 32:64].reshape(512, 128)
        fold[owner] = (upper + pltpu.roll(lower, 64, 1)).reshape(16, 32, 128)

    last(1 - core)
    f_copy = remote(fold.at[1 - core], fold_sib, fs, fr)
    f_copy.start()
    last(core)

    q_arrive()
    lots = []
    for low in range(4):
        lot = q_z[low].astype(f32)
        for high in range(1, 4):
            lot = lot + q_z[high * 4 + low].astype(f32)
        lots.append(lot)
    pivot_row, pivot_col = forms(jnp.concatenate(lots, axis=0), lane)
    pivot_row = pivot_row.astype(bf16)
    pivot_col = pivot_col.astype(bf16)
    line_kernel = kernel_of(pivot_row, zbuf[...].reshape(1024, 128))
    gram_part = exact(line_kernel, line_kernel, NT)
    wide = jnp.concatenate([gram_part, jnp.zeros((64, 64), f32)], axis=1)
    g_own[...] = wide[0:32] + pltpu.roll(wide[32:64], 64, 1)
    g_copy = remote(g_own, g_sib, gs, gr)
    g_copy.start()

    f_copy.wait()
    part[...] = fold[core] + fold_sib[...]
    part_xy[xy] = part[xy]
    s_start, s_arrive, s_left = over_xy(lambda p: part.at[p], part_xy, ps, pr)
    s_start()

    own_kernel = kernel_of(pivot_row, own_col)
    own_kernel_t = kernel_of(own_row, pivot_col)
    pivot_self = kernel_of(pivot_row, pivot_col)
    plane_kernel = kernel_of(pivot_col, xbuf[...].reshape(2048, 128))
    proj = exact(plane_kernel, acc[...].reshape(2048, 128))
    proj = jnp.where(lane < 32, proj, 0.0) + exact(own_kernel, noise_var * dir_t + pltpu.roll(res_t, 32, 1))
    l_own[...] = proj[0:32] + pltpu.roll(proj[32:64], 64, 1)
    l_copy = remote(l_own, l_sib, ls, lr)
    l_copy.start()

    g_copy.wait()
    g_sum[...] = g_own[...] + g_sib[...]
    g_xy[xy] = g_sum[...]
    g_start, g_arrive, g_left = over_xy(lambda p: g_sum, g_xy, gxs, gxr)
    g_start()
    l_copy.wait()
    l_sum[...] = l_own[...] + l_sib[...]
    l_xy[xy] = l_sum[...]
    l_start, l_arrive, l_left = over_xy(lambda p: l_sum, l_xy, lxs, lxr)
    l_start()

    s_arrive()
    images = unfold(jnp.sum(part_xy[...], axis=0))
    image = jnp.where(lane < 32, images + noise_var * dir_t, 0.0)
    slope = jnp.where((lane >= 32) & (lane < 64), images, 0.0)
    sums = jnp.sum(
        dir_t * image
        + pltpu.roll(res_t * image, 32, 1)
        + pltpu.roll(image * image, 64, 1)
        + pltpu.roll(res_t * res_t, 96, 1),
        axis=0,
        keepdims=True,
    )
    e_own[...] = sums
    e_copy = remote(e_own, e_sib, es, er)
    e_copy.start()
    e_copy.wait()
    e_sum[...] = e_own[...] + e_sib[...]
    e_xy[xy] = e_sum[...]
    e_start, e_arrive, e_left = over_xy(lambda p: e_sum, e_xy, exs, exr)
    e_start()

    l_arrive()
    l_tot[...] = jnp.sum(l_xy[...], axis=0)
    l_z[z] = l_tot[pl.ds(pl.multiple_of(core * 16, 16), 16), :]
    lz_start, lz_arrive, lz_left = along_z(l_z.at[z], l_z, lzs, lzr)
    lz_start()

    g_arrive()
    gram = unfold(jnp.sum(g_xy[...], axis=0))
    own_self = jnp.concatenate([noise_var * pivot_self, jnp.zeros((64, 64), f32)], axis=1)
    work = jnp.where(lane < 64, gram + own_self, jnp.where(lane == line + 64, 1.0, 0.0))

    def eliminate(work, low, high):
        for k in range(low, high):
            head = work[k : k + 1, :]
            factor = work[:, k : k + 1] * (1.0 / head[:, k : k + 1])
            work = work - jnp.where(line > k, factor, 0.0) * head
        return work

    work = eliminate(work, 0, 24)
    e_arrive()
    e_z[z] = jnp.sum(e_xy[...], axis=0)
    ez_start, ez_arrive, ez_left = along_z(e_z.at[z], e_z, ezs, ezr)
    ez_start()
    work = eliminate(work, 24, 64)
    diagonal = jnp.sum(jnp.where(lane == line, work, 0.0), axis=1, keepdims=True)
    lower_inv = pltpu.roll(work, 64, 1)[:, 0:64] * lax.rsqrt(diagonal)
    gram_inv = exact(lower_inv.T, lower_inv)
    mapped = exact(own_kernel_t, gram_inv)

    loop(0, 15, lambda k: z_copy(k).wait_send())
    x_left()
    loop(0, 16, lambda p: w_copy(p).wait_send())
    q_left()
    s_left()
    g_left()
    l_left()
    e_left()

    lz_arrive()
    l_half[...] = jnp.sum(l_z[...], axis=0)
    u_copy = remote(l_half, l_other, us, ur)
    u_copy.start()
    lz_left()
    u_copy.wait()
    mine = l_half[...]
    other = l_other[...]
    projs = unfold(jnp.concatenate([jnp.where(core == 0, mine, other), jnp.where(core == 0, other, mine)], axis=0))
    solved = exact(gram_inv, projs)
    spread = exact(mapped, projs)

    def old(values):
        return pltpu.roll(values, 96, 1)

    proj_old = old(projs)
    solved_old = old(solved)
    spread_old = old(spread)
    removed_old = jnp.sum(proj_old * solved_old, axis=0, keepdims=True)

    ez_left()
    ez_arrive()
    curvature = jnp.sum(e_z[...], axis=0)
    cross = pltpu.roll(jnp.broadcast_to(curvature, (8, 128)), 96, 1)[0:1]
    square = pltpu.roll(jnp.broadcast_to(curvature, (8, 128)), 64, 1)[0:1]
    square_old = pltpu.roll(jnp.broadcast_to(curvature, (8, 128)), 32, 1)[0:1]
    norm_old = (square_old - removed_old) / noise_var
    step = norm_old / curvature
    residual_new = res_t - step * image
    proj_new = proj_old - step * projs
    solved_new = solved_old - step * solved
    square_new = square_old - 2.0 * step * cross + step * step * square
    norm_new = (square_new - jnp.sum(proj_new * solved_new, axis=0, keepdims=True)) / noise_var
    precond_new = (residual_new - (spread_old - step * spread)) / noise_var
    direction_new = precond_new + (norm_new / norm_old) * dir_t
    solution_new = sol_t + step * dir_t
    result[...] = jnp.where(
        lane < 32,
        solution_new,
        jnp.where(
            lane < 64,
            pltpu.roll(residual_new, 32, 1),
            jnp.where(lane < 96, pltpu.roll(direction_new, 64, 1), pltpu.roll(slope, 64, 1)),
        ),
    )


def turn_kernel(result, sol_out, res_out, dir_out, slope_out, stage):
    stage[0:64, :] = result[...]
    stage[64:128, :] = jnp.zeros((64, 128), f32)
    turned = stage[...].T
    sol_out[...] = turned[0:32, 0:64]
    res_out[...] = turned[32:64, 0:64]
    dir_out[...] = turned[64:96, 0:64]
    slope_out[...] = turned[96:128, 0:64]


def local(features, inv_scale, pivots, solution, residual, direction):
    vmem = pltpu.VMEM
    dma = pltpu.SemaphoreType.DMA
    one = dma(())
    many = dma((16,))
    fold32 = vmem((16, 32, 128), f32)
    flat32 = vmem((32, 128), f32)
    flat16 = vmem((16, 128), f32)
    flat1 = vmem((1, 128), f32)
    scratch = [
        vmem((64, 64), bf16), vmem((1, 64), f32), vmem((1, 64), jnp.int32),
        vmem((32, 64), f32), vmem((32, 64), f32), vmem((32, 64), f32),
        vmem((128, 128), f32), vmem((128, 128), f32),
        vmem((16, 64, 128), bf16), vmem((2, 16, 64, 128), bf16), vmem((512, 128), bf16), vmem((2, 1024, 128), f32),
        vmem((2, 16, 32, 128), f32), fold32, fold32, fold32,
        vmem((16, 16, 128), bf16),
        flat32, flat32, flat32, fold32,
        flat32, flat32, flat32, fold32, flat32, vmem((16, 16, 128), f32), flat16, flat16,
        flat1, flat1, flat1, vmem((16, 1, 128), f32), vmem((16, 1, 128), f32),
        dma((6,)), many, many, many, many, many, many, one, one, many, many, many, many,
        one, one, many, many, one, one, many, many, many, many, one, one, one, one, many, many, many, many,
    ]
    result = pl.pallas_call(
        step_kernel,
        name="cg_step",
        out_shape=jax.ShapeDtypeStruct((64, 128), f32),
        in_specs=[pl.BlockSpec(memory_space=pltpu.HBM)] * 6,
        out_specs=pl.BlockSpec(memory_space=vmem),
        scratch_shapes=scratch,
        compiler_params=pltpu.CompilerParams(
            collective_id=0, has_side_effects=True, vmem_limit_bytes=60 * 1024 * 1024
        ),
    )(features, inv_scale[None, :], pivots[None, :], solution, residual, direction)
    return pl.pallas_call(
        turn_kernel,
        name="turn",
        out_shape=(jax.ShapeDtypeStruct((32, 64), f32),) * 4,
        in_specs=[pl.BlockSpec(memory_space=vmem)],
        out_specs=(pl.BlockSpec(memory_space=vmem),) * 4,
        scratch_shapes=[vmem((128, 128), f32)],
    )(result)


def solution(mesh):
    split = P(None, ("row", "col"))
    return jax.shard_map(
        local,
        mesh=mesh,
        in_specs=(split, P(), P(), split, split, split),
        out_specs=(split,) * 4,
        check_vma=False,
    )
```

```python
import jax
import jax.numpy as jnp
from jax import lax
from jax.experimental import pallas as pl
from jax.experimental.pallas import tpu as pltpu
from jax.sharding import PartitionSpec as P

noise_var = 1.0
MESH = pl.DeviceIdType.MESH
highest = lax.Precision.HIGHEST
f32 = jnp.float32
bf16 = jnp.bfloat16
NT = (((1,), (1,)), ((), ()))
NN = (((1,), (0,)), ((), ()))


def iota(shape, dim):
    return lax.broadcasted_iota(jnp.int32, shape, dim)


def loop(low, high, body):
    def step(k, carry):
        body(k)
        return carry

    lax.fori_loop(low, high, step, 0)


def exact(left, right, numbers=NN):
    return lax.dot_general(left, right, numbers, precision=highest, preferred_element_type=f32)


def kernel_of(left, right):
    return jnp.exp(lax.dot_general(left, right, NT, preferred_element_type=f32))


def forms(scaled, lane):
    norm = jnp.sum(scaled * scaled, axis=1, keepdims=True)
    high = norm.astype(bf16).astype(f32)
    rest = norm - high
    mid = rest.astype(bf16).astype(f32)
    low = (rest - mid).astype(bf16).astype(f32)
    place = lane - 32
    first = jnp.where(place == 0, high, jnp.where(place == 1, mid, jnp.where(place == 2, low, 0.0)))
    place = lane - 35
    second = jnp.where(place == 0, high, jnp.where(place == 1, mid, jnp.where(place == 2, low, 0.0)))
    in_first = (lane >= 32) & (lane < 35)
    in_second = (lane >= 35) & (lane < 38)
    row_form = scaled + second + jnp.where(in_first, -0.5, 0.0)
    col_form = scaled + first + jnp.where(in_second, -0.5, 0.0)
    return row_form, col_form


def unfold(packed):
    return jnp.concatenate([packed, pltpu.roll(packed, 64, 1)], axis=0)


def step_kernel(
    feat_hbm, inv_hbm, piv_hbm, sol_hbm, res_hbm, dir_hbm,
    result,
    feat_in, inv_in, piv_in, sol_in, res_in, dir_in,
    stage_a, stage_b,
    zbuf, zsib, xbuf, weights, acc,
    part, part_xy,
    q_z, q_own, q_sib, q_xy,
    g_own, g_sib, g_sum, g_xy,
    l_own, l_sib, l_sum, l_xy, l_tot, l_z, l_half, l_other,
    e_own, e_sib, e_sum, e_xy, e_z,
    in_sem, zs, zr, xs, xr, ws, wr, ps, pr, qs, qr, qcs, qcr, qxs, qxr,
    gs, gr, gxs, gxr, ls, lr, lxs, lxr, lzs, lzr, us, ur, es, er, exs, exr, ezs, ezr,
):
    row = lax.axis_index("row")
    col = lax.axis_index("col")
    xy = lax.rem(row, 16)
    core = lax.rem(col, 2)
    z = (col // 2) * 4 + row // 16

    def dev(z_at, xy_at, core_at):
        return (lax.rem(z_at, 4) * 16 + xy_at, (z_at // 4) * 2 + core_at)

    def z_shift(k):
        far = 8 - (k + 1) // 2
        return jnp.where(lax.rem(k, 2) == 1, far, 16 - far)

    def z_peer(k):
        return lax.rem(z + z_shift(k), 16)

    def xy_peer(k):
        return lax.rem(xy + k, 16)

    sibling = dev(z, xy, 1 - core)

    def remote(src, dst, send, recv, where=sibling):
        return pltpu.make_async_remote_copy(
            src_ref=src, dst_ref=dst, send_sem=send, recv_sem=recv, device_id=where, device_id_type=MESH
        )

    def along_z(src, buf, send, recv):
        def copy(k):
            return remote(src, buf.at[z], send.at[k], recv.at[z], dev(z_peer(k), xy, core))

        def arrival(k):
            p = z_peer(k)
            return remote(src, buf.at[p], send.at[k], recv.at[p])

        return (
            lambda: loop(0, 15, lambda k: copy(k).start()),
            lambda: loop(0, 15, lambda k: arrival(k).wait_recv()),
            lambda: loop(0, 15, lambda k: copy(k).wait_send()),
        )

    def over_xy(src_of, buf, send, recv):
        def copy(k):
            p = xy_peer(k)
            return remote(src_of(p), buf.at[xy], send.at[k], recv.at[xy], dev(z, p, core))

        def arrival(k):
            p = xy_peer(k)
            return remote(src_of(p), buf.at[p], send.at[k], recv.at[p])

        return (
            lambda: loop(1, 16, lambda k: copy(k).start()),
            lambda: loop(1, 16, lambda k: arrival(k).wait_recv()),
            lambda: loop(1, 16, lambda k: copy(k).wait_send()),
        )

    barrier = pltpu.get_barrier_semaphore()

    def greet(where):
        pl.semaphore_signal(barrier, inc=1, device_id=where, device_id_type=MESH)

    loop(0, 15, lambda k: greet(dev(z_peer(k), xy, core)))
    loop(1, 16, lambda k: greet(dev(z, xy_peer(k), core)))
    greet(sibling)

    loads = [
        pltpu.make_async_copy(src, dst, in_sem.at[n])
        for n, (src, dst) in enumerate(
            (
                (feat_hbm, feat_in), (inv_hbm, inv_in), (piv_hbm, piv_in),
                (sol_hbm, sol_in), (res_hbm, res_in), (dir_hbm, dir_in),
            )
        )
    ]
    for load in loads:
        load.start()
    stage_a[...] = jnp.zeros((128, 128), f32)
    stage_b[...] = jnp.zeros((128, 128), f32)
    for load in loads:
        load.wait()

    lane = iota((64, 128), 1)
    line = iota((64, 128), 0)
    stage_a[0:32, 0:64] = dir_in[...]
    stage_a[64:128, 0:64] = feat_in[...].astype(f32)
    stage_b[0:32, 0:64] = res_in[...]
    stage_b[32:64, 0:64] = sol_in[...]
    turned = stage_a[...].T[0:64]
    others = stage_b[...].T[0:64]
    dir_t = jnp.where(lane < 32, turned, 0.0)
    res_t = jnp.where(lane < 32, others, 0.0)
    sol_t = jnp.where(lane < 32, pltpu.roll(others, 96, 1), 0.0)
    stage_a[0:1, 0:64] = inv_in[...]
    stage_a[0:1, 64:128] = jnp.zeros((1, 64), f32)
    inv_row = pltpu.roll(stage_a[0:8, :], 64, 1)[0:1]
    scaled = jnp.where(lane >= 64, (turned * inv_row).astype(bf16).astype(f32), 0.0)

    offset = (row * 8 + col) * 64
    hits = piv_in[...] == iota((64, 64), 0) + offset
    picked = jnp.max(jnp.where(hits, 1.0, 0.0), axis=1, keepdims=True)
    q_z[z] = jnp.sum(picked * scaled, axis=0, keepdims=True)
    row_form, col_form = forms(scaled, lane)
    own_row = row_form.astype(bf16)
    own_col = (col_form + dir_t).astype(bf16)
    zbuf[0] = own_col
    xbuf[xy] = own_row

    pl.semaphore_wait(barrier, 31)

    q_start, q_arrive, q_left = along_z(q_z.at[z], q_z, qs, qr)

    def z_copy(k):
        return remote(zbuf.at[0], zbuf.at[k + 1], zs.at[k], zr.at[k], dev(z_peer(k), xy, core))

    def z_arrival(k):
        remote(zbuf.at[0], zbuf.at[k + 1], zs.at[k], zr.at[k]).wait_recv()

    def w_copy(slot):
        return remote(zbuf.at[slot], zsib.at[slot], ws.at[slot], wr.at[slot])

    x_start, x_arrive, x_left = over_xy(lambda p: xbuf.at[xy], xbuf, xs, xr)
    q_start()
    loop(0, 15, lambda k: z_copy(k).start())
    x_start()
    w_copy(0).start()

    def tile(cols):
        count = cols.shape[0]
        direction = jnp.where(iota((count, 128), 1) < 32, cols.astype(f32), 0.0)
        weights[0:count, :] = direction.astype(bf16)
        weights[count : 2 * count, :] = (pltpu.roll(direction, 32, 1) * -2.0).astype(bf16)
        half = lax.dot_general(xbuf[...].reshape(1024, 128), cols, NT, preferred_element_type=f32)
        value = jnp.exp(half)
        images = jnp.dot(value.astype(bf16), weights[0:count, :], preferred_element_type=f32)
        return images + jnp.dot((value * half).astype(bf16), weights[count : 2 * count, :], preferred_element_type=f32)

    def receive(k):
        z_arrival(k)
        w_copy(k + 1).start()

    def lines(group):
        loop(max(group * 4 - 1, 0), group * 4 + 3, receive)
        return zbuf[group * 4 : group * 4 + 4].reshape(256, 128)

    def sibling_lines(group):
        loop(group * 4, group * 4 + 4, lambda slot: w_copy(slot).wait_recv())
        return zsib[group * 4 : group * 4 + 4].reshape(256, 128)

    x_arrive()
    cols = lines(0)
    acc[...] = tile(cols)

    q_arrive()
    line8 = iota((8, 128), 0)
    found = jnp.zeros((8, 128), f32)
    for low in range(4):
        lot = q_z[low] + q_z[4 + low] + q_z[8 + low] + q_z[12 + low]
        found = found + jnp.where(line8 == lax.rem(xy, 2) * 4 + low, lot, 0.0)
    q_own[...] = found
    qc_copy = remote(q_own, q_sib, qcs, qcr)
    qc_copy.start()

    cols = lines(1)
    acc[...] += tile(jnp.concatenate([cols, sibling_lines(0)], axis=0))
    qc_copy.wait()
    q_xy[xy] = q_own[...] + q_sib[...]
    qx_start, qx_arrive, qx_left = over_xy(lambda p: q_xy.at[xy], q_xy, qxs, qxr)
    qx_start()
    cols = lines(2)
    acc[...] += tile(jnp.concatenate([cols, sibling_lines(1)], axis=0))
    cols = lines(3)
    acc[...] += tile(jnp.concatenate([cols, sibling_lines(2)], axis=0))
    total = acc[...] + tile(sibling_lines(3))
    acc[...] = total

    total = total.reshape(16, 64, 128)
    upper = total[:, 0:32].reshape(512, 128)
    lower = total[:, 32:64].reshape(512, 128)
    part[...] = (upper + pltpu.roll(lower, 64, 1)).reshape(16, 32, 128)
    part_xy[xy] = part[xy]
    s_start, s_arrive, s_left = over_xy(lambda p: part.at[p], part_xy, ps, pr)
    s_start()

    qx_arrive()
    lots = [q_xy[2 * pair] + q_xy[2 * pair + 1] for pair in range(8)]
    pivot_row, pivot_col = forms(jnp.concatenate(lots, axis=0), lane)
    pivot_row = pivot_row.astype(bf16)
    pivot_col = pivot_col.astype(bf16)
    line_kernel = kernel_of(pivot_row, zbuf[...].reshape(1024, 128))
    gram_part = exact(line_kernel, line_kernel, NT)
    wide = jnp.concatenate([gram_part, jnp.zeros((64, 64), f32)], axis=1)
    g_own[...] = wide[0:32] + pltpu.roll(wide[32:64], 64, 1)
    g_copy = remote(g_own, g_sib, gs, gr)
    g_copy.start()

    own_kernel = kernel_of(pivot_row, own_col)
    own_kernel_t = kernel_of(own_row, pivot_col)
    pivot_self = kernel_of(pivot_row, pivot_col)
    plane_kernel = kernel_of(pivot_col, xbuf[...].reshape(1024, 128))
    proj = exact(plane_kernel, acc[...])
    proj = jnp.where(lane < 32, proj, 0.0) + exact(own_kernel, noise_var * dir_t + pltpu.roll(res_t, 32, 1))
    l_own[...] = proj[0:32] + pltpu.roll(proj[32:64], 64, 1)
    l_copy = remote(l_own, l_sib, ls, lr)
    l_copy.start()

    g_copy.wait()
    g_sum[...] = g_own[...] + g_sib[...]
    g_xy[xy] = g_sum[...]
    g_start, g_arrive, g_left = over_xy(lambda p: g_sum, g_xy, gxs, gxr)
    g_start()
    l_copy.wait()
    l_sum[...] = l_own[...] + l_sib[...]
    l_xy[xy] = l_sum[...]
    l_start, l_arrive, l_left = over_xy(lambda p: l_sum, l_xy, lxs, lxr)
    l_start()

    s_arrive()
    images = unfold(jnp.sum(part_xy[...], axis=0))
    image = jnp.where(lane < 32, images + noise_var * dir_t, 0.0)
    slope = jnp.where((lane >= 32) & (lane < 64), images, 0.0)
    sums = jnp.sum(
        dir_t * image
        + pltpu.roll(res_t * image, 32, 1)
        + pltpu.roll(image * image, 64, 1)
        + pltpu.roll(res_t * res_t, 96, 1),
        axis=0,
        keepdims=True,
    )
    e_own[...] = sums
    e_copy = remote(e_own, e_sib, es, er)
    e_copy.start()
    e_copy.wait()
    e_sum[...] = e_own[...] + e_sib[...]
    e_xy[xy] = e_sum[...]
    e_start, e_arrive, e_left = over_xy(lambda p: e_sum, e_xy, exs, exr)
    e_start()

    l_arrive()
    l_tot[...] = jnp.sum(l_xy[...], axis=0)
    l_z[z] = l_tot[pl.ds(pl.multiple_of(core * 16, 16), 16), :]
    lz_start, lz_arrive, lz_left = along_z(l_z.at[z], l_z, lzs, lzr)
    lz_start()

    g_arrive()
    gram = unfold(jnp.sum(g_xy[...], axis=0))
    own_self = jnp.concatenate([noise_var * pivot_self, jnp.zeros((64, 64), f32)], axis=1)
    work = jnp.where(lane < 64, gram + own_self, jnp.where(lane == line + 64, 1.0, 0.0))

    def eliminate(work, low, high):
        for k in range(low, high):
            head = work[k : k + 1, :]
            factor = work[:, k : k + 1] * (1.0 / head[:, k : k + 1])
            work = work - jnp.where(line > k, factor, 0.0) * head
        return work

    work = eliminate(work, 0, 24)
    e_arrive()
    e_z[z] = jnp.sum(e_xy[...], axis=0)
    ez_start, ez_arrive, ez_left = along_z(e_z.at[z], e_z, ezs, ezr)
    ez_start()
    work = eliminate(work, 24, 64)
    diagonal = jnp.sum(jnp.where(lane == line, work, 0.0), axis=1, keepdims=True)
    lower_inv = pltpu.roll(work, 64, 1)[:, 0:64] * lax.rsqrt(diagonal)
    gram_inv = exact(lower_inv.T, lower_inv)
    mapped = exact(own_kernel_t, gram_inv)

    loop(0, 15, lambda k: z_copy(k).wait_send())
    x_left()
    loop(0, 16, lambda p: w_copy(p).wait_send())
    q_left()
    qx_left()
    s_left()
    g_left()
    l_left()
    e_left()

    lz_arrive()
    l_half[...] = jnp.sum(l_z[...], axis=0)
    u_copy = remote(l_half, l_other, us, ur)
    u_copy.start()
    lz_left()
    u_copy.wait()
    mine = l_half[...]
    other = l_other[...]
    projs = unfold(jnp.concatenate([jnp.where(core == 0, mine, other), jnp.where(core == 0, other, mine)], axis=0))
    solved = exact(gram_inv, projs)
    spread = exact(mapped, projs)

    def old(values):
        return pltpu.roll(values, 96, 1)

    proj_old = old(projs)
    solved_old = old(solved)
    spread_old = old(spread)
    removed_old = jnp.sum(proj_old * solved_old, axis=0, keepdims=True)

    ez_left()
    ez_arrive()
    curvature = jnp.sum(e_z[...], axis=0)
    cross = pltpu.roll(jnp.broadcast_to(curvature, (8, 128)), 96, 1)[0:1]
    square = pltpu.roll(jnp.broadcast_to(curvature, (8, 128)), 64, 1)[0:1]
    square_old = pltpu.roll(jnp.broadcast_to(curvature, (8, 128)), 32, 1)[0:1]
    norm_old = (square_old - removed_old) / noise_var
    step = norm_old / curvature
    residual_new = res_t - step * image
    proj_new = proj_old - step * projs
    solved_new = solved_old - step * solved
    square_new = square_old - 2.0 * step * cross + step * step * square
    norm_new = (square_new - jnp.sum(proj_new * solved_new, axis=0, keepdims=True)) / noise_var
    precond_new = (residual_new - (spread_old - step * spread)) / noise_var
    direction_new = precond_new + (norm_new / norm_old) * dir_t
    solution_new = sol_t + step * dir_t
    result[...] = jnp.where(
        lane < 32,
        solution_new,
        jnp.where(
            lane < 64,
            pltpu.roll(residual_new, 32, 1),
            jnp.where(lane < 96, pltpu.roll(direction_new, 64, 1), pltpu.roll(slope, 64, 1)),
        ),
    )


def turn_kernel(result, sol_out, res_out, dir_out, slope_out, stage):
    stage[0:64, :] = result[...]
    stage[64:128, :] = jnp.zeros((64, 128), f32)
    turned = stage[...].T
    sol_out[...] = turned[0:32, 0:64]
    res_out[...] = turned[32:64, 0:64]
    dir_out[...] = turned[64:96, 0:64]
    slope_out[...] = turned[96:128, 0:64]


def local(features, inv_scale, pivots, solution, residual, direction):
    vmem = pltpu.VMEM
    dma = pltpu.SemaphoreType.DMA
    one = dma(())
    many = dma((16,))
    fold32 = vmem((16, 32, 128), f32)
    flat32 = vmem((32, 128), f32)
    flat16 = vmem((16, 128), f32)
    flat1 = vmem((1, 128), f32)
    scratch = [
        vmem((64, 64), bf16), vmem((1, 64), f32), vmem((1, 64), jnp.int32),
        vmem((32, 64), f32), vmem((32, 64), f32), vmem((32, 64), f32),
        vmem((128, 128), f32), vmem((128, 128), f32),
        vmem((16, 64, 128), bf16), vmem((16, 64, 128), bf16), vmem((16, 64, 128), bf16),
        vmem((1024, 128), bf16), vmem((1024, 128), f32),
        fold32, fold32,
        vmem((16, 1, 128), f32), vmem((8, 128), f32), vmem((8, 128), f32), vmem((16, 8, 128), f32),
        flat32, flat32, flat32, fold32,
        flat32, flat32, flat32, fold32, flat32, vmem((16, 16, 128), f32), flat16, flat16,
        flat1, flat1, flat1, vmem((16, 1, 128), f32), vmem((16, 1, 128), f32),
        dma((6,)), many, many, many, many, many, many, many, many, many, many, one, one, many, many,
        one, one, many, many, one, one, many, many, many, many, one, one, one, one, many, many, many, many,
    ]
    result = pl.pallas_call(
        step_kernel,
        name="cg_step",
        out_shape=jax.ShapeDtypeStruct((64, 128), f32),
        in_specs=[pl.BlockSpec(memory_space=pltpu.HBM)] * 6,
        out_specs=pl.BlockSpec(memory_space=vmem),
        scratch_shapes=scratch,
        compiler_params=pltpu.CompilerParams(
            collective_id=0, has_side_effects=True, vmem_limit_bytes=60 * 1024 * 1024
        ),
    )(features, inv_scale[None, :], pivots[None, :], solution, residual, direction)
    return pl.pallas_call(
        turn_kernel,
        name="turn",
        out_shape=(jax.ShapeDtypeStruct((32, 64), f32),) * 4,
        in_specs=[pl.BlockSpec(memory_space=vmem)],
        out_specs=(pl.BlockSpec(memory_space=vmem),) * 4,
        scratch_shapes=[vmem((128, 128), f32)],
    )(result)


def solution(mesh):
    split = P(None, ("row", "col"))
    return jax.shard_map(
        local,
        mesh=mesh,
        in_specs=(split, P(), P(), split, split, split),
        out_specs=(split,) * 4,
        check_vma=False,
    )
```

```python
import jax
import jax.numpy as jnp
from jax import lax
from jax.experimental import pallas as pl
from jax.experimental.pallas import tpu as pltpu
from jax.sharding import PartitionSpec as P

noise_var = 1.0
MESH = pl.DeviceIdType.MESH
highest = lax.Precision.HIGHEST
f32 = jnp.float32
bf16 = jnp.bfloat16
NT = (((1,), (1,)), ((), ()))
NN = (((1,), (0,)), ((), ()))


def iota(shape, dim):
    return lax.broadcasted_iota(jnp.int32, shape, dim)


def loop(low, high, body):
    def step(k, carry):
        body(k)
        return carry

    lax.fori_loop(low, high, step, 0)


def exact(left, right, numbers=NN):
    return lax.dot_general(left, right, numbers, precision=highest, preferred_element_type=f32)


def kernel_of(left, right):
    return jnp.exp(lax.dot_general(left, right, NT, preferred_element_type=f32))


def forms(scaled, lane):
    norm = jnp.sum(scaled * scaled, axis=1, keepdims=True)
    high = norm.astype(bf16).astype(f32)
    rest = norm - high
    mid = rest.astype(bf16).astype(f32)
    low = (rest - mid).astype(bf16).astype(f32)
    place = lane - 32
    first = jnp.where(place == 0, high, jnp.where(place == 1, mid, jnp.where(place == 2, low, 0.0)))
    place = lane - 35
    second = jnp.where(place == 0, high, jnp.where(place == 1, mid, jnp.where(place == 2, low, 0.0)))
    in_first = (lane >= 32) & (lane < 35)
    in_second = (lane >= 35) & (lane < 38)
    row_form = scaled + second + jnp.where(in_first, -0.5, 0.0)
    col_form = scaled + first + jnp.where(in_second, -0.5, 0.0)
    return row_form, col_form


def unfold_block(blocks):
    count = blocks.shape[0]
    wide = blocks.astype(f32)
    lane = iota((count * 64, 128), 1)
    near = wide[:, 0:32]
    far = pltpu.roll(near.reshape(count * 32, 128), 64, 1).reshape(count, 32, 128)
    scaled = jnp.concatenate([near, far], axis=1).reshape(count * 64, 128)
    column = forms(jnp.where(lane >= 64, scaled, 0.0), lane)[1].astype(bf16)
    packed = wide[:, 32:48].reshape(count * 16, 128)

    def at(first):
        turned = [pltpu.roll(packed, (first - 32 * q) % 128, 1).reshape(count, 16, 128) for q in range(4)]
        return jnp.concatenate(turned, axis=1).reshape(count * 64, 128)

    plain = jnp.where(lane < 32, at(0), 0.0).astype(bf16)
    slope = jnp.where((lane >= 32) & (lane < 64), -2.0 * at(32), 0.0).astype(bf16)
    return column, plain, slope


def unfold(packed):
    return jnp.concatenate([packed, pltpu.roll(packed, 64, 1)], axis=0)


def step_kernel(
    feat_hbm, inv_hbm, piv_hbm, sol_hbm, res_hbm, dir_hbm,
    result,
    feat_in, inv_in, piv_in, sol_in, res_in, dir_in,
    stage_a, stage_b,
    zbuf, zsib, xbuf, colm, acc,
    part, part_xy,
    q_z, q_own, q_sib, q_xy,
    g_own, g_sib, g_sum, g_xy,
    l_own, l_sib, l_sum, l_xy, l_tot, l_z, l_half, l_other,
    e_own, e_sib, e_sum, e_xy, e_z,
    in_sem, zs, zr, xs, xr, ws, wr, ps, pr, qs, qr, qcs, qcr, qxs, qxr,
    gs, gr, gxs, gxr, ls, lr, lxs, lxr, lzs, lzr, us, ur, es, er, exs, exr, ezs, ezr,
):
    row = lax.axis_index("row")
    col = lax.axis_index("col")
    xy = lax.rem(row, 16)
    core = lax.rem(col, 2)
    z = (col // 2) * 4 + row // 16

    def dev(z_at, xy_at, core_at):
        return (lax.rem(z_at, 4) * 16 + xy_at, (z_at // 4) * 2 + core_at)

    def z_shift(k):
        far = 8 - (k + 1) // 2
        return jnp.where(lax.rem(k, 2) == 1, far, 16 - far)

    def z_peer(k):
        return lax.rem(z + z_shift(k), 16)

    def xy_peer(k):
        return lax.rem(xy + k, 16)

    sibling = dev(z, xy, 1 - core)

    def remote(src, dst, send, recv, where=sibling):
        return pltpu.make_async_remote_copy(
            src_ref=src, dst_ref=dst, send_sem=send, recv_sem=recv, device_id=where, device_id_type=MESH
        )

    def along_z(src, buf, send, recv):
        def copy(k):
            return remote(src, buf.at[z], send.at[k], recv.at[z], dev(z_peer(k), xy, core))

        def arrival(k):
            p = z_peer(k)
            return remote(src, buf.at[p], send.at[k], recv.at[p])

        return (
            lambda: loop(0, 15, lambda k: copy(k).start()),
            lambda: loop(0, 15, lambda k: arrival(k).wait_recv()),
            lambda: loop(0, 15, lambda k: copy(k).wait_send()),
        )

    def over_xy(src_of, buf, send, recv):
        def copy(k):
            p = xy_peer(k)
            return remote(src_of(p), buf.at[xy], send.at[k], recv.at[xy], dev(z, p, core))

        def arrival(k):
            p = xy_peer(k)
            return remote(src_of(p), buf.at[p], send.at[k], recv.at[p])

        return (
            lambda: loop(1, 16, lambda k: copy(k).start()),
            lambda: loop(1, 16, lambda k: arrival(k).wait_recv()),
            lambda: loop(1, 16, lambda k: copy(k).wait_send()),
        )

    barrier = pltpu.get_barrier_semaphore()

    def greet(where):
        pl.semaphore_signal(barrier, inc=1, device_id=where, device_id_type=MESH)

    loop(0, 15, lambda k: greet(dev(z_peer(k), xy, core)))
    loop(1, 16, lambda k: greet(dev(z, xy_peer(k), core)))
    greet(sibling)

    loads = [
        pltpu.make_async_copy(src, dst, in_sem.at[n])
        for n, (src, dst) in enumerate(
            (
                (feat_hbm, feat_in), (inv_hbm, inv_in), (piv_hbm, piv_in),
                (sol_hbm, sol_in), (res_hbm, res_in), (dir_hbm, dir_in),
            )
        )
    ]
    for load in loads:
        load.start()
    stage_a[...] = jnp.zeros((128, 128), f32)
    stage_b[...] = jnp.zeros((128, 128), f32)
    for load in loads:
        load.wait()

    lane = iota((64, 128), 1)
    line = iota((64, 128), 0)
    stage_a[0:32, 0:64] = dir_in[...]
    stage_a[64:128, 0:64] = feat_in[...].astype(f32)
    stage_b[0:32, 0:64] = res_in[...]
    stage_b[32:64, 0:64] = sol_in[...]
    turned = stage_a[...].T[0:64]
    others = stage_b[...].T[0:64]
    dir_t = jnp.where(lane < 32, turned, 0.0)
    res_t = jnp.where(lane < 32, others, 0.0)
    sol_t = jnp.where(lane < 32, pltpu.roll(others, 96, 1), 0.0)
    stage_a[0:1, 0:64] = inv_in[...]
    stage_a[0:1, 64:128] = jnp.zeros((1, 64), f32)
    inv_row = pltpu.roll(stage_a[0:8, :], 64, 1)[0:1]
    scaled = jnp.where(lane >= 64, (turned * inv_row).astype(bf16).astype(f32), 0.0)

    offset = (row * 8 + col) * 64
    hits = piv_in[...] == iota((64, 64), 0) + offset
    picked = jnp.max(jnp.where(hits, 1.0, 0.0), axis=1, keepdims=True)
    q_z[z] = jnp.sum(picked * scaled, axis=0, keepdims=True)
    row_form, col_form = forms(scaled, lane)
    own_row = row_form.astype(bf16)
    own_col = col_form.astype(bf16)
    zbuf[0, 0:32, :] = (scaled[0:32] + pltpu.roll(scaled[32:64], 64, 1)).astype(bf16)
    zbuf[0, 32:48, :] = sum(
        (pltpu.roll(dir_t[16 * q : 16 * q + 16], 32 * q, 1) for q in range(1, 4)), dir_t[0:16]
    ).astype(bf16)
    xbuf[xy] = own_row

    pl.semaphore_wait(barrier, 31)

    q_start, q_arrive, q_left = along_z(q_z.at[z], q_z, qs, qr)

    def z_copy(k):
        return remote(zbuf.at[0], zbuf.at[k + 1], zs.at[k], zr.at[k], dev(z_peer(k), xy, core))

    def z_arrival(k):
        remote(zbuf.at[0], zbuf.at[k + 1], zs.at[k], zr.at[k]).wait_recv()

    def w_copy(slot):
        return remote(zbuf.at[slot], zsib.at[slot], ws.at[slot], wr.at[slot])

    x_start, x_arrive, x_left = over_xy(lambda p: xbuf.at[xy], xbuf, xs, xr)
    q_start()
    loop(0, 15, lambda k: z_copy(k).start())
    x_start()
    w_copy(0).start()

    def tile(blocks, keep=None):
        cols, plain, slope = unfold_block(blocks)
        if keep is not None:
            colm[keep * 256 : keep * 256 + 256, :] = cols[0:256]
        half = lax.dot_general(xbuf[...].reshape(1024, 128), cols, NT, preferred_element_type=f32)
        value = jnp.exp(half)
        images = jnp.dot(value.astype(bf16), plain, preferred_element_type=f32)
        return images + jnp.dot((value * half).astype(bf16), slope, preferred_element_type=f32)

    def receive(k):
        z_arrival(k)
        w_copy(k + 1).start()

    def lines(group):
        loop(max(group * 4 - 1, 0), group * 4 + 3, receive)
        return zbuf[group * 4 : group * 4 + 4]

    def sibling_lines(group):
        loop(group * 4, group * 4 + 4, lambda slot: w_copy(slot).wait_recv())
        return zsib[group * 4 : group * 4 + 4]

    x_arrive()
    acc[...] = tile(lines(0), 0)

    q_arrive()
    line8 = iota((8, 128), 0)
    found = jnp.zeros((8, 128), f32)
    for low in range(4):
        lot = q_z[low] + q_z[4 + low] + q_z[8 + low] + q_z[12 + low]
        found = found + jnp.where(line8 == lax.rem(xy, 2) * 4 + low, lot, 0.0)
    q_own[...] = found
    qc_copy = remote(q_own, q_sib, qcs, qcr)
    qc_copy.start()

    blocks = lines(1)
    acc[...] += tile(jnp.concatenate([blocks, sibling_lines(0)], axis=0), 1)
    qc_copy.wait()
    q_xy[xy] = q_own[...] + q_sib[...]
    qx_start, qx_arrive, qx_left = over_xy(lambda p: q_xy.at[xy], q_xy, qxs, qxr)
    qx_start()
    blocks = lines(2)
    acc[...] += tile(jnp.concatenate([blocks, sibling_lines(1)], axis=0), 2)
    blocks = lines(3)
    acc[...] += tile(jnp.concatenate([blocks, sibling_lines(2)], axis=0), 3)
    total = acc[...] + tile(sibling_lines(3))
    acc[...] = total

    total = total.reshape(16, 64, 128)
    upper = total[:, 0:32].reshape(512, 128)
    lower = total[:, 32:64].reshape(512, 128)
    part[...] = (upper + pltpu.roll(lower, 64, 1)).reshape(16, 32, 128)
    part_xy[xy] = part[xy]
    s_start, s_arrive, s_left = over_xy(lambda p: part.at[p], part_xy, ps, pr)
    s_start()

    qx_arrive()
    lots = [q_xy[2 * pair] + q_xy[2 * pair + 1] for pair in range(8)]
    pivot_row, pivot_col = forms(jnp.concatenate(lots, axis=0), lane)
    pivot_row = pivot_row.astype(bf16)
    pivot_col = pivot_col.astype(bf16)
    own_kernel = kernel_of(pivot_row, own_col)
    plane_kernel = kernel_of(pivot_col, xbuf[...].reshape(1024, 128))
    proj = exact(plane_kernel, acc[...])
    proj = jnp.where(lane < 32, proj, 0.0) + exact(own_kernel, noise_var * dir_t + pltpu.roll(res_t, 32, 1))
    l_own[...] = proj[0:32] + pltpu.roll(proj[32:64], 64, 1)
    l_copy = remote(l_own, l_sib, ls, lr)
    l_copy.start()

    line_kernel = kernel_of(pivot_row, colm[...])
    gram_part = exact(line_kernel, line_kernel, NT)
    wide = jnp.concatenate([gram_part, jnp.zeros((64, 64), f32)], axis=1)
    g_own[...] = wide[0:32] + pltpu.roll(wide[32:64], 64, 1)
    g_copy = remote(g_own, g_sib, gs, gr)
    g_copy.start()
    l_copy.wait()
    l_sum[...] = l_own[...] + l_sib[...]
    l_xy[xy] = l_sum[...]
    l_start, l_arrive, l_left = over_xy(lambda p: l_sum, l_xy, lxs, lxr)
    l_start()
    own_kernel_t = kernel_of(own_row, pivot_col)
    pivot_self = kernel_of(pivot_row, pivot_col)
    g_copy.wait()
    g_sum[...] = g_own[...] + g_sib[...]
    g_xy[xy] = g_sum[...]
    g_start, g_arrive, g_left = over_xy(lambda p: g_sum, g_xy, gxs, gxr)
    g_start()

    s_arrive()
    images = unfold(jnp.sum(part_xy[...], axis=0))
    image = jnp.where(lane < 32, images + noise_var * dir_t, 0.0)
    slope = jnp.where((lane >= 32) & (lane < 64), images, 0.0)
    sums = jnp.sum(
        dir_t * image
        + pltpu.roll(res_t * image, 32, 1)
        + pltpu.roll(image * image, 64, 1)
        + pltpu.roll(res_t * res_t, 96, 1),
        axis=0,
        keepdims=True,
    )
    e_own[...] = sums
    e_copy = remote(e_own, e_sib, es, er)
    e_copy.start()
    e_copy.wait()
    e_sum[...] = e_own[...] + e_sib[...]
    e_xy[xy] = e_sum[...]
    e_start, e_arrive, e_left = over_xy(lambda p: e_sum, e_xy, exs, exr)
    e_start()

    l_arrive()
    l_tot[...] = jnp.sum(l_xy[...], axis=0)
    l_z[z] = l_tot[pl.ds(pl.multiple_of(core * 16, 16), 16), :]
    lz_start, lz_arrive, lz_left = along_z(l_z.at[z], l_z, lzs, lzr)
    lz_start()

    g_arrive()
    gram = unfold(jnp.sum(g_xy[...], axis=0))
    own_self = jnp.concatenate([noise_var * pivot_self, jnp.zeros((64, 64), f32)], axis=1)
    work = jnp.where(lane < 64, gram + own_self, jnp.where(lane == line + 64, 1.0, 0.0))

    def eliminate(work, low, high):
        for k in range(low, high):
            head = work[k : k + 1, :]
            factor = work[:, k : k + 1] * (1.0 / head[:, k : k + 1])
            work = work - jnp.where(line > k, factor, 0.0) * head
        return work

    work = eliminate(work, 0, 24)
    e_arrive()
    e_z[z] = jnp.sum(e_xy[...], axis=0)
    ez_start, ez_arrive, ez_left = along_z(e_z.at[z], e_z, ezs, ezr)
    ez_start()
    work = eliminate(work, 24, 64)
    diagonal = jnp.sum(jnp.where(lane == line, work, 0.0), axis=1, keepdims=True)
    lower_inv = pltpu.roll(work, 64, 1)[:, 0:64] * lax.rsqrt(diagonal)
    gram_inv = exact(lower_inv.T, lower_inv)
    mapped = exact(own_kernel_t, gram_inv)

    loop(0, 15, lambda k: z_copy(k).wait_send())
    x_left()
    loop(0, 16, lambda p: w_copy(p).wait_send())
    q_left()
    qx_left()
    s_left()
    g_left()
    l_left()
    e_left()

    lz_arrive()
    l_half[...] = jnp.sum(l_z[...], axis=0)
    u_copy = remote(l_half, l_other, us, ur)
    u_copy.start()
    lz_left()
    u_copy.wait()
    mine = l_half[...]
    other = l_other[...]
    projs = unfold(jnp.concatenate([jnp.where(core == 0, mine, other), jnp.where(core == 0, other, mine)], axis=0))
    solved = exact(gram_inv, projs)
    spread = exact(mapped, projs)

    def old(values):
        return pltpu.roll(values, 96, 1)

    proj_old = old(projs)
    solved_old = old(solved)
    spread_old = old(spread)
    removed_old = jnp.sum(proj_old * solved_old, axis=0, keepdims=True)

    ez_left()
    ez_arrive()
    curvature = jnp.sum(e_z[...], axis=0)
    cross = pltpu.roll(jnp.broadcast_to(curvature, (8, 128)), 96, 1)[0:1]
    square = pltpu.roll(jnp.broadcast_to(curvature, (8, 128)), 64, 1)[0:1]
    square_old = pltpu.roll(jnp.broadcast_to(curvature, (8, 128)), 32, 1)[0:1]
    norm_old = (square_old - removed_old) / noise_var
    step = norm_old / curvature
    residual_new = res_t - step * image
    proj_new = proj_old - step * projs
    solved_new = solved_old - step * solved
    square_new = square_old - 2.0 * step * cross + step * step * square
    norm_new = (square_new - jnp.sum(proj_new * solved_new, axis=0, keepdims=True)) / noise_var
    precond_new = (residual_new - (spread_old - step * spread)) / noise_var
    direction_new = precond_new + (norm_new / norm_old) * dir_t
    solution_new = sol_t + step * dir_t
    result[...] = jnp.where(
        lane < 32,
        solution_new,
        jnp.where(
            lane < 64,
            pltpu.roll(residual_new, 32, 1),
            jnp.where(lane < 96, pltpu.roll(direction_new, 64, 1), pltpu.roll(slope, 64, 1)),
        ),
    )


def turn_kernel(result, sol_out, res_out, dir_out, slope_out, stage):
    stage[0:64, :] = result[...]
    stage[64:128, :] = jnp.zeros((64, 128), f32)
    turned = stage[...].T
    sol_out[...] = turned[0:32, 0:64]
    res_out[...] = turned[32:64, 0:64]
    dir_out[...] = turned[64:96, 0:64]
    slope_out[...] = turned[96:128, 0:64]


def local(features, inv_scale, pivots, solution, residual, direction):
    vmem = pltpu.VMEM
    dma = pltpu.SemaphoreType.DMA
    one = dma(())
    many = dma((16,))
    fold32 = vmem((16, 32, 128), f32)
    flat32 = vmem((32, 128), f32)
    flat16 = vmem((16, 128), f32)
    flat1 = vmem((1, 128), f32)
    scratch = [
        vmem((64, 64), bf16), vmem((1, 64), f32), vmem((1, 64), jnp.int32),
        vmem((32, 64), f32), vmem((32, 64), f32), vmem((32, 64), f32),
        vmem((128, 128), f32), vmem((128, 128), f32),
        vmem((16, 48, 128), bf16), vmem((16, 48, 128), bf16), vmem((16, 64, 128), bf16),
        vmem((1024, 128), bf16), vmem((1024, 128), f32),
        fold32, fold32,
        vmem((16, 1, 128), f32), vmem((8, 128), f32), vmem((8, 128), f32), vmem((16, 8, 128), f32),
        flat32, flat32, flat32, fold32,
        flat32, flat32, flat32, fold32, flat32, vmem((16, 16, 128), f32), flat16, flat16,
        flat1, flat1, flat1, vmem((16, 1, 128), f32), vmem((16, 1, 128), f32),
        dma((6,)), many, many, many, many, many, many, many, many, many, many, one, one, many, many,
        one, one, many, many, one, one, many, many, many, many, one, one, one, one, many, many, many, many,
    ]
    result = pl.pallas_call(
        step_kernel,
        name="cg_step",
        out_shape=jax.ShapeDtypeStruct((64, 128), f32),
        in_specs=[pl.BlockSpec(memory_space=pltpu.HBM)] * 6,
        out_specs=pl.BlockSpec(memory_space=vmem),
        scratch_shapes=scratch,
        compiler_params=pltpu.CompilerParams(
            collective_id=0, has_side_effects=True, vmem_limit_bytes=60 * 1024 * 1024
        ),
    )(features, inv_scale[None, :], pivots[None, :], solution, residual, direction)
    return pl.pallas_call(
        turn_kernel,
        name="turn",
        out_shape=(jax.ShapeDtypeStruct((32, 64), f32),) * 4,
        in_specs=[pl.BlockSpec(memory_space=vmem)],
        out_specs=(pl.BlockSpec(memory_space=vmem),) * 4,
        scratch_shapes=[vmem((128, 128), f32)],
    )(result)


def solution(mesh):
    split = P(None, ("row", "col"))
    return jax.shard_map(
        local,
        mesh=mesh,
        in_specs=(split, P(), P(), split, split, split),
        out_specs=(split,) * 4,
        check_vma=False,
    )
```

```python
import jax
import jax.numpy as jnp
from jax import lax
from jax.experimental import pallas as pl
from jax.experimental.pallas import tpu as pltpu
from jax.sharding import PartitionSpec as P

noise_var = 1.0
MESH = pl.DeviceIdType.MESH
highest = lax.Precision.HIGHEST
f32 = jnp.float32
bf16 = jnp.bfloat16
NT = (((1,), (1,)), ((), ()))
NN = (((1,), (0,)), ((), ()))


def iota(shape, dim):
    return lax.broadcasted_iota(jnp.int32, shape, dim)


def loop(low, high, body):
    def step(k, carry):
        body(k)
        return carry

    lax.fori_loop(low, high, step, 0)


def exact(left, right, numbers=NN):
    return lax.dot_general(left, right, numbers, precision=highest, preferred_element_type=f32)


def kernel_of(left, right):
    return jnp.exp(lax.dot_general(left, right, NT, preferred_element_type=f32))


def forms(scaled, lane):
    norm = jnp.sum(scaled * scaled, axis=1, keepdims=True)
    high = norm.astype(bf16).astype(f32)
    rest = norm - high
    mid = rest.astype(bf16).astype(f32)
    low = (rest - mid).astype(bf16).astype(f32)
    place = lane - 32
    first = jnp.where(place == 0, high, jnp.where(place == 1, mid, jnp.where(place == 2, low, 0.0)))
    place = lane - 35
    second = jnp.where(place == 0, high, jnp.where(place == 1, mid, jnp.where(place == 2, low, 0.0)))
    in_first = (lane >= 32) & (lane < 35)
    in_second = (lane >= 35) & (lane < 38)
    row_form = scaled + second + jnp.where(in_first, -0.5, 0.0)
    col_form = scaled + first + jnp.where(in_second, -0.5, 0.0)
    return row_form, col_form


def unfold_block(blocks):
    count = blocks.shape[0]
    wide = blocks.astype(f32)
    lane = iota((count * 64, 128), 1)
    near = wide[:, 0:32]
    far = pltpu.roll(near.reshape(count * 32, 128), 64, 1).reshape(count, 32, 128)
    scaled = jnp.concatenate([near, far], axis=1).reshape(count * 64, 128)
    column = forms(jnp.where(lane >= 64, scaled, 0.0), lane)[1].astype(bf16)
    packed = wide[:, 32:48].reshape(count * 16, 128)

    def at(first):
        turned = [pltpu.roll(packed, (first - 32 * q) % 128, 1).reshape(count, 16, 128) for q in range(4)]
        return jnp.concatenate(turned, axis=1).reshape(count * 64, 128)

    plain = jnp.where(lane < 32, at(0), 0.0).astype(bf16)
    slope = jnp.where((lane >= 32) & (lane < 64), -2.0 * at(32), 0.0).astype(bf16)
    return column, plain, slope


def unfold(packed):
    return jnp.concatenate([packed, pltpu.roll(packed, 64, 1)], axis=0)


def step_kernel(
    feat_hbm, inv_hbm, piv_hbm, sol_hbm, res_hbm, dir_hbm,
    result,
    feat_in, inv_in, piv_in, sol_in, res_in, dir_in,
    stage_a, stage_b,
    zbuf, zsib, xbuf, colm, acc,
    part, part_xy,
    q_z, q_own, q_sib, q_xy,
    g_own, g_sib, g_sum, g_xy, g_half, g_other,
    l_own, l_sib, l_sum, l_xy, l_z, l_half, l_other,
    e_own, e_sib, e_sum, e_xy, e_z,
    in_sem, zs, zr, xs, xr, ws, wr, ps, pr, qs, qr, qcs, qcr, qxs, qxr,
    gs, gr, gxs, gxr, vs, vr, ls, lr, lxs, lxr, lzs, lzr, us, ur, es, er, exs, exr, ezs, ezr,
):
    row = lax.axis_index("row")
    col = lax.axis_index("col")
    xy = lax.rem(row, 16)
    core = lax.rem(col, 2)
    z = (col // 2) * 4 + row // 16

    def dev(z_at, xy_at, core_at):
        return (lax.rem(z_at, 4) * 16 + xy_at, (z_at // 4) * 2 + core_at)

    def z_shift(k):
        far = 8 - (k + 1) // 2
        return jnp.where(lax.rem(k, 2) == 1, far, 16 - far)

    def z_peer(k):
        return lax.rem(z + z_shift(k), 16)

    def xy_peer(k):
        return lax.rem(xy + k, 16)

    sibling = dev(z, xy, 1 - core)
    kept = pl.ds(pl.multiple_of(core * 16, 16), 16)
    given = pl.ds(pl.multiple_of((1 - core) * 16, 16), 16)

    def remote(src, dst, send, recv, where=sibling):
        return pltpu.make_async_remote_copy(
            src_ref=src, dst_ref=dst, send_sem=send, recv_sem=recv, device_id=where, device_id_type=MESH
        )

    def halves(mine, other):
        first = jnp.where(core == 0, mine, other)
        second = jnp.where(core == 0, other, mine)
        return unfold(jnp.concatenate([first, second], axis=0))

    def along_z(src, buf, send, recv):
        def copy(k):
            return remote(src, buf.at[z], send.at[k], recv.at[z], dev(z_peer(k), xy, core))

        def arrival(k):
            p = z_peer(k)
            return remote(src, buf.at[p], send.at[k], recv.at[p])

        return (
            lambda: loop(0, 15, lambda k: copy(k).start()),
            lambda: loop(0, 15, lambda k: arrival(k).wait_recv()),
            lambda: loop(0, 15, lambda k: copy(k).wait_send()),
        )

    def over_xy(src_of, buf, send, recv):
        def copy(k):
            p = xy_peer(k)
            return remote(src_of(p), buf.at[xy], send.at[k], recv.at[xy], dev(z, p, core))

        def arrival(k):
            p = xy_peer(k)
            return remote(src_of(p), buf.at[p], send.at[k], recv.at[p])

        return (
            lambda: loop(1, 16, lambda k: copy(k).start()),
            lambda: loop(1, 16, lambda k: arrival(k).wait_recv()),
            lambda: loop(1, 16, lambda k: copy(k).wait_send()),
        )

    barrier = pltpu.get_barrier_semaphore()

    def greet(where):
        pl.semaphore_signal(barrier, inc=1, device_id=where, device_id_type=MESH)

    loop(0, 15, lambda k: greet(dev(z_peer(k), xy, core)))
    loop(1, 16, lambda k: greet(dev(z, xy_peer(k), core)))
    greet(sibling)

    loads = [
        pltpu.make_async_copy(src, dst, in_sem.at[n])
        for n, (src, dst) in enumerate(
            (
                (feat_hbm, feat_in), (inv_hbm, inv_in), (piv_hbm, piv_in),
                (sol_hbm, sol_in), (res_hbm, res_in), (dir_hbm, dir_in),
            )
        )
    ]
    for load in loads:
        load.start()
    stage_a[...] = jnp.zeros((128, 128), f32)
    stage_b[...] = jnp.zeros((128, 128), f32)
    for load in loads:
        load.wait()

    lane = iota((64, 128), 1)
    line = iota((64, 128), 0)
    stage_a[0:32, 0:64] = dir_in[...]
    stage_a[64:128, 0:64] = feat_in[...].astype(f32)
    stage_b[0:32, 0:64] = res_in[...]
    stage_b[32:64, 0:64] = sol_in[...]
    turned = stage_a[...].T[0:64]
    others = stage_b[...].T[0:64]
    dir_t = jnp.where(lane < 32, turned, 0.0)
    res_t = jnp.where(lane < 32, others, 0.0)
    sol_t = jnp.where(lane < 32, pltpu.roll(others, 96, 1), 0.0)
    stage_a[0:1, 0:64] = inv_in[...]
    stage_a[0:1, 64:128] = jnp.zeros((1, 64), f32)
    inv_row = pltpu.roll(stage_a[0:8, :], 64, 1)[0:1]
    scaled = jnp.where(lane >= 64, (turned * inv_row).astype(bf16).astype(f32), 0.0)

    offset = (row * 8 + col) * 64
    hits = piv_in[...] == iota((64, 64), 0) + offset
    picked = jnp.max(jnp.where(hits, 1.0, 0.0), axis=1, keepdims=True)
    q_z[z] = jnp.sum(picked * scaled, axis=0, keepdims=True)
    row_form, col_form = forms(scaled, lane)
    own_row = row_form.astype(bf16)
    own_col = col_form.astype(bf16)
    zbuf[0, 0:32, :] = (scaled[0:32] + pltpu.roll(scaled[32:64], 64, 1)).astype(bf16)
    zbuf[0, 32:48, :] = sum(
        (pltpu.roll(dir_t[16 * q : 16 * q + 16], 32 * q, 1) for q in range(1, 4)), dir_t[0:16]
    ).astype(bf16)
    xbuf[xy] = own_row

    pl.semaphore_wait(barrier, 31)

    q_start, q_arrive, q_left = along_z(q_z.at[z], q_z, qs, qr)

    def z_near(k):
        far = 4 - k // 2
        return dev(lax.rem(z + jnp.where(lax.rem(k, 2) == 0, far, 16 - far), 16), xy, core)

    def z_copy(k):
        return remote(zbuf.at[0], zbuf.at[k + 1], zs.at[k], zr.at[k], z_near(k))

    def relay_up(k):
        return remote(zbuf.at[1], zbuf.at[k + 9], zs.at[k + 8], zr.at[k + 8], dev(lax.rem(z + 4 - k, 16), xy, core))

    def relay_down(k):
        return remote(zbuf.at[2], zbuf.at[k + 13], zs.at[k + 12], zr.at[k + 12], dev(lax.rem(z + 13 + k, 16), xy, core))

    def z_arrival(slot):
        remote(zbuf.at[0], zbuf.at[slot], zs.at[slot - 1], zr.at[slot - 1]).wait_recv()

    def w_copy(slot):
        return remote(zbuf.at[slot], zsib.at[slot], ws.at[slot], wr.at[slot])

    def receive(slot):
        z_arrival(slot)
        w_copy(slot).start()

    x_start, x_arrive, x_left = over_xy(lambda p: xbuf.at[xy], xbuf, xs, xr)
    loop(0, 8, lambda k: z_copy(k).start())
    q_start()
    x_start()
    w_copy(0).start()

    def tile(blocks, keep=None):
        cols, plain, slope = unfold_block(blocks)
        if keep is not None:
            colm[keep * 512 : keep * 512 + 512, :] = cols
        half = lax.dot_general(xbuf[...].reshape(1024, 128), cols, NT, preferred_element_type=f32)
        value = jnp.exp(half)
        images = jnp.dot(value.astype(bf16), plain, preferred_element_type=f32)
        return images + jnp.dot((value * half).astype(bf16), slope, preferred_element_type=f32)

    def sibling_lines(group):
        loop(group * 8, group * 8 + 8, lambda slot: w_copy(slot).wait_recv())
        return zsib[group * 8 : group * 8 + 8]

    z_arrival(1)
    loop(0, 4, lambda k: relay_up(k).start())
    z_arrival(2)
    loop(0, 3, lambda k: relay_down(k).start())
    loop(1, 3, lambda slot: w_copy(slot).start())
    loop(3, 9, receive)
    x_arrive()
    acc[...] = tile(zbuf[0:8], 0)

    q_arrive()
    line8 = iota((8, 128), 0)
    found = jnp.zeros((8, 128), f32)
    for low in range(4):
        lot = q_z[low] + q_z[4 + low] + q_z[8 + low] + q_z[12 + low]
        found = found + jnp.where(line8 == lax.rem(xy, 2) * 4 + low, lot, 0.0)
    q_own[...] = found
    qc_copy = remote(q_own, q_sib, qcs, qcr)
    qc_copy.start()

    acc[...] += tile(sibling_lines(0))
    qc_copy.wait()
    q_xy[xy] = q_own[...] + q_sib[...]
    qx_start, qx_arrive, qx_left = over_xy(lambda p: q_xy.at[xy], q_xy, qxs, qxr)
    qx_start()
    loop(9, 16, receive)
    acc[...] += tile(zbuf[8:16], 1)
    total = acc[...] + tile(sibling_lines(1))
    acc[...] = total

    total = total.reshape(16, 64, 128)
    upper = total[:, 0:32].reshape(512, 128)
    lower = total[:, 32:64].reshape(512, 128)
    part[...] = (upper + pltpu.roll(lower, 64, 1)).reshape(16, 32, 128)
    part_xy[xy] = part[xy]
    s_start, s_arrive, s_left = over_xy(lambda p: part.at[p], part_xy, ps, pr)
    s_start()

    qx_arrive()
    lots = [q_xy[2 * pair] + q_xy[2 * pair + 1] for pair in range(8)]
    pivot_row, pivot_col = forms(jnp.concatenate(lots, axis=0), lane)
    pivot_row = pivot_row.astype(bf16)
    pivot_col = pivot_col.astype(bf16)
    own_kernel = kernel_of(pivot_row, own_col)
    plane_kernel = kernel_of(pivot_col, xbuf[...].reshape(1024, 128))
    proj = exact(plane_kernel, acc[...])
    proj = jnp.where(lane < 32, proj, 0.0) + exact(own_kernel, noise_var * dir_t + pltpu.roll(res_t, 32, 1))
    l_own[...] = proj[0:32] + pltpu.roll(proj[32:64], 64, 1)
    l_copy = remote(l_own.at[given], l_sib, ls, lr)
    l_copy.start()

    line_kernel = kernel_of(pivot_row, colm[...])
    gram_part = exact(line_kernel, line_kernel, NT)
    wide = jnp.concatenate([gram_part, jnp.zeros((64, 64), f32)], axis=1)
    g_own[...] = wide[0:32] + pltpu.roll(wide[32:64], 64, 1)
    g_copy = remote(g_own.at[given], g_sib, gs, gr)
    g_copy.start()
    l_copy.wait()
    l_sum[...] = l_own[kept, :] + l_sib[...]
    l_xy[xy] = l_sum[...]
    l_start, l_arrive, l_left = over_xy(lambda p: l_sum, l_xy, lxs, lxr)
    l_start()
    own_kernel_t = kernel_of(own_row, pivot_col)
    pivot_self = kernel_of(pivot_row, pivot_col)
    g_copy.wait()
    g_sum[...] = g_own[kept, :] + g_sib[...]
    g_xy[xy] = g_sum[...]
    g_start, g_arrive, g_left = over_xy(lambda p: g_sum, g_xy, gxs, gxr)
    g_start()

    s_arrive()
    images = unfold(jnp.sum(part_xy[...], axis=0))
    image = jnp.where(lane < 32, images + noise_var * dir_t, 0.0)
    slope = jnp.where((lane >= 32) & (lane < 64), images, 0.0)
    sums = jnp.sum(
        dir_t * image
        + pltpu.roll(res_t * image, 32, 1)
        + pltpu.roll(image * image, 64, 1)
        + pltpu.roll(res_t * res_t, 96, 1),
        axis=0,
        keepdims=True,
    )
    e_own[...] = sums
    e_copy = remote(e_own, e_sib, es, er)
    e_copy.start()
    e_copy.wait()
    e_sum[...] = e_own[...] + e_sib[...]
    e_xy[xy] = e_sum[...]
    e_start, e_arrive, e_left = over_xy(lambda p: e_sum, e_xy, exs, exr)
    e_start()

    l_arrive()
    l_z[z] = jnp.sum(l_xy[...], axis=0)
    lz_start, lz_arrive, lz_left = along_z(l_z.at[z], l_z, lzs, lzr)
    lz_start()

    g_arrive()
    g_half[...] = jnp.sum(g_xy[...], axis=0)
    v_copy = remote(g_half, g_other, vs, vr)
    v_copy.start()
    e_arrive()
    e_z[z] = jnp.sum(e_xy[...], axis=0)
    ez_start, ez_arrive, ez_left = along_z(e_z.at[z], e_z, ezs, ezr)
    ez_start()
    v_copy.wait()
    gram = halves(g_half[...], g_other[...])
    own_self = jnp.concatenate([noise_var * pivot_self, jnp.zeros((64, 64), f32)], axis=1)
    work = jnp.where(lane < 64, gram + own_self, jnp.where(lane == line + 64, 1.0, 0.0))

    def eliminate(work, low, high):
        for k in range(low, high):
            head = work[k : k + 1, :]
            factor = work[:, k : k + 1] * (1.0 / head[:, k : k + 1])
            work = work - jnp.where(line > k, factor, 0.0) * head
        return work

    work = eliminate(work, 0, 64)
    diagonal = jnp.sum(jnp.where(lane == line, work, 0.0), axis=1, keepdims=True)
    lower_inv = pltpu.roll(work, 64, 1)[:, 0:64] * lax.rsqrt(diagonal)
    gram_inv = exact(lower_inv.T, lower_inv)
    mapped = exact(own_kernel_t, gram_inv)

    loop(0, 8, lambda k: z_copy(k).wait_send())
    loop(0, 4, lambda k: relay_up(k).wait_send())
    loop(0, 3, lambda k: relay_down(k).wait_send())
    x_left()
    loop(0, 16, lambda p: w_copy(p).wait_send())
    q_left()
    qx_left()
    s_left()
    g_left()
    l_left()
    e_left()

    lz_arrive()
    l_half[...] = jnp.sum(l_z[...], axis=0)
    u_copy = remote(l_half, l_other, us, ur)
    u_copy.start()
    lz_left()
    u_copy.wait()
    projs = halves(l_half[...], l_other[...])
    solved = exact(gram_inv, projs)
    spread = exact(mapped, projs)

    def old(values):
        return pltpu.roll(values, 96, 1)

    proj_old = old(projs)
    solved_old = old(solved)
    spread_old = old(spread)
    removed_old = jnp.sum(proj_old * solved_old, axis=0, keepdims=True)

    ez_left()
    ez_arrive()
    curvature = jnp.sum(e_z[...], axis=0)
    cross = pltpu.roll(jnp.broadcast_to(curvature, (8, 128)), 96, 1)[0:1]
    square = pltpu.roll(jnp.broadcast_to(curvature, (8, 128)), 64, 1)[0:1]
    square_old = pltpu.roll(jnp.broadcast_to(curvature, (8, 128)), 32, 1)[0:1]
    norm_old = (square_old - removed_old) / noise_var
    step = norm_old / curvature
    residual_new = res_t - step * image
    proj_new = proj_old - step * projs
    solved_new = solved_old - step * solved
    square_new = square_old - 2.0 * step * cross + step * step * square
    norm_new = (square_new - jnp.sum(proj_new * solved_new, axis=0, keepdims=True)) / noise_var
    precond_new = (residual_new - (spread_old - step * spread)) / noise_var
    direction_new = precond_new + (norm_new / norm_old) * dir_t
    solution_new = sol_t + step * dir_t
    result[...] = jnp.where(
        lane < 32,
        solution_new,
        jnp.where(
            lane < 64,
            pltpu.roll(residual_new, 32, 1),
            jnp.where(lane < 96, pltpu.roll(direction_new, 64, 1), pltpu.roll(slope, 64, 1)),
        ),
    )


def turn_kernel(result, sol_out, res_out, dir_out, slope_out, stage):
    stage[0:64, :] = result[...]
    stage[64:128, :] = jnp.zeros((64, 128), f32)
    turned = stage[...].T
    sol_out[...] = turned[0:32, 0:64]
    res_out[...] = turned[32:64, 0:64]
    dir_out[...] = turned[64:96, 0:64]
    slope_out[...] = turned[96:128, 0:64]


def local(features, inv_scale, pivots, solution, residual, direction):
    vmem = pltpu.VMEM
    dma = pltpu.SemaphoreType.DMA
    one = dma(())
    many = dma((16,))
    fold32 = vmem((16, 32, 128), f32)
    fold16 = vmem((16, 16, 128), f32)
    flat32 = vmem((32, 128), f32)
    flat16 = vmem((16, 128), f32)
    flat1 = vmem((1, 128), f32)
    scratch = [
        vmem((64, 64), bf16), vmem((1, 64), f32), vmem((1, 64), jnp.int32),
        vmem((32, 64), f32), vmem((32, 64), f32), vmem((32, 64), f32),
        vmem((128, 128), f32), vmem((128, 128), f32),
        vmem((16, 48, 128), bf16), vmem((16, 48, 128), bf16), vmem((16, 64, 128), bf16),
        vmem((1024, 128), bf16), vmem((1024, 128), f32),
        fold32, fold32,
        vmem((16, 1, 128), f32), vmem((8, 128), f32), vmem((8, 128), f32), vmem((16, 8, 128), f32),
        flat32, flat16, flat16, fold16, flat16, flat16,
        flat32, flat16, flat16, fold16, fold16, flat16, flat16,
        flat1, flat1, flat1, vmem((16, 1, 128), f32), vmem((16, 1, 128), f32),
        dma((6,)), many, many, many, many, many, many, many, many, many, many, one, one, many, many,
        one, one, many, many, one, one, one, one, many, many, many, many, one, one, one, one, many, many, many, many,
    ]
    result = pl.pallas_call(
        step_kernel,
        name="cg_step",
        out_shape=jax.ShapeDtypeStruct((64, 128), f32),
        in_specs=[pl.BlockSpec(memory_space=pltpu.HBM)] * 6,
        out_specs=pl.BlockSpec(memory_space=vmem),
        scratch_shapes=scratch,
        compiler_params=pltpu.CompilerParams(
            collective_id=0, has_side_effects=True, vmem_limit_bytes=60 * 1024 * 1024
        ),
    )(features, inv_scale[None, :], pivots[None, :], solution, residual, direction)
    return pl.pallas_call(
        turn_kernel,
        name="turn",
        out_shape=(jax.ShapeDtypeStruct((32, 64), f32),) * 4,
        in_specs=[pl.BlockSpec(memory_space=vmem)],
        out_specs=(pl.BlockSpec(memory_space=vmem),) * 4,
        scratch_shapes=[vmem((128, 128), f32)],
    )(result)


def solution(mesh):
    split = P(None, ("row", "col"))
    return jax.shard_map(
        local,
        mesh=mesh,
        in_specs=(split, P(), P(), split, split, split),
        out_specs=(split,) * 4,
        check_vma=False,
    )
```

```python
import jax
import jax.numpy as jnp
from jax import lax
from jax.experimental import pallas as pl
from jax.experimental.pallas import tpu as pltpu
from jax.sharding import PartitionSpec as P

noise_var = 1.0
MESH = pl.DeviceIdType.MESH
highest = lax.Precision.HIGHEST
f32 = jnp.float32
bf16 = jnp.bfloat16
NT = (((1,), (1,)), ((), ()))
NN = (((1,), (0,)), ((), ()))


def iota(shape, dim):
    return lax.broadcasted_iota(jnp.int32, shape, dim)


def loop(low, high, body):
    def step(k, carry):
        body(k)
        return carry

    lax.fori_loop(low, high, step, 0)


def each(low, high, body):
    for k in range(low, high):
        body(jnp.int32(k))


def exact(left, right, numbers=NN):
    return lax.dot_general(left, right, numbers, precision=highest, preferred_element_type=f32)


def kernel_of(left, right):
    return jnp.exp(lax.dot_general(left, right, NT, preferred_element_type=f32))


def forms(scaled, lane):
    norm = jnp.sum(scaled * scaled, axis=1, keepdims=True)
    high = norm.astype(bf16).astype(f32)
    rest = norm - high
    mid = rest.astype(bf16).astype(f32)
    low = (rest - mid).astype(bf16).astype(f32)
    place = lane - 32
    first = jnp.where(place == 0, high, jnp.where(place == 1, mid, jnp.where(place == 2, low, 0.0)))
    place = lane - 35
    second = jnp.where(place == 0, high, jnp.where(place == 1, mid, jnp.where(place == 2, low, 0.0)))
    in_first = (lane >= 32) & (lane < 35)
    in_second = (lane >= 35) & (lane < 38)
    row_form = scaled + second + jnp.where(in_first, -0.5, 0.0)
    col_form = scaled + first + jnp.where(in_second, -0.5, 0.0)
    return row_form, col_form


def unfold_block(blocks):
    count = blocks.shape[0]
    wide = blocks.astype(f32)
    lane = iota((count * 64, 128), 1)
    near = wide[:, 0:32]
    far = pltpu.roll(near.reshape(count * 32, 128), 64, 1).reshape(count, 32, 128)
    scaled = jnp.concatenate([near, far], axis=1).reshape(count * 64, 128)
    column = forms(jnp.where(lane >= 64, scaled, 0.0), lane)[1].astype(bf16)
    packed = wide[:, 32:48].reshape(count * 16, 128)

    def at(first):
        turned = [pltpu.roll(packed, (first - 32 * q) % 128, 1).reshape(count, 16, 128) for q in range(4)]
        return jnp.concatenate(turned, axis=1).reshape(count * 64, 128)

    plain = jnp.where(lane < 32, at(0), 0.0).astype(bf16)
    slope = jnp.where((lane >= 32) & (lane < 64), -2.0 * at(32), 0.0).astype(bf16)
    return column, plain, slope


def unfold(packed):
    return jnp.concatenate([packed, pltpu.roll(packed, 64, 1)], axis=0)


def step_kernel(
    feat_hbm, inv_hbm, piv_hbm, sol_hbm, res_hbm, dir_hbm,
    result,
    feat_in, inv_in, piv_in, sol_in, res_in, dir_in,
    stage_a, stage_b,
    zbuf, zsib, xbuf, colm, acc,
    part, part_xy, slopes, slopes_xy,
    q_z, q_own, q_sib, q_xy,
    g_own, g_sib, g_sum, g_xy, g_half, g_other,
    l_own, l_sib, l_sum, l_xy, l_z, l_half, l_other,
    e_own, e_sib, e_sum, e_xy, e_z,
    in_sem, zs, zr, xs, xr, ws, wr, ps, pr, ds, dr, qs, qr, qcs, qcr, qxs, qxr,
    gs, gr, gxs, gxr, vs, vr, ls, lr, lxs, lxr, lzs, lzr, us, ur, es, er, exs, exr, ezs, ezr,
):
    row = lax.axis_index("row")
    col = lax.axis_index("col")
    xy = lax.rem(row, 16)
    core = lax.rem(col, 2)
    z = (col // 2) * 4 + row // 16

    def dev(z_at, xy_at, core_at):
        return (lax.rem(z_at, 4) * 16 + xy_at, (z_at // 4) * 2 + core_at)

    def z_shift(k):
        far = 8 - (k + 1) // 2
        return jnp.where(lax.rem(k, 2) == 1, far, 16 - far)

    def z_peer(k):
        return lax.rem(z + z_shift(k), 16)

    def xy_peer(k):
        return lax.rem(xy + k, 16)

    sibling = dev(z, xy, 1 - core)
    kept = pl.ds(pl.multiple_of(core * 16, 16), 16)
    given = pl.ds(pl.multiple_of((1 - core) * 16, 16), 16)

    def remote(src, dst, send, recv, where=sibling):
        return pltpu.make_async_remote_copy(
            src_ref=src, dst_ref=dst, send_sem=send, recv_sem=recv, device_id=where, device_id_type=MESH
        )

    def halves(mine, other):
        first = jnp.where(core == 0, mine, other)
        second = jnp.where(core == 0, other, mine)
        return unfold(jnp.concatenate([first, second], axis=0))

    def along_z(src, buf, send, recv):
        def copy(k):
            return remote(src, buf.at[z], send.at[k], recv.at[z], dev(z_peer(k), xy, core))

        def arrival(k):
            p = z_peer(k)
            return remote(src, buf.at[p], send.at[k], recv.at[p])

        return (
            lambda: each(0, 15, lambda k: copy(k).start()),
            lambda: loop(0, 15, lambda k: arrival(k).wait_recv()),
            lambda: loop(0, 15, lambda k: copy(k).wait_send()),
        )

    def over_xy(src_of, buf, send, recv):
        def copy(k):
            p = xy_peer(k)
            return remote(src_of(p), buf.at[xy], send.at[k], recv.at[xy], dev(z, p, core))

        def arrival(k):
            p = xy_peer(k)
            return remote(src_of(p), buf.at[p], send.at[k], recv.at[p])

        return (
            lambda: each(1, 16, lambda k: copy(k).start()),
            lambda: loop(1, 16, lambda k: arrival(k).wait_recv()),
            lambda: loop(1, 16, lambda k: copy(k).wait_send()),
        )

    barrier = pltpu.get_barrier_semaphore()

    def greet(where):
        pl.semaphore_signal(barrier, inc=1, device_id=where, device_id_type=MESH)

    loop(0, 15, lambda k: greet(dev(z_peer(k), xy, core)))
    loop(1, 16, lambda k: greet(dev(z, xy_peer(k), core)))
    greet(sibling)

    loads = [
        pltpu.make_async_copy(src, dst, in_sem.at[n])
        for n, (src, dst) in enumerate(
            (
                (feat_hbm, feat_in), (inv_hbm, inv_in), (piv_hbm, piv_in),
                (sol_hbm, sol_in), (res_hbm, res_in), (dir_hbm, dir_in),
            )
        )
    ]
    for load in loads:
        load.start()
    stage_a[...] = jnp.zeros((128, 128), f32)
    stage_b[...] = jnp.zeros((128, 128), f32)
    for load in loads:
        load.wait()

    lane = iota((64, 128), 1)
    line = iota((64, 128), 0)
    stage_a[0:32, 0:64] = dir_in[...]
    stage_a[64:128, 0:64] = feat_in[...].astype(f32)
    stage_b[0:32, 0:64] = res_in[...]
    stage_b[32:64, 0:64] = sol_in[...]
    turned = stage_a[...].T[0:64]
    others = stage_b[...].T[0:64]
    dir_t = jnp.where(lane < 32, turned, 0.0)
    res_t = jnp.where(lane < 32, others, 0.0)
    sol_t = jnp.where(lane < 32, pltpu.roll(others, 96, 1), 0.0)
    stage_a[0:1, 0:64] = inv_in[...]
    stage_a[0:1, 64:128] = jnp.zeros((1, 64), f32)
    inv_row = pltpu.roll(stage_a[0:8, :], 64, 1)[0:1]
    scaled = jnp.where(lane >= 64, (turned * inv_row).astype(bf16).astype(f32), 0.0)

    offset = (row * 8 + col) * 64
    hits = piv_in[...] == iota((64, 64), 0) + offset
    picked = jnp.max(jnp.where(hits, 1.0, 0.0), axis=1, keepdims=True)
    q_z[z] = jnp.sum(picked * scaled, axis=0, keepdims=True)
    row_form, col_form = forms(scaled, lane)
    own_row = row_form.astype(bf16)
    own_col = col_form.astype(bf16)
    zbuf[0, 0:32, :] = (scaled[0:32] + pltpu.roll(scaled[32:64], 64, 1)).astype(bf16)
    zbuf[0, 32:48, :] = sum(
        (pltpu.roll(dir_t[16 * q : 16 * q + 16], 32 * q, 1) for q in range(1, 4)), dir_t[0:16]
    ).astype(bf16)
    xbuf[xy] = own_row

    pl.semaphore_wait(barrier, 31)

    q_start, q_arrive, q_left = along_z(q_z.at[z], q_z, qs, qr)

    def z_near(k):
        far = 4 - k // 2
        return dev(lax.rem(z + jnp.where(lax.rem(k, 2) == 0, far, 16 - far), 16), xy, core)

    def z_copy(k):
        return remote(zbuf.at[0], zbuf.at[k + 1], zs.at[k], zr.at[k], z_near(k))

    def relay_up(k):
        return remote(zbuf.at[1], zbuf.at[k + 9], zs.at[k + 8], zr.at[k + 8], dev(lax.rem(z + 4 - k, 16), xy, core))

    def relay_down(k):
        return remote(zbuf.at[2], zbuf.at[k + 13], zs.at[k + 12], zr.at[k + 12], dev(lax.rem(z + 13 + k, 16), xy, core))

    def z_arrival(slot):
        remote(zbuf.at[0], zbuf.at[slot], zs.at[slot - 1], zr.at[slot - 1]).wait_recv()

    def w_copy(slot):
        return remote(zbuf.at[slot], zsib.at[slot], ws.at[slot], wr.at[slot])

    def receive(slot):
        z_arrival(slot)
        w_copy(slot).start()

    x_start, x_arrive, x_left = over_xy(lambda p: xbuf.at[xy], xbuf, xs, xr)
    q_start()
    each(0, 8, lambda k: z_copy(k).start())
    x_start()
    w_copy(0).start()

    def tile(blocks, keep=None):
        cols, plain, slope = unfold_block(blocks)
        if keep is not None:
            colm[keep * 512 : keep * 512 + 512, :] = cols
        half = lax.dot_general(xbuf[...].reshape(1024, 128), cols, NT, preferred_element_type=f32)
        value = jnp.exp(half)
        images = jnp.dot(value.astype(bf16), plain, preferred_element_type=f32)
        return images + jnp.dot((value * half).astype(bf16), slope, preferred_element_type=f32)

    def sibling_lines(group):
        loop(group * 8, group * 8 + 8, lambda slot: w_copy(slot).wait_recv())
        return zsib[group * 8 : group * 8 + 8]

    z_arrival(1)
    each(0, 4, lambda k: relay_up(k).start())
    z_arrival(2)
    each(0, 3, lambda k: relay_down(k).start())
    loop(1, 3, lambda slot: w_copy(slot).start())
    loop(3, 9, receive)
    x_arrive()
    acc[...] = tile(zbuf[0:8], 0)

    q_arrive()
    line8 = iota((8, 128), 0)
    found = jnp.zeros((8, 128), f32)
    for low in range(4):
        lot = q_z[low] + q_z[4 + low] + q_z[8 + low] + q_z[12 + low]
        found = found + jnp.where(line8 == lax.rem(xy, 2) * 4 + low, lot, 0.0)
    q_own[...] = found
    qc_copy = remote(q_own, q_sib, qcs, qcr)
    qc_copy.start()

    acc[...] += tile(sibling_lines(0))
    qc_copy.wait()
    q_xy[xy] = q_own[...] + q_sib[...]
    qx_start, qx_arrive, qx_left = over_xy(lambda p: q_xy.at[xy], q_xy, qxs, qxr)
    qx_start()
    loop(9, 16, receive)
    acc[...] += tile(zbuf[8:16], 1)
    total = acc[...] + tile(sibling_lines(1))
    acc[...] = total

    quarters = total.reshape(16, 4, 16, 128)
    lane_q = iota((256, 128), 1)

    def pack(first):
        packed = jnp.zeros((256, 128), f32)
        for q in range(4):
            turned = pltpu.roll(quarters[:, q].reshape(256, 128), (32 * q - first) % 128, 1)
            packed = jnp.where((lane_q >= 32 * q) & (lane_q < 32 * q + 32), turned, packed)
        return packed.reshape(16, 16, 128)

    def unpack(packed, first):
        return jnp.concatenate([pltpu.roll(packed, (first - 32 * q) % 128, 1) for q in range(4)], axis=0)

    part[...] = pack(0)
    part_xy[xy] = part[xy]
    s_start, s_arrive, s_left = over_xy(lambda p: part.at[p], part_xy, ps, pr)
    s_start()
    slopes[...] = pack(32)
    slopes_xy[xy] = slopes[xy]
    d_start, d_arrive, d_left = over_xy(lambda p: slopes.at[p], slopes_xy, ds, dr)

    qx_arrive()
    lots = [q_xy[2 * pair] + q_xy[2 * pair + 1] for pair in range(8)]
    pivot_row, pivot_col = forms(jnp.concatenate(lots, axis=0), lane)
    pivot_row = pivot_row.astype(bf16)
    pivot_col = pivot_col.astype(bf16)
    own_kernel = kernel_of(pivot_row, own_col)
    plane_kernel = kernel_of(pivot_col, xbuf[...].reshape(1024, 128))
    proj = exact(plane_kernel, acc[...])
    proj = jnp.where(lane < 32, proj, 0.0) + exact(own_kernel, noise_var * dir_t + pltpu.roll(res_t, 32, 1))
    l_own[...] = proj[0:32] + pltpu.roll(proj[32:64], 64, 1)
    l_copy = remote(l_own.at[given], l_sib, ls, lr)
    l_copy.start()

    line_kernel = kernel_of(pivot_row, colm[...])
    gram_part = exact(line_kernel, line_kernel, NT)
    wide = jnp.concatenate([gram_part, jnp.zeros((64, 64), f32)], axis=1)
    g_own[...] = wide[0:32] + pltpu.roll(wide[32:64], 64, 1)
    g_copy = remote(g_own.at[given], g_sib, gs, gr)
    g_copy.start()
    l_copy.wait()
    l_sum[...] = l_own[kept, :] + l_sib[...]
    l_xy[xy] = l_sum[...]
    l_start, l_arrive, l_left = over_xy(lambda p: l_sum, l_xy, lxs, lxr)
    l_start()
    own_kernel_t = kernel_of(own_row, pivot_col)
    pivot_self = kernel_of(pivot_row, pivot_col)
    g_copy.wait()
    g_sum[...] = g_own[kept, :] + g_sib[...]
    g_xy[xy] = g_sum[...]
    g_start, g_arrive, g_left = over_xy(lambda p: g_sum, g_xy, gxs, gxr)
    g_start()

    s_arrive()
    images = unpack(jnp.sum(part_xy[...], axis=0), 0)
    image = jnp.where(lane < 32, images + noise_var * dir_t, 0.0)
    sums = jnp.sum(
        dir_t * image
        + pltpu.roll(res_t * image, 32, 1)
        + pltpu.roll(image * image, 64, 1)
        + pltpu.roll(res_t * res_t, 96, 1),
        axis=0,
        keepdims=True,
    )
    e_own[...] = sums
    e_copy = remote(e_own, e_sib, es, er)
    e_copy.start()
    e_copy.wait()
    e_sum[...] = e_own[...] + e_sib[...]
    e_xy[xy] = e_sum[...]
    e_start, e_arrive, e_left = over_xy(lambda p: e_sum, e_xy, exs, exr)
    e_start()
    d_start()

    l_arrive()
    l_z[z] = jnp.sum(l_xy[...], axis=0)
    lz_start, lz_arrive, lz_left = along_z(l_z.at[z], l_z, lzs, lzr)
    lz_start()

    g_arrive()
    g_half[...] = jnp.sum(g_xy[...], axis=0)
    v_copy = remote(g_half, g_other, vs, vr)
    v_copy.start()
    v_copy.wait()
    gram = halves(g_half[...], g_other[...])
    own_self = jnp.concatenate([noise_var * pivot_self, jnp.zeros((64, 64), f32)], axis=1)
    work = jnp.where(lane < 64, gram + own_self, jnp.where(lane == line + 64, 1.0, 0.0))

    def eliminate(work, low, high):
        for k in range(low, high):
            head = work[k : k + 1, :]
            factor = work[:, k : k + 1] * (1.0 / head[:, k : k + 1])
            work = work - jnp.where(line > k, factor, 0.0) * head
        return work

    work = eliminate(work, 0, 20)
    e_arrive()
    e_z[z] = jnp.sum(e_xy[...], axis=0)
    ez_start, ez_arrive, ez_left = along_z(e_z.at[z], e_z, ezs, ezr)
    ez_start()
    work = eliminate(work, 20, 64)
    diagonal = jnp.sum(jnp.where(lane == line, work, 0.0), axis=1, keepdims=True)
    lower_inv = pltpu.roll(work, 64, 1)[:, 0:64] * lax.rsqrt(diagonal)
    gram_inv = exact(lower_inv.T, lower_inv)
    mapped = exact(own_kernel_t, gram_inv)

    loop(0, 8, lambda k: z_copy(k).wait_send())
    loop(0, 4, lambda k: relay_up(k).wait_send())
    loop(0, 3, lambda k: relay_down(k).wait_send())
    x_left()
    loop(0, 16, lambda p: w_copy(p).wait_send())
    q_left()
    qx_left()
    s_left()
    g_left()
    l_left()
    e_left()
    d_arrive()
    d_left()
    slope = unpack(jnp.sum(slopes_xy[...], axis=0), 96)

    lz_arrive()
    l_half[...] = jnp.sum(l_z[...], axis=0)
    u_copy = remote(l_half, l_other, us, ur)
    u_copy.start()
    lz_left()
    u_copy.wait()
    projs = halves(l_half[...], l_other[...])
    solved = exact(gram_inv, projs)
    spread = exact(mapped, projs)

    def old(values):
        return pltpu.roll(values, 96, 1)

    proj_old = old(projs)
    solved_old = old(solved)
    spread_old = old(spread)
    removed_old = jnp.sum(proj_old * solved_old, axis=0, keepdims=True)

    ez_left()
    ez_arrive()
    curvature = jnp.sum(e_z[...], axis=0)
    cross = pltpu.roll(jnp.broadcast_to(curvature, (8, 128)), 96, 1)[0:1]
    square = pltpu.roll(jnp.broadcast_to(curvature, (8, 128)), 64, 1)[0:1]
    square_old = pltpu.roll(jnp.broadcast_to(curvature, (8, 128)), 32, 1)[0:1]
    norm_old = (square_old - removed_old) / noise_var
    step = norm_old / curvature
    residual_new = res_t - step * image
    proj_new = proj_old - step * projs
    solved_new = solved_old - step * solved
    square_new = square_old - 2.0 * step * cross + step * step * square
    norm_new = (square_new - jnp.sum(proj_new * solved_new, axis=0, keepdims=True)) / noise_var
    precond_new = (residual_new - (spread_old - step * spread)) / noise_var
    direction_new = precond_new + (norm_new / norm_old) * dir_t
    solution_new = sol_t + step * dir_t
    result[...] = jnp.where(
        lane < 32,
        solution_new,
        jnp.where(
            lane < 64,
            pltpu.roll(residual_new, 32, 1),
            jnp.where(lane < 96, pltpu.roll(direction_new, 64, 1), slope),
        ),
    )


def turn_kernel(result, sol_out, res_out, dir_out, slope_out, stage):
    stage[0:64, :] = result[...]
    stage[64:128, :] = jnp.zeros((64, 128), f32)
    turned = stage[...].T
    sol_out[...] = turned[0:32, 0:64]
    res_out[...] = turned[32:64, 0:64]
    dir_out[...] = turned[64:96, 0:64]
    slope_out[...] = turned[96:128, 0:64]


def local(features, inv_scale, pivots, solution, residual, direction):
    vmem = pltpu.VMEM
    dma = pltpu.SemaphoreType.DMA
    one = dma(())
    many = dma((16,))
    fold16 = vmem((16, 16, 128), f32)
    flat32 = vmem((32, 128), f32)
    flat16 = vmem((16, 128), f32)
    flat1 = vmem((1, 128), f32)
    scratch = [
        vmem((64, 64), bf16), vmem((1, 64), f32), vmem((1, 64), jnp.int32),
        vmem((32, 64), f32), vmem((32, 64), f32), vmem((32, 64), f32),
        vmem((128, 128), f32), vmem((128, 128), f32),
        vmem((16, 48, 128), bf16), vmem((16, 48, 128), bf16), vmem((16, 64, 128), bf16),
        vmem((1024, 128), bf16), vmem((1024, 128), f32),
        fold16, fold16, fold16, fold16,
        vmem((16, 1, 128), f32), vmem((8, 128), f32), vmem((8, 128), f32), vmem((16, 8, 128), f32),
        flat32, flat16, flat16, fold16, flat16, flat16,
        flat32, flat16, flat16, fold16, fold16, flat16, flat16,
        flat1, flat1, flat1, vmem((16, 1, 128), f32), vmem((16, 1, 128), f32),
        dma((6,)), many, many, many, many, many, many, many, many, many, many, many, many, one, one, many, many,
        one, one, many, many, one, one, one, one, many, many, many, many, one, one, one, one, many, many, many, many,
    ]
    result = pl.pallas_call(
        step_kernel,
        name="cg_step",
        out_shape=jax.ShapeDtypeStruct((64, 128), f32),
        in_specs=[pl.BlockSpec(memory_space=pltpu.HBM)] * 6,
        out_specs=pl.BlockSpec(memory_space=vmem),
        scratch_shapes=scratch,
        compiler_params=pltpu.CompilerParams(
            collective_id=0, has_side_effects=True, vmem_limit_bytes=60 * 1024 * 1024
        ),
    )(features, inv_scale[None, :], pivots[None, :], solution, residual, direction)
    return pl.pallas_call(
        turn_kernel,
        name="turn",
        out_shape=(jax.ShapeDtypeStruct((32, 64), f32),) * 4,
        in_specs=[pl.BlockSpec(memory_space=vmem)],
        out_specs=(pl.BlockSpec(memory_space=vmem),) * 4,
        scratch_shapes=[vmem((128, 128), f32)],
    )(result)


def solution(mesh):
    split = P(None, ("row", "col"))
    return jax.shard_map(
        local,
        mesh=mesh,
        in_specs=(split, P(), P(), split, split, split),
        out_specs=(split,) * 4,
        check_vma=False,
    )
```

```python
import jax
import jax.numpy as jnp
from jax import lax
from jax.experimental import pallas as pl
from jax.experimental.pallas import tpu as pltpu
from jax.sharding import PartitionSpec as P

noise_var = 1.0
MESH = pl.DeviceIdType.MESH
highest = lax.Precision.HIGHEST
f32 = jnp.float32
bf16 = jnp.bfloat16
NT = (((1,), (1,)), ((), ()))
NN = (((1,), (0,)), ((), ()))


def iota(shape, dim):
    return lax.broadcasted_iota(jnp.int32, shape, dim)


def loop(low, high, body):
    def step(k, carry):
        body(k)
        return carry

    lax.fori_loop(low, high, step, 0)


def each(low, high, body):
    for k in range(low, high):
        body(jnp.int32(k))


def exact(left, right, numbers=NN):
    return lax.dot_general(left, right, numbers, precision=highest, preferred_element_type=f32)


def kernel_of(left, right):
    return jnp.exp(lax.dot_general(left, right, NT, preferred_element_type=f32))


def forms(scaled, lane):
    norm = jnp.sum(scaled * scaled, axis=1, keepdims=True)
    high = norm.astype(bf16).astype(f32)
    rest = norm - high
    mid = rest.astype(bf16).astype(f32)
    low = (rest - mid).astype(bf16).astype(f32)
    place = lane - 32
    first = jnp.where(place == 0, high, jnp.where(place == 1, mid, jnp.where(place == 2, low, 0.0)))
    place = lane - 35
    second = jnp.where(place == 0, high, jnp.where(place == 1, mid, jnp.where(place == 2, low, 0.0)))
    in_first = (lane >= 32) & (lane < 35)
    in_second = (lane >= 35) & (lane < 38)
    row_form = scaled + second + jnp.where(in_first, -0.5, 0.0)
    col_form = scaled + first + jnp.where(in_second, -0.5, 0.0)
    return row_form, col_form


def unfold_block(blocks):
    count = blocks.shape[0]
    wide = blocks.astype(f32)
    lane = iota((count * 64, 128), 1)
    near = wide[:, 0:32]
    far = pltpu.roll(near.reshape(count * 32, 128), 64, 1).reshape(count, 32, 128)
    scaled = jnp.concatenate([near, far], axis=1).reshape(count * 64, 128)
    column = forms(jnp.where(lane >= 64, scaled, 0.0), lane)[1].astype(bf16)
    packed = wide[:, 32:48].reshape(count * 16, 128)

    def at(first):
        turned = [pltpu.roll(packed, (first - 32 * q) % 128, 1).reshape(count, 16, 128) for q in range(4)]
        return jnp.concatenate(turned, axis=1).reshape(count * 64, 128)

    plain = jnp.where(lane < 32, at(0), 0.0).astype(bf16)
    slope = jnp.where((lane >= 32) & (lane < 64), -2.0 * at(32), 0.0).astype(bf16)
    return column, plain, slope


def unfold(packed):
    return jnp.concatenate([packed, pltpu.roll(packed, 64, 1)], axis=0)


def step_kernel(
    feat_hbm, inv_hbm, piv_hbm, sol_hbm, res_hbm, dir_hbm,
    result,
    feat_in, inv_in, piv_in, sol_in, res_in, dir_in,
    stage_a, stage_b,
    zbuf, zsib, xbuf, colm, acc,
    part, part_xy, slopes, slopes_xy,
    q_z, q_own, q_sib, q_xy,
    g_own, g_sib, g_sum, g_xy, g_half, g_other,
    l_own, l_sib, l_sum, l_xy, l_z, l_half, l_other,
    e_own, e_sib, e_sum, e_xy, e_z,
    in_sem, zs, zr, xs, xr, ws, wr, ps, pr, ds, dr, qs, qr, qcs, qcr, qxs, qxr,
    gs, gr, gxs, gxr, vs, vr, ls, lr, lxs, lxr, lzs, lzr, us, ur, es, er, exs, exr, ezs, ezr,
):
    row = lax.axis_index("row")
    col = lax.axis_index("col")
    xy = lax.rem(row, 16)
    core = lax.rem(col, 2)
    z = (col // 2) * 4 + row // 16

    def dev(z_at, xy_at, core_at):
        return (lax.rem(z_at, 4) * 16 + xy_at, (z_at // 4) * 2 + core_at)

    def z_shift(k):
        far = 8 - (k + 1) // 2
        return jnp.where(lax.rem(k, 2) == 1, far, 16 - far)

    def z_peer(k):
        return lax.rem(z + z_shift(k), 16)

    def xy_peer(k):
        return lax.rem(xy + k, 16)

    sibling = dev(z, xy, 1 - core)
    kept = pl.ds(pl.multiple_of(core * 16, 16), 16)
    given = pl.ds(pl.multiple_of((1 - core) * 16, 16), 16)

    def remote(src, dst, send, recv, where=sibling):
        return pltpu.make_async_remote_copy(
            src_ref=src, dst_ref=dst, send_sem=send, recv_sem=recv, device_id=where, device_id_type=MESH
        )

    def halves(mine, other):
        first = jnp.where(core == 0, mine, other)
        second = jnp.where(core == 0, other, mine)
        return unfold(jnp.concatenate([first, second], axis=0))

    def exchange(count, copy, buf, send, recv):
        whole = remote(buf.at[0:count], buf.at[0:count], send, recv)
        return (lambda: each(0, count, lambda k: copy(k).start())), whole.wait_recv, whole.wait_send

    def along_z(src, buf, send, recv):
        return exchange(15, lambda k: remote(src, buf.at[z], send, recv, dev(z_peer(k), xy, core)), buf, send, recv)

    def over_xy(src_of, buf, send, recv):
        def copy(k):
            p = xy_peer(k + 1)
            return remote(src_of(p), buf.at[xy], send, recv, dev(z, p, core))

        return exchange(15, copy, buf, send, recv)

    barrier = pltpu.get_barrier_semaphore()

    def greet(where):
        pl.semaphore_signal(barrier, inc=1, device_id=where, device_id_type=MESH)

    loop(0, 15, lambda k: greet(dev(z_peer(k), xy, core)))
    loop(1, 16, lambda k: greet(dev(z, xy_peer(k), core)))
    greet(sibling)

    loads = [
        pltpu.make_async_copy(src, dst, in_sem.at[n])
        for n, (src, dst) in enumerate(
            (
                (feat_hbm, feat_in), (inv_hbm, inv_in), (piv_hbm, piv_in),
                (sol_hbm, sol_in), (res_hbm, res_in), (dir_hbm, dir_in),
            )
        )
    ]
    for load in loads:
        load.start()
    stage_a[...] = jnp.zeros((128, 128), f32)
    stage_b[...] = jnp.zeros((128, 128), f32)
    for load in loads:
        load.wait()

    lane = iota((64, 128), 1)
    line = iota((64, 128), 0)
    stage_a[0:32, 0:64] = dir_in[...]
    stage_a[64:128, 0:64] = feat_in[...].astype(f32)
    stage_b[0:32, 0:64] = res_in[...]
    stage_b[32:64, 0:64] = sol_in[...]
    turned = stage_a[...].T[0:64]
    others = stage_b[...].T[0:64]
    dir_t = jnp.where(lane < 32, turned, 0.0)
    res_t = jnp.where(lane < 32, others, 0.0)
    sol_t = jnp.where(lane < 32, pltpu.roll(others, 96, 1), 0.0)
    stage_a[0:1, 0:64] = inv_in[...]
    stage_a[0:1, 64:128] = jnp.zeros((1, 64), f32)
    inv_row = pltpu.roll(stage_a[0:8, :], 64, 1)[0:1]
    scaled = jnp.where(lane >= 64, (turned * inv_row).astype(bf16).astype(f32), 0.0)

    offset = (row * 8 + col) * 64
    hits = piv_in[...] == iota((64, 64), 0) + offset
    picked = jnp.max(jnp.where(hits, 1.0, 0.0), axis=1, keepdims=True)
    q_z[z] = jnp.sum(picked * scaled, axis=0, keepdims=True)
    row_form, col_form = forms(scaled, lane)
    own_row = row_form.astype(bf16)
    own_col = col_form.astype(bf16)
    zbuf[0, 0:32, :] = (scaled[0:32] + pltpu.roll(scaled[32:64], 64, 1)).astype(bf16)
    zbuf[0, 32:48, :] = sum(
        (pltpu.roll(dir_t[16 * q : 16 * q + 16], 32 * q, 1) for q in range(1, 4)), dir_t[0:16]
    ).astype(bf16)
    xbuf[xy] = own_row

    pl.semaphore_wait(barrier, 31)

    q_start, q_arrive, q_left = along_z(q_z.at[z], q_z, qs, qr)

    def z_near(k):
        far = 4 - k // 2
        return dev(lax.rem(z + jnp.where(lax.rem(k, 2) == 0, far, 16 - far), 16), xy, core)

    def z_copy(k):
        at = min(k, 2)
        return remote(zbuf.at[0], zbuf.at[k + 1], zs, zr.at[at], z_near(jnp.int32(k)))

    def relay_up(k):
        return remote(zbuf.at[1], zbuf.at[k + 9], zs, zr.at[3], dev(lax.rem(z + 4 - k, 16), xy, core))

    def relay_down(k):
        return remote(zbuf.at[2], zbuf.at[k + 13], zs, zr.at[3], dev(lax.rem(z + 13 + k, 16), xy, core))

    def z_arrival(slots, at):
        remote(zbuf.at[slots], zbuf.at[slots], zs, zr.at[at]).wait_recv()

    def z_left():
        remote(zbuf.at[0:15], zbuf.at[0:15], zs, zr.at[0]).wait_send()

    shared = [
        remote(zbuf.at[slots], zsib.at[slots], ws.at[n], wr.at[n])
        for n, slots in enumerate((pl.ds(0, 3), pl.ds(3, 6), pl.ds(9, 7)))
    ]

    x_start, x_arrive, x_left = over_xy(lambda p: xbuf.at[xy], xbuf, xs, xr)
    for k in range(2):
        z_copy(k).start()
    q_start()
    for k in range(2, 8):
        z_copy(k).start()
    x_start()

    def tile(blocks, keep=None):
        cols, plain, slope = unfold_block(blocks)
        if keep is not None:
            colm[keep * 512 : keep * 512 + 512, :] = cols
        half = lax.dot_general(xbuf[...].reshape(1024, 128), cols, NT, preferred_element_type=f32)
        value = jnp.exp(half)
        images = jnp.dot(value.astype(bf16), plain, preferred_element_type=f32)
        return images + jnp.dot((value * half).astype(bf16), slope, preferred_element_type=f32)

    z_arrival(pl.ds(1, 1), 0)
    for k in range(4):
        relay_up(k).start()
    z_arrival(pl.ds(2, 1), 1)
    for k in range(3):
        relay_down(k).start()
    shared[0].start()
    z_arrival(pl.ds(3, 6), 2)
    shared[1].start()
    x_arrive()
    acc[...] = tile(zbuf[0:8], 0)

    q_arrive()
    line8 = iota((8, 128), 0)
    found = jnp.zeros((8, 128), f32)
    for low in range(4):
        lot = q_z[low] + q_z[4 + low] + q_z[8 + low] + q_z[12 + low]
        found = found + jnp.where(line8 == lax.rem(xy, 2) * 4 + low, lot, 0.0)
    q_own[...] = found
    qc_copy = remote(q_own, q_sib, qcs, qcr)
    qc_copy.start()

    shared[0].wait_recv()
    shared[1].wait_recv()
    acc[...] += tile(zsib[0:8])
    qc_copy.wait()
    q_xy[xy] = q_own[...] + q_sib[...]
    qx_start, qx_arrive, qx_left = over_xy(lambda p: q_xy.at[xy], q_xy, qxs, qxr)
    qx_start()
    z_arrival(pl.ds(9, 7), 3)
    shared[2].start()
    acc[...] += tile(zbuf[8:16], 1)
    shared[2].wait_recv()
    total = acc[...] + tile(zsib[8:16])
    acc[...] = total

    quarters = total.reshape(16, 4, 16, 128)
    lane_q = iota((256, 128), 1)

    def pack(first):
        packed = jnp.zeros((256, 128), f32)
        for q in range(4):
            turned = pltpu.roll(quarters[:, q].reshape(256, 128), (32 * q - first) % 128, 1)
            packed = jnp.where((lane_q >= 32 * q) & (lane_q < 32 * q + 32), turned, packed)
        return packed.reshape(16, 16, 128)

    def unpack(packed, first):
        return jnp.concatenate([pltpu.roll(packed, (first - 32 * q) % 128, 1) for q in range(4)], axis=0)

    part[...] = pack(0)
    part_xy[xy] = part[xy]
    s_start, s_arrive, s_left = over_xy(lambda p: part.at[p], part_xy, ps, pr)
    s_start()
    slopes[...] = pack(32)
    slopes_xy[xy] = slopes[xy]
    d_start, d_arrive, d_left = over_xy(lambda p: slopes.at[p], slopes_xy, ds, dr)

    qx_arrive()
    lots = [q_xy[2 * pair] + q_xy[2 * pair + 1] for pair in range(8)]
    pivot_row, pivot_col = forms(jnp.concatenate(lots, axis=0), lane)
    pivot_row = pivot_row.astype(bf16)
    pivot_col = pivot_col.astype(bf16)
    own_kernel = kernel_of(pivot_row, own_col)
    plane_kernel = kernel_of(pivot_col, xbuf[...].reshape(1024, 128))
    proj = exact(plane_kernel, acc[...])
    proj = jnp.where(lane < 32, proj, 0.0) + exact(own_kernel, noise_var * dir_t + pltpu.roll(res_t, 32, 1))
    l_own[...] = proj[0:32] + pltpu.roll(proj[32:64], 64, 1)
    l_copy = remote(l_own.at[given], l_sib, ls, lr)
    l_copy.start()

    line_kernel = kernel_of(pivot_row, colm[...])
    gram_part = exact(line_kernel, line_kernel, NT)
    wide = jnp.concatenate([gram_part, jnp.zeros((64, 64), f32)], axis=1)
    g_own[...] = wide[0:32] + pltpu.roll(wide[32:64], 64, 1)
    g_copy = remote(g_own.at[given], g_sib, gs, gr)
    g_copy.start()
    l_copy.wait()
    l_sum[...] = l_own[kept, :] + l_sib[...]
    l_xy[xy] = l_sum[...]
    l_start, l_arrive, l_left = over_xy(lambda p: l_sum, l_xy, lxs, lxr)
    l_start()
    own_kernel_t = kernel_of(own_row, pivot_col)
    pivot_self = kernel_of(pivot_row, pivot_col)
    g_copy.wait()
    g_sum[...] = g_own[kept, :] + g_sib[...]
    g_xy[xy] = g_sum[...]
    g_start, g_arrive, g_left = over_xy(lambda p: g_sum, g_xy, gxs, gxr)
    g_start()

    s_arrive()
    images = unpack(jnp.sum(part_xy[...], axis=0), 0)
    image = jnp.where(lane < 32, images + noise_var * dir_t, 0.0)
    sums = jnp.sum(
        dir_t * image
        + pltpu.roll(res_t * image, 32, 1)
        + pltpu.roll(image * image, 64, 1)
        + pltpu.roll(res_t * res_t, 96, 1),
        axis=0,
        keepdims=True,
    )
    e_own[...] = sums
    e_copy = remote(e_own, e_sib, es, er)
    e_copy.start()
    z_left()
    for copy in shared:
        copy.wait_send()
    x_left()
    q_left()
    qx_left()
    s_left()
    e_copy.wait()
    e_sum[...] = e_own[...] + e_sib[...]
    e_xy[xy] = e_sum[...]
    e_start, e_arrive, e_left = over_xy(lambda p: e_sum, e_xy, exs, exr)
    e_start()
    d_start()

    l_arrive()
    l_z[z] = jnp.sum(l_xy[...], axis=0)
    lz_start, lz_arrive, lz_left = along_z(l_z.at[z], l_z, lzs, lzr)
    lz_start()

    g_arrive()
    g_half[...] = jnp.sum(g_xy[...], axis=0)
    v_copy = remote(g_half, g_other, vs, vr)
    v_copy.start()
    g_left()
    l_left()
    v_copy.wait()
    gram = halves(g_half[...], g_other[...])
    own_self = jnp.concatenate([noise_var * pivot_self, jnp.zeros((64, 64), f32)], axis=1)
    work = jnp.where(lane < 64, gram + own_self, jnp.where(lane == line + 64, 1.0, 0.0))

    def eliminate(work, low, high):
        for k in range(low, high):
            head = work[k : k + 1, :]
            factor = work[:, k : k + 1] * (1.0 / head[:, k : k + 1])
            work = work - jnp.where(line > k, factor, 0.0) * head
        return work

    work = eliminate(work, 0, 20)
    e_arrive()
    e_z[z] = jnp.sum(e_xy[...], axis=0)
    ez_start, ez_arrive, ez_left = along_z(e_z.at[z], e_z, ezs, ezr)
    ez_start()
    work = eliminate(work, 20, 64)
    diagonal = jnp.sum(jnp.where(lane == line, work, 0.0), axis=1, keepdims=True)
    lower_inv = pltpu.roll(work, 64, 1)[:, 0:64] * lax.rsqrt(diagonal)
    gram_inv = exact(lower_inv.T, lower_inv)
    mapped = exact(own_kernel_t, gram_inv)

    e_left()
    d_arrive()
    d_left()
    slope = unpack(jnp.sum(slopes_xy[...], axis=0), 96)

    lz_arrive()
    l_half[...] = jnp.sum(l_z[...], axis=0)
    u_copy = remote(l_half, l_other, us, ur)
    u_copy.start()
    lz_left()
    u_copy.wait()
    projs = halves(l_half[...], l_other[...])
    solved = exact(gram_inv, projs)
    spread = exact(mapped, projs)

    def old(values):
        return pltpu.roll(values, 96, 1)

    proj_old = old(projs)
    solved_old = old(solved)
    spread_old = old(spread)
    removed_old = jnp.sum(proj_old * solved_old, axis=0, keepdims=True)

    ez_left()
    ez_arrive()
    curvature = jnp.sum(e_z[...], axis=0)
    cross = pltpu.roll(jnp.broadcast_to(curvature, (8, 128)), 96, 1)[0:1]
    square = pltpu.roll(jnp.broadcast_to(curvature, (8, 128)), 64, 1)[0:1]
    square_old = pltpu.roll(jnp.broadcast_to(curvature, (8, 128)), 32, 1)[0:1]
    norm_old = (square_old - removed_old) / noise_var
    step = norm_old / curvature
    residual_new = res_t - step * image
    proj_new = proj_old - step * projs
    solved_new = solved_old - step * solved
    square_new = square_old - 2.0 * step * cross + step * step * square
    norm_new = (square_new - jnp.sum(proj_new * solved_new, axis=0, keepdims=True)) / noise_var
    precond_new = (residual_new - (spread_old - step * spread)) / noise_var
    direction_new = precond_new + (norm_new / norm_old) * dir_t
    solution_new = sol_t + step * dir_t
    result[...] = jnp.where(
        lane < 32,
        solution_new,
        jnp.where(
            lane < 64,
            pltpu.roll(residual_new, 32, 1),
            jnp.where(lane < 96, pltpu.roll(direction_new, 64, 1), slope),
        ),
    )


def turn_kernel(result, sol_out, res_out, dir_out, slope_out, stage):
    stage[0:64, :] = result[...]
    stage[64:128, :] = jnp.zeros((64, 128), f32)
    turned = stage[...].T
    sol_out[...] = turned[0:32, 0:64]
    res_out[...] = turned[32:64, 0:64]
    dir_out[...] = turned[64:96, 0:64]
    slope_out[...] = turned[96:128, 0:64]


def local(features, inv_scale, pivots, solution, residual, direction):
    vmem = pltpu.VMEM
    dma = pltpu.SemaphoreType.DMA
    one = dma(())
    fold16 = vmem((16, 16, 128), f32)
    flat32 = vmem((32, 128), f32)
    flat16 = vmem((16, 128), f32)
    flat1 = vmem((1, 128), f32)
    scratch = [
        vmem((64, 64), bf16), vmem((1, 64), f32), vmem((1, 64), jnp.int32),
        vmem((32, 64), f32), vmem((32, 64), f32), vmem((32, 64), f32),
        vmem((128, 128), f32), vmem((128, 128), f32),
        vmem((16, 48, 128), bf16), vmem((16, 48, 128), bf16), vmem((16, 64, 128), bf16),
        vmem((1024, 128), bf16), vmem((1024, 128), f32),
        fold16, fold16, fold16, fold16,
        vmem((16, 1, 128), f32), vmem((8, 128), f32), vmem((8, 128), f32), vmem((16, 8, 128), f32),
        flat32, flat16, flat16, fold16, flat16, flat16,
        flat32, flat16, flat16, fold16, fold16, flat16, flat16,
        flat1, flat1, flat1, vmem((16, 1, 128), f32), vmem((16, 1, 128), f32),
        dma((6,)), one, dma((4,)), one, one, dma((3,)), dma((3,)), *[one] * 30,
    ]
    result = pl.pallas_call(
        step_kernel,
        name="cg_step",
        out_shape=jax.ShapeDtypeStruct((64, 128), f32),
        in_specs=[pl.BlockSpec(memory_space=pltpu.HBM)] * 6,
        out_specs=pl.BlockSpec(memory_space=vmem),
        scratch_shapes=scratch,
        compiler_params=pltpu.CompilerParams(
            collective_id=0, has_side_effects=True, vmem_limit_bytes=60 * 1024 * 1024
        ),
    )(features, inv_scale[None, :], pivots[None, :], solution, residual, direction)
    return pl.pallas_call(
        turn_kernel,
        name="turn",
        out_shape=(jax.ShapeDtypeStruct((32, 64), f32),) * 4,
        in_specs=[pl.BlockSpec(memory_space=vmem)],
        out_specs=(pl.BlockSpec(memory_space=vmem),) * 4,
        scratch_shapes=[vmem((128, 128), f32)],
    )(result)


def solution(mesh):
    split = P(None, ("row", "col"))
    return jax.shard_map(
        local,
        mesh=mesh,
        in_specs=(split, P(), P(), split, split, split),
        out_specs=(split,) * 4,
        check_vma=False,
    )
```

```python
import jax
import jax.numpy as jnp
from jax import lax
from jax.experimental import pallas as pl
from jax.experimental.pallas import tpu as pltpu
from jax.sharding import PartitionSpec as P

noise_var = 1.0
MESH = pl.DeviceIdType.MESH
highest = lax.Precision.HIGHEST
f32 = jnp.float32
bf16 = jnp.bfloat16
NT = (((1,), (1,)), ((), ()))
NN = (((1,), (0,)), ((), ()))


def iota(shape, dim):
    return lax.broadcasted_iota(jnp.int32, shape, dim)


def loop(low, high, body):
    def step(k, carry):
        body(k)
        return carry

    lax.fori_loop(low, high, step, 0)


def each(low, high, body):
    for k in range(low, high):
        body(jnp.int32(k))


def exact(left, right, numbers=NN):
    return lax.dot_general(left, right, numbers, precision=highest, preferred_element_type=f32)


def kernel_of(left, right):
    return jnp.exp(lax.dot_general(left, right, NT, preferred_element_type=f32))


def forms(scaled, lane):
    norm = jnp.sum(scaled * scaled, axis=1, keepdims=True)
    high = norm.astype(bf16).astype(f32)
    rest = norm - high
    mid = rest.astype(bf16).astype(f32)
    low = (rest - mid).astype(bf16).astype(f32)
    place = lane - 32
    first = jnp.where(place == 0, high, jnp.where(place == 1, mid, jnp.where(place == 2, low, 0.0)))
    place = lane - 35
    second = jnp.where(place == 0, high, jnp.where(place == 1, mid, jnp.where(place == 2, low, 0.0)))
    in_first = (lane >= 32) & (lane < 35)
    in_second = (lane >= 35) & (lane < 38)
    row_form = scaled + second + jnp.where(in_first, -0.5, 0.0)
    col_form = scaled + first + jnp.where(in_second, -0.5, 0.0)
    return row_form, col_form


def unfold_block(blocks):
    count = blocks.shape[0]
    wide = blocks.astype(f32)
    lane = iota((count * 64, 128), 1)
    near = wide[:, 0:32]
    far = pltpu.roll(near.reshape(count * 32, 128), 64, 1).reshape(count, 32, 128)
    scaled = jnp.concatenate([near, far], axis=1).reshape(count * 64, 128)
    column = forms(jnp.where(lane >= 64, scaled, 0.0), lane)[1].astype(bf16)
    packed = wide[:, 32:48].reshape(count * 16, 128)

    def at(first):
        turned = [pltpu.roll(packed, (first - 32 * q) % 128, 1).reshape(count, 16, 128) for q in range(4)]
        return jnp.concatenate(turned, axis=1).reshape(count * 64, 128)

    plain = jnp.where(lane < 32, at(0), 0.0).astype(bf16)
    slope = jnp.where((lane >= 32) & (lane < 64), -2.0 * at(32), 0.0).astype(bf16)
    return column, plain, slope


def unfold(packed):
    return jnp.concatenate([packed, pltpu.roll(packed, 64, 1)], axis=0)


def step_kernel(
    feat_hbm, inv_hbm, piv_hbm, sol_hbm, res_hbm, dir_hbm,
    result,
    feat_in, inv_in, piv_in, sol_in, res_in, dir_in,
    stage_a, stage_b,
    zbuf, zsib, xbuf, colm, acc,
    part, part_xy, slopes, slopes_xy,
    q_z, q_own, q_sib, q_xy,
    g_own, g_sib, g_sum, g_xy, g_half, g_other,
    l_own, l_sib, l_sum, l_xy, l_z, l_half, l_other,
    e_own, e_sib, e_sum, e_xy, e_z,
    in_sem, zs, zr, xs, xr, ws, wr, ps, pr, ds, dr, qs, qr, qcs, qcr, qxs, qxr,
    gs, gr, gxs, gxr, vs, vr, ls, lr, lxs, lxr, lzs, lzr, us, ur, es, er, exs, exr, ezs, ezr,
):
    row = lax.axis_index("row")
    col = lax.axis_index("col")
    xy = lax.rem(row, 16)
    core = lax.rem(col, 2)
    z = (col // 2) * 4 + row // 16

    def dev(z_at, xy_at, core_at):
        return (lax.rem(z_at, 4) * 16 + xy_at, (z_at // 4) * 2 + core_at)

    def z_shift(k):
        far = 8 - (k + 1) // 2
        return jnp.where(lax.rem(k, 2) == 1, far, 16 - far)

    def z_peer(k):
        return lax.rem(z + z_shift(k), 16)

    def xy_peer(k):
        return lax.rem(xy + k, 16)

    sibling = dev(z, xy, 1 - core)
    kept = pl.ds(pl.multiple_of(core * 16, 16), 16)
    given = pl.ds(pl.multiple_of((1 - core) * 16, 16), 16)

    def remote(src, dst, send, recv, where=sibling):
        return pltpu.make_async_remote_copy(
            src_ref=src, dst_ref=dst, send_sem=send, recv_sem=recv, device_id=where, device_id_type=MESH
        )

    def halves(mine, other):
        first = jnp.where(core == 0, mine, other)
        second = jnp.where(core == 0, other, mine)
        return unfold(jnp.concatenate([first, second], axis=0))

    def exchange(count, copy, buf, send, recv):
        whole = remote(buf.at[0:count], buf.at[0:count], send, recv)
        return (lambda: each(0, count, lambda k: copy(k).start())), whole.wait_recv, whole.wait_send

    def along_z(src, buf, send, recv):
        return exchange(15, lambda k: remote(src, buf.at[z], send, recv, dev(z_peer(k), xy, core)), buf, send, recv)

    def over_xy(src_of, buf, send, recv):
        def copy(k):
            p = xy_peer(k + 1)
            return remote(src_of(p), buf.at[xy], send, recv, dev(z, p, core))

        return exchange(15, copy, buf, send, recv)

    barrier = pltpu.get_barrier_semaphore()

    def greet(where):
        pl.semaphore_signal(barrier, inc=1, device_id=where, device_id_type=MESH)

    loop(0, 15, lambda k: greet(dev(z_peer(k), xy, core)))
    loop(1, 16, lambda k: greet(dev(z, xy_peer(k), core)))
    greet(sibling)

    loads = [
        pltpu.make_async_copy(src, dst, in_sem.at[n])
        for n, (src, dst) in enumerate(
            (
                (feat_hbm, feat_in), (inv_hbm, inv_in), (piv_hbm, piv_in),
                (sol_hbm, sol_in), (res_hbm, res_in), (dir_hbm, dir_in),
            )
        )
    ]
    for load in loads:
        load.start()
    stage_a[...] = jnp.zeros((128, 128), f32)
    stage_b[...] = jnp.zeros((128, 128), f32)
    for load in loads:
        load.wait()

    lane = iota((64, 128), 1)
    line = iota((64, 128), 0)
    stage_a[0:32, 0:64] = dir_in[...]
    stage_a[64:128, 0:64] = feat_in[...].astype(f32)
    stage_b[0:32, 0:64] = res_in[...]
    stage_b[32:64, 0:64] = sol_in[...]
    turned = stage_a[...].T[0:64]
    others = stage_b[...].T[0:64]
    dir_t = jnp.where(lane < 32, turned, 0.0)
    res_t = jnp.where(lane < 32, others, 0.0)
    sol_t = jnp.where(lane < 32, pltpu.roll(others, 96, 1), 0.0)
    stage_a[0:1, 0:64] = inv_in[...]
    stage_a[0:1, 64:128] = jnp.zeros((1, 64), f32)
    inv_row = pltpu.roll(stage_a[0:8, :], 64, 1)[0:1]
    scaled = jnp.where(lane >= 64, (turned * inv_row).astype(bf16).astype(f32), 0.0)

    offset = (row * 8 + col) * 64
    hits = piv_in[...] == iota((64, 64), 0) + offset
    picked = jnp.max(jnp.where(hits, 1.0, 0.0), axis=1, keepdims=True)
    q_z[z] = jnp.sum(picked * scaled, axis=0, keepdims=True)
    row_form, col_form = forms(scaled, lane)
    own_row = row_form.astype(bf16)
    own_col = col_form.astype(bf16)
    zbuf[0, 0:32, :] = (scaled[0:32] + pltpu.roll(scaled[32:64], 64, 1)).astype(bf16)
    zbuf[0, 32:48, :] = sum(
        (pltpu.roll(dir_t[16 * q : 16 * q + 16], 32 * q, 1) for q in range(1, 4)), dir_t[0:16]
    ).astype(bf16)
    xbuf[xy] = own_row

    pl.semaphore_wait(barrier, 31)

    q_start, q_arrive, q_left = along_z(q_z.at[z], q_z, qs, qr)

    def z_near(k):
        far = 4 - k // 2
        return dev(lax.rem(z + jnp.where(lax.rem(k, 2) == 0, far, 16 - far), 16), xy, core)

    def z_copy(k):
        at = min(k, 2)
        return remote(zbuf.at[0], zbuf.at[k + 1], zs, zr.at[at], z_near(jnp.int32(k)))

    def relay_up(k):
        return remote(zbuf.at[1], zbuf.at[k + 9], zs, zr.at[3], dev(lax.rem(z + 4 - k, 16), xy, core))

    def relay_down(k):
        return remote(zbuf.at[2], zbuf.at[k + 13], zs, zr.at[3], dev(lax.rem(z + 13 + k, 16), xy, core))

    def z_arrival(slots, at):
        remote(zbuf.at[slots], zbuf.at[slots], zs, zr.at[at]).wait_recv()

    def z_left():
        remote(zbuf.at[0:15], zbuf.at[0:15], zs, zr.at[0]).wait_send()

    shared = [
        remote(zbuf.at[slots], zsib.at[slots], ws.at[n], wr.at[n])
        for n, slots in enumerate((pl.ds(0, 3), pl.ds(3, 6), pl.ds(9, 7)))
    ]

    x_start, x_arrive, x_left = over_xy(lambda p: xbuf.at[xy], xbuf, xs, xr)
    for k in range(2):
        z_copy(k).start()
    q_start()
    for k in range(2, 8):
        z_copy(k).start()
    x_start()

    def tile(blocks, keep=None):
        cols, plain, slope = unfold_block(blocks)
        if keep is not None:
            colm[keep * 512 : keep * 512 + 512, :] = cols
        half = lax.dot_general(xbuf[...].reshape(1024, 128), cols, NT, preferred_element_type=f32)
        value = jnp.exp(half)
        images = jnp.dot(value.astype(bf16), plain, preferred_element_type=f32)
        return images + jnp.dot((value * half).astype(bf16), slope, preferred_element_type=f32)

    z_arrival(pl.ds(1, 1), 0)
    for k in range(4):
        relay_up(k).start()
    z_arrival(pl.ds(2, 1), 1)
    for k in range(3):
        relay_down(k).start()
    shared[0].start()
    z_arrival(pl.ds(3, 6), 2)
    shared[1].start()
    x_arrive()
    acc[...] = tile(zbuf[0:8], 0)

    q_arrive()
    line8 = iota((8, 128), 0)
    found = jnp.zeros((8, 128), f32)
    for low in range(4):
        lot = q_z[low] + q_z[4 + low] + q_z[8 + low] + q_z[12 + low]
        found = found + jnp.where(line8 == lax.rem(xy, 2) * 4 + low, lot, 0.0)
    q_own[...] = found
    qc_copy = remote(q_own, q_sib, qcs, qcr)
    qc_copy.start()

    shared[0].wait_recv()
    shared[1].wait_recv()
    acc[...] += tile(zsib[0:8])
    qc_copy.wait()
    q_xy[xy] = q_own[...] + q_sib[...]
    qx_start, qx_arrive, qx_left = over_xy(lambda p: q_xy.at[xy], q_xy, qxs, qxr)
    qx_start()
    z_arrival(pl.ds(9, 7), 3)
    shared[2].start()
    acc[...] += tile(zbuf[8:16], 1)
    shared[2].wait_recv()
    total = acc[...] + tile(zsib[8:16])
    acc[...] = total

    quarters = total.reshape(16, 4, 16, 128)
    lane_q = iota((256, 128), 1)

    def pack(first):
        packed = jnp.zeros((256, 128), f32)
        for q in range(4):
            turned = pltpu.roll(quarters[:, q].reshape(256, 128), (32 * q - first) % 128, 1)
            packed = jnp.where((lane_q >= 32 * q) & (lane_q < 32 * q + 32), turned, packed)
        return packed.reshape(16, 16, 128)

    def unpack(packed, first):
        return jnp.concatenate([pltpu.roll(packed, (first - 32 * q) % 128, 1) for q in range(4)], axis=0)

    part[...] = pack(0)
    part_xy[xy] = part[xy]
    s_start, s_arrive, s_left = over_xy(lambda p: part.at[p], part_xy, ps, pr)
    s_start()
    slopes[...] = pack(32)
    slopes_xy[xy] = slopes[xy]
    d_start, d_arrive, d_left = over_xy(lambda p: slopes.at[p], slopes_xy, ds, dr)

    qx_arrive()
    lots = [q_xy[2 * pair] + q_xy[2 * pair + 1] for pair in range(8)]
    pivot_row, pivot_col = forms(jnp.concatenate(lots, axis=0), lane)
    pivot_row = pivot_row.astype(bf16)
    pivot_col = pivot_col.astype(bf16)
    own_kernel = kernel_of(pivot_row, own_col)
    plane_kernel = kernel_of(pivot_col, xbuf[...].reshape(1024, 128))
    proj = exact(plane_kernel, acc[...])
    proj = jnp.where(lane < 32, proj, 0.0) + exact(own_kernel, noise_var * dir_t + pltpu.roll(res_t, 32, 1))
    l_own[...] = proj[0:32] + pltpu.roll(proj[32:64], 64, 1)
    l_copy = remote(l_own.at[given], l_sib, ls, lr)
    l_copy.start()

    line_kernel = kernel_of(pivot_row, colm[...])
    gram_part = exact(line_kernel, line_kernel, NT)
    wide = jnp.concatenate([gram_part, jnp.zeros((64, 64), f32)], axis=1)
    g_own[...] = wide[0:32] + pltpu.roll(wide[32:64], 64, 1)
    g_copy = remote(g_own.at[given], g_sib, gs, gr)
    g_copy.start()
    l_copy.wait()
    l_sum[...] = l_own[kept, :] + l_sib[...]
    l_xy[xy] = l_sum[...]
    l_start, l_arrive, l_left = over_xy(lambda p: l_sum, l_xy, lxs, lxr)
    l_start()
    own_kernel_t = kernel_of(own_row, pivot_col)
    pivot_self = kernel_of(pivot_row, pivot_col)
    g_copy.wait()
    g_sum[...] = g_own[kept, :] + g_sib[...]
    g_xy[xy] = g_sum[...]
    g_start, g_arrive, g_left = over_xy(lambda p: g_sum, g_xy, gxs, gxr)
    g_start()

    s_arrive()
    images = unpack(jnp.sum(part_xy[...], axis=0), 0)
    image = jnp.where(lane < 32, images + noise_var * dir_t, 0.0)
    sums = jnp.sum(
        dir_t * image
        + pltpu.roll(res_t * image, 32, 1)
        + pltpu.roll(image * image, 64, 1)
        + pltpu.roll(res_t * res_t, 96, 1),
        axis=0,
        keepdims=True,
    )
    e_own[...] = sums
    e_copy = remote(e_own, e_sib, es, er)
    e_copy.start()
    z_left()
    for copy in shared:
        copy.wait_send()
    x_left()
    q_left()
    qx_left()
    s_left()
    e_copy.wait()
    e_sum[...] = e_own[...] + e_sib[...]
    e_xy[xy] = e_sum[...]
    e_start, e_arrive, e_left = over_xy(lambda p: e_sum, e_xy, exs, exr)
    e_start()

    l_arrive()
    l_z[z] = jnp.sum(l_xy[...], axis=0)
    lz_start, lz_arrive, lz_left = along_z(l_z.at[z], l_z, lzs, lzr)
    lz_start()
    e_arrive()
    e_z[z] = jnp.sum(e_xy[...], axis=0)
    ez_start, ez_arrive, ez_left = along_z(e_z.at[z], e_z, ezs, ezr)
    ez_start()
    d_start()

    g_arrive()
    g_half[...] = jnp.sum(g_xy[...], axis=0)
    v_copy = remote(g_half, g_other, vs, vr)
    v_copy.start()
    g_left()
    l_left()
    v_copy.wait()
    gram = halves(g_half[...], g_other[...])
    own_self = jnp.concatenate([noise_var * pivot_self, jnp.zeros((64, 64), f32)], axis=1)
    work = jnp.where(lane < 64, gram + own_self, jnp.where(lane == line + 64, 1.0, 0.0))

    done = []
    for panel in range(8):
        count = 64 - 8 * panel
        below = iota((count, 128), 0)
        cols = [jnp.broadcast_to(work[:, 8 * panel + j : 8 * panel + j + 1], (count, 128)) for j in range(8)]
        for k in range(8):
            factor = jnp.where(below > k, cols[k] * (1.0 / cols[k][k : k + 1]), 0.0)
            work = work - factor * work[k : k + 1]
            for j in range(k + 1, 8):
                cols[j] = cols[j] - factor * cols[j][k : k + 1]
        done.append(work[0:8])
        work = work[8:]
    work = jnp.concatenate(done, axis=0)
    diagonal = jnp.sum(jnp.where(lane == line, work, 0.0), axis=1, keepdims=True)
    lower_inv = pltpu.roll(work, 64, 1)[:, 0:64] * lax.rsqrt(diagonal)
    gram_inv = exact(lower_inv.T, lower_inv)
    mapped = exact(own_kernel_t, gram_inv)

    e_left()
    d_arrive()
    d_left()
    slope = unpack(jnp.sum(slopes_xy[...], axis=0), 96)

    lz_arrive()
    l_half[...] = jnp.sum(l_z[...], axis=0)
    u_copy = remote(l_half, l_other, us, ur)
    u_copy.start()
    lz_left()
    u_copy.wait()
    projs = halves(l_half[...], l_other[...])
    solved = exact(gram_inv, projs)
    spread = exact(mapped, projs)

    def old(values):
        return pltpu.roll(values, 96, 1)

    proj_old = old(projs)
    solved_old = old(solved)
    spread_old = old(spread)
    removed_old = jnp.sum(proj_old * solved_old, axis=0, keepdims=True)

    ez_left()
    ez_arrive()
    curvature = jnp.sum(e_z[...], axis=0)
    cross = pltpu.roll(jnp.broadcast_to(curvature, (8, 128)), 96, 1)[0:1]
    square = pltpu.roll(jnp.broadcast_to(curvature, (8, 128)), 64, 1)[0:1]
    square_old = pltpu.roll(jnp.broadcast_to(curvature, (8, 128)), 32, 1)[0:1]
    norm_old = (square_old - removed_old) / noise_var
    step = norm_old / curvature
    residual_new = res_t - step * image
    proj_new = proj_old - step * projs
    solved_new = solved_old - step * solved
    square_new = square_old - 2.0 * step * cross + step * step * square
    norm_new = (square_new - jnp.sum(proj_new * solved_new, axis=0, keepdims=True)) / noise_var
    precond_new = (residual_new - (spread_old - step * spread)) / noise_var
    direction_new = precond_new + (norm_new / norm_old) * dir_t
    solution_new = sol_t + step * dir_t
    result[...] = jnp.where(
        lane < 32,
        solution_new,
        jnp.where(
            lane < 64,
            pltpu.roll(residual_new, 32, 1),
            jnp.where(lane < 96, pltpu.roll(direction_new, 64, 1), slope),
        ),
    )


def turn_kernel(result, sol_out, res_out, dir_out, slope_out, stage):
    stage[0:64, :] = result[...]
    stage[64:128, :] = jnp.zeros((64, 128), f32)
    turned = stage[...].T
    sol_out[...] = turned[0:32, 0:64]
    res_out[...] = turned[32:64, 0:64]
    dir_out[...] = turned[64:96, 0:64]
    slope_out[...] = turned[96:128, 0:64]


def local(features, inv_scale, pivots, solution, residual, direction):
    vmem = pltpu.VMEM
    dma = pltpu.SemaphoreType.DMA
    one = dma(())
    fold16 = vmem((16, 16, 128), f32)
    flat32 = vmem((32, 128), f32)
    flat16 = vmem((16, 128), f32)
    flat1 = vmem((1, 128), f32)
    scratch = [
        vmem((64, 64), bf16), vmem((1, 64), f32), vmem((1, 64), jnp.int32),
        vmem((32, 64), f32), vmem((32, 64), f32), vmem((32, 64), f32),
        vmem((128, 128), f32), vmem((128, 128), f32),
        vmem((16, 48, 128), bf16), vmem((16, 48, 128), bf16), vmem((16, 64, 128), bf16),
        vmem((1024, 128), bf16), vmem((1024, 128), f32),
        fold16, fold16, fold16, fold16,
        vmem((16, 1, 128), f32), vmem((8, 128), f32), vmem((8, 128), f32), vmem((16, 8, 128), f32),
        flat32, flat16, flat16, fold16, flat16, flat16,
        flat32, flat16, flat16, fold16, fold16, flat16, flat16,
        flat1, flat1, flat1, vmem((16, 1, 128), f32), vmem((16, 1, 128), f32),
        dma((6,)), one, dma((4,)), one, one, dma((3,)), dma((3,)), *[one] * 30,
    ]
    result = pl.pallas_call(
        step_kernel,
        name="cg_step",
        out_shape=jax.ShapeDtypeStruct((64, 128), f32),
        in_specs=[pl.BlockSpec(memory_space=pltpu.HBM)] * 6,
        out_specs=pl.BlockSpec(memory_space=vmem),
        scratch_shapes=scratch,
        compiler_params=pltpu.CompilerParams(
            collective_id=0, has_side_effects=True, vmem_limit_bytes=60 * 1024 * 1024
        ),
    )(features, inv_scale[None, :], pivots[None, :], solution, residual, direction)
    return pl.pallas_call(
        turn_kernel,
        name="turn",
        out_shape=(jax.ShapeDtypeStruct((32, 64), f32),) * 4,
        in_specs=[pl.BlockSpec(memory_space=vmem)],
        out_specs=(pl.BlockSpec(memory_space=vmem),) * 4,
        scratch_shapes=[vmem((128, 128), f32)],
    )(result)


def solution(mesh):
    split = P(None, ("row", "col"))
    return jax.shard_map(
        local,
        mesh=mesh,
        in_specs=(split, P(), P(), split, split, split),
        out_specs=(split,) * 4,
        check_vma=False,
    )
```

```python
import jax
import jax.numpy as jnp
from jax import lax
from jax.experimental import pallas as pl
from jax.experimental.pallas import tpu as pltpu
from jax.sharding import PartitionSpec as P

noise_var = 1.0
MESH = pl.DeviceIdType.MESH
highest = lax.Precision.HIGHEST
f32 = jnp.float32
bf16 = jnp.bfloat16
NT = (((1,), (1,)), ((), ()))
NN = (((1,), (0,)), ((), ()))


def iota(shape, dim):
    return lax.broadcasted_iota(jnp.int32, shape, dim)


def loop(low, high, body):
    def step(k, carry):
        body(k)
        return carry

    lax.fori_loop(low, high, step, 0)


def each(low, high, body):
    for k in range(low, high):
        body(jnp.int32(k))


def exact(left, right, numbers=NN):
    return lax.dot_general(left, right, numbers, precision=highest, preferred_element_type=f32)


def kernel_of(left, right):
    return jnp.exp(lax.dot_general(left, right, NT, preferred_element_type=f32))


def forms(scaled, lane):
    norm = jnp.sum(scaled * scaled, axis=1, keepdims=True)
    high = norm.astype(bf16).astype(f32)
    rest = norm - high
    mid = rest.astype(bf16).astype(f32)
    low = (rest - mid).astype(bf16).astype(f32)
    place = lane - 32
    first = jnp.where(place == 0, high, jnp.where(place == 1, mid, jnp.where(place == 2, low, 0.0)))
    place = lane - 35
    second = jnp.where(place == 0, high, jnp.where(place == 1, mid, jnp.where(place == 2, low, 0.0)))
    in_first = (lane >= 32) & (lane < 35)
    in_second = (lane >= 35) & (lane < 38)
    row_form = scaled + second + jnp.where(in_first, -0.5, 0.0)
    col_form = scaled + first + jnp.where(in_second, -0.5, 0.0)
    return row_form, col_form


def unfold_block(blocks):
    count = blocks.shape[0]
    wide = blocks.astype(f32)
    lane = iota((count * 64, 128), 1)
    near = wide[:, 0:32]
    far = pltpu.roll(near.reshape(count * 32, 128), 64, 1).reshape(count, 32, 128)
    scaled = jnp.concatenate([near, far], axis=1).reshape(count * 64, 128)
    column = forms(jnp.where(lane >= 64, scaled, 0.0), lane)[1].astype(bf16)
    packed = wide[:, 32:48].reshape(count * 16, 128)

    def at(first):
        turned = [pltpu.roll(packed, (first - 32 * q) % 128, 1).reshape(count, 16, 128) for q in range(4)]
        return jnp.concatenate(turned, axis=1).reshape(count * 64, 128)

    plain = jnp.where(lane < 32, at(0), 0.0).astype(bf16)
    slope = jnp.where((lane >= 32) & (lane < 64), -2.0 * at(32), 0.0).astype(bf16)
    return column, plain, slope


def unfold(packed):
    return jnp.concatenate([packed, pltpu.roll(packed, 64, 1)], axis=0)


def step_kernel(
    feat_hbm, inv_hbm, piv_hbm, sol_hbm, res_hbm, dir_hbm,
    result,
    feat_in, inv_in, piv_in, sol_in, res_in, dir_in,
    stage_a, stage_b,
    zbuf, zsib, xbuf, colm, acc,
    part, part_xy, slopes, slopes_xy,
    q_z, q_own, q_sib, q_xy,
    g_own, g_sib, g_sum, g_xy, g_half, g_other,
    l_own, l_sib, l_sum, l_xy, l_z, l_half, l_other,
    e_own, e_sib, e_sum, e_xy, e_z,
    in_sem, zs, zr, xs, xr, ws, wr, ps, pr, ds, dr, qs, qr, qcs, qcr, qxs, qxr,
    gs, gr, gxs, gxr, vs, vr, ls, lr, lxs, lxr, lzs, lzr, us, ur, es, er, exs, exr, ezs, ezr,
):
    row = lax.axis_index("row")
    col = lax.axis_index("col")
    xy = lax.rem(row, 16)
    core = lax.rem(col, 2)
    z = (col // 2) * 4 + row // 16

    def dev(z_at, xy_at, core_at):
        return (lax.rem(z_at, 4) * 16 + xy_at, (z_at // 4) * 2 + core_at)

    def z_shift(k):
        far = 8 - (k + 1) // 2
        return jnp.where(lax.rem(k, 2) == 1, far, 16 - far)

    def z_peer(k):
        return lax.rem(z + z_shift(k), 16)

    def z_near(k):
        far = 4 - k // 2
        return dev(lax.rem(z + jnp.where(lax.rem(k, 2) == 0, far, 16 - far), 16), xy, core)

    def xy_peer(k):
        return lax.rem(xy + k, 16)

    sibling = dev(z, xy, 1 - core)
    kept = pl.ds(pl.multiple_of(core * 16, 16), 16)
    given = pl.ds(pl.multiple_of((1 - core) * 16, 16), 16)

    def remote(src, dst, send, recv, where=sibling):
        return pltpu.make_async_remote_copy(
            src_ref=src, dst_ref=dst, send_sem=send, recv_sem=recv, device_id=where, device_id_type=MESH
        )

    def halves(mine, other):
        first = jnp.where(core == 0, mine, other)
        second = jnp.where(core == 0, other, mine)
        return unfold(jnp.concatenate([first, second], axis=0))

    def exchange(count, copy, buf, send, recv):
        whole = remote(buf.at[0:count], buf.at[0:count], send, recv)
        return (lambda: each(0, count, lambda k: copy(k).start())), whole.wait_recv, whole.wait_send

    def along_z(src, buf, send, recv):
        return exchange(15, lambda k: remote(src, buf.at[z], send, recv, dev(z_peer(k), xy, core)), buf, send, recv)

    def over_xy(src_of, buf, send, recv):
        def copy(k):
            p = xy_peer(k + 1)
            return remote(src_of(p), buf.at[xy], send, recv, dev(z, p, core))

        return exchange(15, copy, buf, send, recv)

    barrier = pltpu.get_barrier_semaphore()

    def greet(where):
        pl.semaphore_signal(barrier, inc=1, device_id=where, device_id_type=MESH)

    loop(0, 8, lambda k: greet(z_near(k)))
    loop(1, 16, lambda k: greet(dev(z, xy_peer(k), core)))
    greet(sibling)

    loads = [
        pltpu.make_async_copy(src, dst, in_sem.at[n])
        for n, (src, dst) in enumerate(
            (
                (feat_hbm, feat_in), (inv_hbm, inv_in), (piv_hbm, piv_in),
                (sol_hbm, sol_in), (res_hbm, res_in), (dir_hbm, dir_in),
            )
        )
    ]
    for load in loads:
        load.start()
    stage_a[...] = jnp.zeros((128, 128), f32)
    stage_b[...] = jnp.zeros((128, 128), f32)
    for load in loads:
        load.wait()

    lane = iota((64, 128), 1)
    line = iota((64, 128), 0)
    stage_a[0:32, 0:64] = dir_in[...]
    stage_a[64:128, 0:64] = feat_in[...].astype(f32)
    stage_b[0:32, 0:64] = res_in[...]
    stage_b[32:64, 0:64] = sol_in[...]
    turned = stage_a[...].T[0:64]
    others = stage_b[...].T[0:64]
    dir_t = jnp.where(lane < 32, turned, 0.0)
    res_t = jnp.where(lane < 32, others, 0.0)
    sol_t = jnp.where(lane < 32, pltpu.roll(others, 96, 1), 0.0)
    stage_a[0:1, 0:64] = inv_in[...]
    stage_a[0:1, 64:128] = jnp.zeros((1, 64), f32)
    inv_row = pltpu.roll(stage_a[0:8, :], 64, 1)[0:1]
    scaled = jnp.where(lane >= 64, (turned * inv_row).astype(bf16).astype(f32), 0.0)

    offset = (row * 8 + col) * 64
    hits = piv_in[...] == iota((64, 64), 0) + offset
    picked = jnp.max(jnp.where(hits, 1.0, 0.0), axis=1, keepdims=True)
    q_z[z] = jnp.sum(picked * scaled, axis=0, keepdims=True)
    row_form, col_form = forms(scaled, lane)
    own_row = row_form.astype(bf16)
    own_col = col_form.astype(bf16)
    zbuf[0, 0:32, :] = (scaled[0:32] + pltpu.roll(scaled[32:64], 64, 1)).astype(bf16)
    zbuf[0, 32:48, :] = sum(
        (pltpu.roll(dir_t[16 * q : 16 * q + 16], 32 * q, 1) for q in range(1, 4)), dir_t[0:16]
    ).astype(bf16)
    xbuf[xy] = own_row

    pl.semaphore_wait(barrier, 24)

    def z_copy(k):
        at = min(k, 2)
        return remote(zbuf.at[0], zbuf.at[k + 1], zs, zr.at[at], z_near(jnp.int32(k)))

    def relay_up(k):
        return remote(zbuf.at[1], zbuf.at[k + 9], zs, zr.at[3], dev(lax.rem(z + 4 - k, 16), xy, core))

    def relay_down(k):
        return remote(zbuf.at[2], zbuf.at[k + 13], zs, zr.at[3], dev(lax.rem(z + 13 + k, 16), xy, core))

    def q_copy(k):
        return remote(q_z.at[z], q_z.at[z], qs, qr.at[min(k, 2)], z_near(jnp.int32(k)))

    def q_up(k):
        p = lax.rem(z + 12, 16)
        return remote(q_z.at[p], q_z.at[p], qs, qr.at[3], dev(lax.rem(z + 4 - k, 16), xy, core))

    def q_down(k):
        p = lax.rem(z + 4, 16)
        return remote(q_z.at[p], q_z.at[p], qs, qr.at[3], dev(lax.rem(z + 13 + k, 16), xy, core))

    def q_arrival(count, at):
        remote(q_z.at[0:count], q_z.at[0:count], qs, qr.at[at]).wait_recv()

    def q_left():
        remote(q_z.at[0:15], q_z.at[0:15], qs, qr.at[0]).wait_send()

    def z_arrival(slots, at):
        remote(zbuf.at[slots], zbuf.at[slots], zs, zr.at[at]).wait_recv()

    def z_left():
        remote(zbuf.at[0:15], zbuf.at[0:15], zs, zr.at[0]).wait_send()

    shared = [
        remote(zbuf.at[slots], zsib.at[slots], ws.at[n], wr.at[n])
        for n, slots in enumerate((pl.ds(0, 3), pl.ds(3, 6), pl.ds(9, 7)))
    ]

    x_start, x_arrive, x_left = over_xy(lambda p: xbuf.at[xy], xbuf, xs, xr)
    for k in range(2):
        z_copy(k).start()
        q_copy(k).start()
    for k in range(2, 8):
        q_copy(k).start()
    for k in range(2, 8):
        z_copy(k).start()
    x_start()

    def tile(blocks, keep=None):
        cols, plain, slope = unfold_block(blocks)
        if keep is not None:
            colm[keep * 512 : keep * 512 + 512, :] = cols
        half = lax.dot_general(xbuf[...].reshape(1024, 128), cols, NT, preferred_element_type=f32)
        value = jnp.exp(half)
        images = jnp.dot(value.astype(bf16), plain, preferred_element_type=f32)
        return images + jnp.dot((value * half).astype(bf16), slope, preferred_element_type=f32)

    q_arrival(1, 0)
    for k in range(4):
        q_up(k).start()
    z_arrival(pl.ds(1, 1), 0)
    for k in range(4):
        relay_up(k).start()
    q_arrival(1, 1)
    for k in range(3):
        q_down(k).start()
    z_arrival(pl.ds(2, 1), 1)
    for k in range(3):
        relay_down(k).start()
    shared[0].start()
    z_arrival(pl.ds(3, 6), 2)
    shared[1].start()
    x_arrive()
    acc[...] = tile(zbuf[0:8], 0)

    q_arrival(6, 2)
    q_arrival(7, 3)
    line8 = iota((8, 128), 0)
    found = jnp.zeros((8, 128), f32)
    for low in range(4):
        lot = q_z[low] + q_z[4 + low] + q_z[8 + low] + q_z[12 + low]
        found = found + jnp.where(line8 == lax.rem(xy, 2) * 4 + low, lot, 0.0)
    q_own[...] = found
    qc_copy = remote(q_own, q_sib, qcs, qcr)
    qc_copy.start()

    shared[0].wait_recv()
    shared[1].wait_recv()
    acc[...] += tile(zsib[0:8])
    qc_copy.wait()
    q_xy[xy] = q_own[...] + q_sib[...]
    qx_start, qx_arrive, qx_left = over_xy(lambda p: q_xy.at[xy], q_xy, qxs, qxr)
    qx_start()
    z_arrival(pl.ds(9, 7), 3)
    shared[2].start()
    acc[...] += tile(zbuf[8:16], 1)
    shared[2].wait_recv()
    total = acc[...] + tile(zsib[8:16])
    acc[...] = total

    quarters = total.reshape(16, 4, 16, 128)
    lane_q = iota((256, 128), 1)

    def pack(first):
        packed = jnp.zeros((256, 128), f32)
        for q in range(4):
            turned = pltpu.roll(quarters[:, q].reshape(256, 128), (32 * q - first) % 128, 1)
            packed = jnp.where((lane_q >= 32 * q) & (lane_q < 32 * q + 32), turned, packed)
        return packed.reshape(16, 16, 128)

    def unpack(packed, first):
        return jnp.concatenate([pltpu.roll(packed, (first - 32 * q) % 128, 1) for q in range(4)], axis=0)

    part[...] = pack(0)
    part_xy[xy] = part[xy]
    s_start, s_arrive, s_left = over_xy(lambda p: part.at[p], part_xy, ps, pr)
    s_start()
    slopes[...] = pack(32)
    slopes_xy[xy] = slopes[xy]
    d_start, d_arrive, d_left = over_xy(lambda p: slopes.at[p], slopes_xy, ds, dr)

    qx_arrive()
    lots = [q_xy[2 * pair] + q_xy[2 * pair + 1] for pair in range(8)]
    pivot_row, pivot_col = forms(jnp.concatenate(lots, axis=0), lane)
    pivot_row = pivot_row.astype(bf16)
    pivot_col = pivot_col.astype(bf16)
    own_kernel = kernel_of(pivot_row, own_col)
    plane_kernel = kernel_of(pivot_col, xbuf[...].reshape(1024, 128))
    proj = exact(plane_kernel, acc[...])
    proj = jnp.where(lane < 32, proj, 0.0) + exact(own_kernel, noise_var * dir_t + pltpu.roll(res_t, 32, 1))
    l_own[...] = proj[0:32] + pltpu.roll(proj[32:64], 64, 1)
    l_copy = remote(l_own.at[given], l_sib, ls, lr)
    l_copy.start()

    line_kernel = kernel_of(pivot_row, colm[...])
    gram_part = exact(line_kernel, line_kernel, NT)
    wide = jnp.concatenate([gram_part, jnp.zeros((64, 64), f32)], axis=1)
    g_own[...] = wide[0:32] + pltpu.roll(wide[32:64], 64, 1)
    g_copy = remote(g_own.at[given], g_sib, gs, gr)
    g_copy.start()
    l_copy.wait()
    l_sum[...] = l_own[kept, :] + l_sib[...]
    l_xy[xy] = l_sum[...]
    l_start, l_arrive, l_left = over_xy(lambda p: l_sum, l_xy, lxs, lxr)
    l_start()
    own_kernel_t = kernel_of(own_row, pivot_col)
    pivot_self = kernel_of(pivot_row, pivot_col)
    g_copy.wait()
    g_sum[...] = g_own[kept, :] + g_sib[...]
    g_xy[xy] = g_sum[...]
    g_start, g_arrive, g_left = over_xy(lambda p: g_sum, g_xy, gxs, gxr)
    g_start()

    s_arrive()
    images = unpack(jnp.sum(part_xy[...], axis=0), 0)
    image = jnp.where(lane < 32, images + noise_var * dir_t, 0.0)
    sums = jnp.sum(
        dir_t * image
        + pltpu.roll(res_t * image, 32, 1)
        + pltpu.roll(image * image, 64, 1)
        + pltpu.roll(res_t * res_t, 96, 1),
        axis=0,
        keepdims=True,
    )
    e_own[...] = sums
    e_copy = remote(e_own, e_sib, es, er)
    e_copy.start()
    z_left()
    for copy in shared:
        copy.wait_send()
    x_left()
    q_left()
    qx_left()
    s_left()
    e_copy.wait()
    e_sum[...] = e_own[...] + e_sib[...]
    e_xy[xy] = e_sum[...]
    e_start, e_arrive, e_left = over_xy(lambda p: e_sum, e_xy, exs, exr)
    e_start()

    l_arrive()
    l_z[z] = jnp.sum(l_xy[...], axis=0)
    lz_start, lz_arrive, lz_left = along_z(l_z.at[z], l_z, lzs, lzr)
    lz_start()
    e_arrive()
    e_z[z] = jnp.sum(e_xy[...], axis=0)
    ez_start, ez_arrive, ez_left = along_z(e_z.at[z], e_z, ezs, ezr)
    ez_start()
    d_start()

    g_arrive()
    g_half[...] = jnp.sum(g_xy[...], axis=0)
    v_copy = remote(g_half, g_other, vs, vr)
    v_copy.start()
    g_left()
    l_left()
    v_copy.wait()
    gram = halves(g_half[...], g_other[...])
    own_self = jnp.concatenate([noise_var * pivot_self, jnp.zeros((64, 64), f32)], axis=1)
    work = jnp.where(lane < 64, gram + own_self, jnp.where(lane == line + 64, 1.0, 0.0))

    done = []
    for panel in range(8):
        count = 64 - 8 * panel
        below = iota((count, 128), 0)
        cols = [jnp.broadcast_to(work[:, 8 * panel + j : 8 * panel + j + 1], (count, 128)) for j in range(8)]
        for k in range(8):
            factor = jnp.where(below > k, cols[k] * (1.0 / cols[k][k : k + 1]), 0.0)
            work = work - factor * work[k : k + 1]
            for j in range(k + 1, 8):
                cols[j] = cols[j] - factor * cols[j][k : k + 1]
        done.append(work[0:8])
        work = work[8:]
    work = jnp.concatenate(done, axis=0)
    diagonal = jnp.sum(jnp.where(lane == line, work, 0.0), axis=1, keepdims=True)
    lower_inv = pltpu.roll(work, 64, 1)[:, 0:64] * lax.rsqrt(diagonal)
    gram_inv = exact(lower_inv.T, lower_inv)
    mapped = exact(own_kernel_t, gram_inv)

    e_left()
    d_arrive()
    d_left()
    slope = unpack(jnp.sum(slopes_xy[...], axis=0), 96)

    lz_arrive()
    l_half[...] = jnp.sum(l_z[...], axis=0)
    u_copy = remote(l_half, l_other, us, ur)
    u_copy.start()
    lz_left()
    u_copy.wait()
    projs = halves(l_half[...], l_other[...])
    solved = exact(gram_inv, projs)
    spread = exact(mapped, projs)

    def old(values):
        return pltpu.roll(values, 96, 1)

    proj_old = old(projs)
    solved_old = old(solved)
    spread_old = old(spread)
    removed_old = jnp.sum(proj_old * solved_old, axis=0, keepdims=True)

    ez_left()
    ez_arrive()
    curvature = jnp.sum(e_z[...], axis=0)
    cross = pltpu.roll(jnp.broadcast_to(curvature, (8, 128)), 96, 1)[0:1]
    square = pltpu.roll(jnp.broadcast_to(curvature, (8, 128)), 64, 1)[0:1]
    square_old = pltpu.roll(jnp.broadcast_to(curvature, (8, 128)), 32, 1)[0:1]
    norm_old = (square_old - removed_old) / noise_var
    step = norm_old / curvature
    residual_new = res_t - step * image
    proj_new = proj_old - step * projs
    solved_new = solved_old - step * solved
    square_new = square_old - 2.0 * step * cross + step * step * square
    norm_new = (square_new - jnp.sum(proj_new * solved_new, axis=0, keepdims=True)) / noise_var
    precond_new = (residual_new - (spread_old - step * spread)) / noise_var
    direction_new = precond_new + (norm_new / norm_old) * dir_t
    solution_new = sol_t + step * dir_t
    result[...] = jnp.where(
        lane < 32,
        solution_new,
        jnp.where(
            lane < 64,
            pltpu.roll(residual_new, 32, 1),
            jnp.where(lane < 96, pltpu.roll(direction_new, 64, 1), slope),
        ),
    )


def turn_kernel(result, sol_out, res_out, dir_out, slope_out, stage):
    stage[0:64, :] = result[...]
    stage[64:128, :] = jnp.zeros((64, 128), f32)
    turned = stage[...].T
    sol_out[...] = turned[0:32, 0:64]
    res_out[...] = turned[32:64, 0:64]
    dir_out[...] = turned[64:96, 0:64]
    slope_out[...] = turned[96:128, 0:64]


def local(features, inv_scale, pivots, solution, residual, direction):
    vmem = pltpu.VMEM
    dma = pltpu.SemaphoreType.DMA
    one = dma(())
    fold16 = vmem((16, 16, 128), f32)
    flat32 = vmem((32, 128), f32)
    flat16 = vmem((16, 128), f32)
    flat1 = vmem((1, 128), f32)
    scratch = [
        vmem((64, 64), bf16), vmem((1, 64), f32), vmem((1, 64), jnp.int32),
        vmem((32, 64), f32), vmem((32, 64), f32), vmem((32, 64), f32),
        vmem((128, 128), f32), vmem((128, 128), f32),
        vmem((16, 48, 128), bf16), vmem((16, 48, 128), bf16), vmem((16, 64, 128), bf16),
        vmem((1024, 128), bf16), vmem((1024, 128), f32),
        fold16, fold16, fold16, fold16,
        vmem((16, 1, 128), f32), vmem((8, 128), f32), vmem((8, 128), f32), vmem((16, 8, 128), f32),
        flat32, flat16, flat16, fold16, flat16, flat16,
        flat32, flat16, flat16, fold16, fold16, flat16, flat16,
        flat1, flat1, flat1, vmem((16, 1, 128), f32), vmem((16, 1, 128), f32),
        dma((6,)), one, dma((4,)), one, one, dma((3,)), dma((3,)), *[one] * 4, one, dma((4,)), *[one] * 24,
    ]
    result = pl.pallas_call(
        step_kernel,
        name="cg_step",
        out_shape=jax.ShapeDtypeStruct((64, 128), f32),
        in_specs=[pl.BlockSpec(memory_space=pltpu.HBM)] * 6,
        out_specs=pl.BlockSpec(memory_space=vmem),
        scratch_shapes=scratch,
        compiler_params=pltpu.CompilerParams(
            collective_id=0, has_side_effects=True, vmem_limit_bytes=60 * 1024 * 1024
        ),
    )(features, inv_scale[None, :], pivots[None, :], solution, residual, direction)
    return pl.pallas_call(
        turn_kernel,
        name="turn",
        out_shape=(jax.ShapeDtypeStruct((32, 64), f32),) * 4,
        in_specs=[pl.BlockSpec(memory_space=vmem)],
        out_specs=(pl.BlockSpec(memory_space=vmem),) * 4,
        scratch_shapes=[vmem((128, 128), f32)],
    )(result)


def solution(mesh):
    split = P(None, ("row", "col"))
    return jax.shard_map(
        local,
        mesh=mesh,
        in_specs=(split, P(), P(), split, split, split),
        out_specs=(split,) * 4,
        check_vma=False,
    )
```

```python
import jax
import jax.numpy as jnp
from jax import lax
from jax.experimental import pallas as pl
from jax.experimental.pallas import tpu as pltpu
from jax.sharding import PartitionSpec as P

noise_var = 1.0
MESH = pl.DeviceIdType.MESH
highest = lax.Precision.HIGHEST
f32 = jnp.float32
bf16 = jnp.bfloat16
NT = (((1,), (1,)), ((), ()))
NN = (((1,), (0,)), ((), ()))


def iota(shape, dim):
    return lax.broadcasted_iota(jnp.int32, shape, dim)


def loop(low, high, body):
    def step(k, carry):
        body(k)
        return carry

    lax.fori_loop(low, high, step, 0)


def each(low, high, body):
    for k in range(low, high):
        body(jnp.int32(k))


def exact(left, right, numbers=NN):
    return lax.dot_general(left, right, numbers, precision=highest, preferred_element_type=f32)


def kernel_of(left, right):
    return jnp.exp(lax.dot_general(left, right, NT, preferred_element_type=f32))


def forms(scaled, lane):
    norm = jnp.sum(scaled * scaled, axis=1, keepdims=True)
    high = norm.astype(bf16).astype(f32)
    rest = norm - high
    mid = rest.astype(bf16).astype(f32)
    low = (rest - mid).astype(bf16).astype(f32)
    place = lane - 32
    first = jnp.where(place == 0, high, jnp.where(place == 1, mid, jnp.where(place == 2, low, 0.0)))
    place = lane - 35
    second = jnp.where(place == 0, high, jnp.where(place == 1, mid, jnp.where(place == 2, low, 0.0)))
    in_first = (lane >= 32) & (lane < 35)
    in_second = (lane >= 35) & (lane < 38)
    row_form = scaled + second + jnp.where(in_first, -0.5, 0.0)
    col_form = scaled + first + jnp.where(in_second, -0.5, 0.0)
    return row_form, col_form


def unfold_block(blocks):
    count = blocks.shape[0]
    wide = blocks.astype(f32)
    lane = iota((count * 64, 128), 1)
    near = wide[:, 0:32]
    far = pltpu.roll(near.reshape(count * 32, 128), 64, 1).reshape(count, 32, 128)
    scaled = jnp.concatenate([near, far], axis=1).reshape(count * 64, 128)
    column = forms(jnp.where(lane >= 64, scaled, 0.0), lane)[1].astype(bf16)
    packed = wide[:, 32:48].reshape(count * 16, 128)

    def at(first):
        turned = [pltpu.roll(packed, (first - 32 * q) % 128, 1).reshape(count, 16, 128) for q in range(4)]
        return jnp.concatenate(turned, axis=1).reshape(count * 64, 128)

    plain = jnp.where(lane < 32, at(0), 0.0).astype(bf16)
    slope = jnp.where((lane >= 32) & (lane < 64), -2.0 * at(32), 0.0).astype(bf16)
    return column, plain, slope


def unfold(packed):
    return jnp.concatenate([packed, pltpu.roll(packed, 64, 1)], axis=0)


def step_kernel(
    feat_hbm, inv_hbm, piv_hbm, sol_hbm, res_hbm, dir_hbm,
    result,
    feat_in, inv_in, piv_in, sol_in, res_in, dir_in,
    stage_a, stage_b,
    zall, xbuf, colm, acc,
    part, part_xy, slopes, slopes_xy,
    q_z, q_own, q_sib, q_xy,
    g_own, g_sib, g_sum, g_xy, g_half, g_other,
    l_own, l_sib, l_sum, l_xy, l_z, l_half, l_other,
    e_own, e_sib, e_sum, e_xy, e_z,
    in_sem, zs, zr, xs, xr, ws, wr, ps, pr, ds, dr, qs, qr, qcs, qcr, qxs, qxr,
    gs, gr, gxs, gxr, vs, vr, ls, lr, lxs, lxr, lzs, lzr, us, ur, es, er, exs, exr, ezs, ezr,
):
    zbuf = zall.at[0]
    zsib = zall.at[1]
    row = lax.axis_index("row")
    col = lax.axis_index("col")
    xy = lax.rem(row, 16)
    core = lax.rem(col, 2)
    z = (col // 2) * 4 + row // 16

    def dev(z_at, xy_at, core_at):
        return (lax.rem(z_at, 4) * 16 + xy_at, (z_at // 4) * 2 + core_at)

    def z_shift(k):
        far = 8 - (k + 1) // 2
        return jnp.where(lax.rem(k, 2) == 1, far, 16 - far)

    def z_peer(k):
        return lax.rem(z + z_shift(k), 16)

    def xy_peer(k):
        return lax.rem(xy + k, 16)

    sibling = dev(z, xy, 1 - core)
    kept = pl.ds(pl.multiple_of(core * 16, 16), 16)
    given = pl.ds(pl.multiple_of((1 - core) * 16, 16), 16)

    def remote(src, dst, send, recv, where=sibling):
        return pltpu.make_async_remote_copy(
            src_ref=src, dst_ref=dst, send_sem=send, recv_sem=recv, device_id=where, device_id_type=MESH
        )

    def halves(mine, other):
        first = jnp.where(core == 0, mine, other)
        second = jnp.where(core == 0, other, mine)
        return unfold(jnp.concatenate([first, second], axis=0))

    def exchange(count, copy, buf, send, recv):
        whole = remote(buf.at[0:count], buf.at[0:count], send, recv)
        return (lambda: each(0, count, lambda k: copy(k).start())), whole.wait_recv, whole.wait_send

    def along_z(src, buf, send, recv):
        return exchange(15, lambda k: remote(src, buf.at[z], send, recv, dev(z_peer(k), xy, core)), buf, send, recv)

    def over_xy(src_of, buf, send, recv):
        def copy(k):
            p = xy_peer(k + 1)
            return remote(src_of(p), buf.at[xy], send, recv, dev(z, p, core))

        return exchange(15, copy, buf, send, recv)

    barrier = pltpu.get_barrier_semaphore()

    def greet(where):
        pl.semaphore_signal(barrier, inc=1, device_id=where, device_id_type=MESH)

    loop(0, 15, lambda k: greet(dev(z_peer(k), xy, core)))
    loop(1, 16, lambda k: greet(dev(z, xy_peer(k), core)))
    greet(sibling)

    loads = [
        pltpu.make_async_copy(src, dst, in_sem.at[n])
        for n, (src, dst) in enumerate(
            (
                (feat_hbm, feat_in), (inv_hbm, inv_in), (piv_hbm, piv_in),
                (sol_hbm, sol_in), (res_hbm, res_in), (dir_hbm, dir_in),
            )
        )
    ]
    for load in loads:
        load.start()
    stage_a[...] = jnp.zeros((128, 128), f32)
    stage_b[...] = jnp.zeros((128, 128), f32)
    for load in loads:
        load.wait()

    lane = iota((64, 128), 1)
    line = iota((64, 128), 0)
    stage_a[0:32, 0:64] = dir_in[...]
    stage_a[64:128, 0:64] = feat_in[...].astype(f32)
    stage_b[0:32, 0:64] = res_in[...]
    stage_b[32:64, 0:64] = sol_in[...]
    turned = stage_a[...].T[0:64]
    others = stage_b[...].T[0:64]
    dir_t = jnp.where(lane < 32, turned, 0.0)
    res_t = jnp.where(lane < 32, others, 0.0)
    sol_t = jnp.where(lane < 32, pltpu.roll(others, 96, 1), 0.0)
    stage_a[0:1, 0:64] = inv_in[...]
    stage_a[0:1, 64:128] = jnp.zeros((1, 64), f32)
    inv_row = pltpu.roll(stage_a[0:8, :], 64, 1)[0:1]
    scaled = jnp.where(lane >= 64, (turned * inv_row).astype(bf16).astype(f32), 0.0)

    offset = (row * 8 + col) * 64
    hits = piv_in[...] == iota((64, 64), 0) + offset
    picked = jnp.max(jnp.where(hits, 1.0, 0.0), axis=1, keepdims=True)
    q_z[z] = jnp.sum(picked * scaled, axis=0, keepdims=True)
    row_form, col_form = forms(scaled, lane)
    own_row = row_form.astype(bf16)
    own_col = col_form.astype(bf16)
    zbuf[0, 0:32, :] = (scaled[0:32] + pltpu.roll(scaled[32:64], 64, 1)).astype(bf16)
    zbuf[0, 32:48, :] = sum(
        (pltpu.roll(dir_t[16 * q : 16 * q + 16], 32 * q, 1) for q in range(1, 4)), dir_t[0:16]
    ).astype(bf16)
    xbuf[xy] = own_row

    pl.semaphore_wait(barrier, 31)

    q_start, q_arrive, q_left = along_z(q_z.at[z], q_z, qs, qr)

    def z_near(k):
        far = 4 - k // 2
        return dev(lax.rem(z + jnp.where(lax.rem(k, 2) == 0, far, 16 - far), 16), xy, core)

    def z_copy(k):
        at = min(k, 2)
        return remote(zbuf.at[0], zbuf.at[k + 1], zs, zr.at[at], z_near(jnp.int32(k)))

    def relay_up(k):
        return remote(zbuf.at[1], zbuf.at[k + 9], zs, zr.at[3], dev(lax.rem(z + 4 - k, 16), xy, core))

    def relay_down(k):
        return remote(zbuf.at[2], zbuf.at[k + 13], zs, zr.at[3], dev(lax.rem(z + 13 + k, 16), xy, core))

    def z_arrival(slots, at):
        remote(zbuf.at[slots], zbuf.at[slots], zs, zr.at[at]).wait_recv()

    def z_left():
        remote(zbuf.at[0:15], zbuf.at[0:15], zs, zr.at[0]).wait_send()

    shared = [
        remote(zbuf.at[slots], zsib.at[slots], ws.at[n], wr.at[n])
        for n, slots in enumerate((pl.ds(0, 3), pl.ds(3, 6), pl.ds(9, 7)))
    ]

    x_start, x_arrive, x_left = over_xy(lambda p: xbuf.at[xy], xbuf, xs, xr)
    for k in range(2):
        z_copy(k).start()
    q_start()
    for k in range(2, 8):
        z_copy(k).start()
    x_start()

    z_arrival(pl.ds(1, 1), 0)
    for k in range(4):
        relay_up(k).start()
    z_arrival(pl.ds(2, 1), 1)
    for k in range(3):
        relay_down(k).start()
    shared[0].start()
    z_arrival(pl.ds(3, 6), 2)
    shared[1].start()
    x_arrive()
    acc[...] = jnp.zeros((1024, 128), f32)
    qc_copy = remote(q_own, q_sib, qcs, qcr)
    qx_start, qx_arrive, qx_left = over_xy(lambda p: q_xy.at[xy], q_xy, qxs, qxr)

    def tile(step):
        @pl.when(step == 1)
        def _():
            q_arrive()
            line8 = iota((8, 128), 0)
            found = jnp.zeros((8, 128), f32)
            for low in range(4):
                lot = q_z[low] + q_z[4 + low] + q_z[8 + low] + q_z[12 + low]
                found = found + jnp.where(line8 == lax.rem(xy, 2) * 4 + low, lot, 0.0)
            q_own[...] = found
            qc_copy.start()
            shared[0].wait_recv()
            shared[1].wait_recv()

        @pl.when(step == 2)
        def _():
            qc_copy.wait()
            q_xy[xy] = q_own[...] + q_sib[...]
            qx_start()
            z_arrival(pl.ds(9, 7), 3)
            shared[2].start()

        @pl.when(step == 3)
        def _():
            shared[2].wait_recv()

        side = lax.rem(step, 2)
        group = step // 2
        cols, plain, slope = unfold_block(zall[side, pl.ds(pl.multiple_of(group * 8, 8), 8)])
        colm[side, pl.ds(pl.multiple_of(group * 512, 512), 512), :] = cols
        half = lax.dot_general(xbuf[...].reshape(1024, 128), cols, NT, preferred_element_type=f32)
        value = jnp.exp(half)
        images = jnp.dot(value.astype(bf16), plain, preferred_element_type=f32)
        acc[...] += images + jnp.dot((value * half).astype(bf16), slope, preferred_element_type=f32)

    loop(0, 4, tile)
    total = acc[...]

    quarters = total.reshape(16, 4, 16, 128)
    lane_q = iota((256, 128), 1)

    def pack(first):
        packed = jnp.zeros((256, 128), f32)
        for q in range(4):
            turned = pltpu.roll(quarters[:, q].reshape(256, 128), (32 * q - first) % 128, 1)
            packed = jnp.where((lane_q >= 32 * q) & (lane_q < 32 * q + 32), turned, packed)
        return packed.reshape(16, 16, 128)

    def unpack(packed, first):
        return jnp.concatenate([pltpu.roll(packed, (first - 32 * q) % 128, 1) for q in range(4)], axis=0)

    part[...] = pack(0)
    part_xy[xy] = part[xy]
    s_start, s_arrive, s_left = over_xy(lambda p: part.at[p], part_xy, ps, pr)
    s_start()
    slopes[...] = pack(32)
    slopes_xy[xy] = slopes[xy]
    d_start, d_arrive, d_left = over_xy(lambda p: slopes.at[p], slopes_xy, ds, dr)

    qx_arrive()
    lots = [q_xy[2 * pair] + q_xy[2 * pair + 1] for pair in range(8)]
    pivot_row, pivot_col = forms(jnp.concatenate(lots, axis=0), lane)
    pivot_row = pivot_row.astype(bf16)
    pivot_col = pivot_col.astype(bf16)
    own_kernel = kernel_of(pivot_row, own_col)
    plane_kernel = kernel_of(pivot_col, xbuf[...].reshape(1024, 128))
    proj = exact(plane_kernel, acc[...])
    proj = jnp.where(lane < 32, proj, 0.0) + exact(own_kernel, noise_var * dir_t + pltpu.roll(res_t, 32, 1))
    l_own[...] = proj[0:32] + pltpu.roll(proj[32:64], 64, 1)
    l_copy = remote(l_own.at[given], l_sib, ls, lr)
    l_copy.start()

    line_kernel = kernel_of(pivot_row, colm[0])
    gram_part = exact(line_kernel, line_kernel, NT)
    wide = jnp.concatenate([gram_part, jnp.zeros((64, 64), f32)], axis=1)
    g_own[...] = wide[0:32] + pltpu.roll(wide[32:64], 64, 1)
    g_copy = remote(g_own.at[given], g_sib, gs, gr)
    g_copy.start()
    l_copy.wait()
    l_sum[...] = l_own[kept, :] + l_sib[...]
    l_xy[xy] = l_sum[...]
    l_start, l_arrive, l_left = over_xy(lambda p: l_sum, l_xy, lxs, lxr)
    l_start()
    own_kernel_t = kernel_of(own_row, pivot_col)
    pivot_self = kernel_of(pivot_row, pivot_col)
    g_copy.wait()
    g_sum[...] = g_own[kept, :] + g_sib[...]
    g_xy[xy] = g_sum[...]
    g_start, g_arrive, g_left = over_xy(lambda p: g_sum, g_xy, gxs, gxr)
    g_start()

    s_arrive()
    images = unpack(jnp.sum(part_xy[...], axis=0), 0)
    image = jnp.where(lane < 32, images + noise_var * dir_t, 0.0)
    sums = jnp.sum(
        dir_t * image
        + pltpu.roll(res_t * image, 32, 1)
        + pltpu.roll(image * image, 64, 1)
        + pltpu.roll(res_t * res_t, 96, 1),
        axis=0,
        keepdims=True,
    )
    e_own[...] = sums
    e_copy = remote(e_own, e_sib, es, er)
    e_copy.start()
    z_left()
    for copy in shared:
        copy.wait_send()
    x_left()
    q_left()
    qx_left()
    s_left()
    e_copy.wait()
    e_sum[...] = e_own[...] + e_sib[...]
    e_xy[xy] = e_sum[...]
    e_start, e_arrive, e_left = over_xy(lambda p: e_sum, e_xy, exs, exr)
    e_start()

    l_arrive()
    l_z[z] = jnp.sum(l_xy[...], axis=0)
    lz_start, lz_arrive, lz_left = along_z(l_z.at[z], l_z, lzs, lzr)
    lz_start()
    e_arrive()
    e_z[z] = jnp.sum(e_xy[...], axis=0)
    ez_start, ez_arrive, ez_left = along_z(e_z.at[z], e_z, ezs, ezr)
    ez_start()
    d_start()

    g_arrive()
    g_half[...] = jnp.sum(g_xy[...], axis=0)
    v_copy = remote(g_half, g_other, vs, vr)
    v_copy.start()
    g_left()
    l_left()
    v_copy.wait()
    gram = halves(g_half[...], g_other[...])
    own_self = jnp.concatenate([noise_var * pivot_self, jnp.zeros((64, 64), f32)], axis=1)
    work = jnp.where(lane < 64, gram + own_self, jnp.where(lane == line + 64, 1.0, 0.0))

    done = []
    for panel in range(8):
        count = 64 - 8 * panel
        below = iota((count, 128), 0)
        cols = [jnp.broadcast_to(work[:, 8 * panel + j : 8 * panel + j + 1], (count, 128)) for j in range(8)]
        for k in range(8):
            factor = jnp.where(below > k, cols[k] * (1.0 / cols[k][k : k + 1]), 0.0)
            work = work - factor * work[k : k + 1]
            for j in range(k + 1, 8):
                cols[j] = cols[j] - factor * cols[j][k : k + 1]
        done.append(work[0:8])
        work = work[8:]
    work = jnp.concatenate(done, axis=0)
    diagonal = jnp.sum(jnp.where(lane == line, work, 0.0), axis=1, keepdims=True)
    lower_inv = pltpu.roll(work, 64, 1)[:, 0:64] * lax.rsqrt(diagonal)
    gram_inv = exact(lower_inv.T, lower_inv)
    mapped = exact(own_kernel_t, gram_inv)

    e_left()
    d_arrive()
    d_left()
    slope = unpack(jnp.sum(slopes_xy[...], axis=0), 96)

    lz_arrive()
    l_half[...] = jnp.sum(l_z[...], axis=0)
    u_copy = remote(l_half, l_other, us, ur)
    u_copy.start()
    lz_left()
    u_copy.wait()
    projs = halves(l_half[...], l_other[...])
    solved = exact(gram_inv, projs)
    spread = exact(mapped, projs)

    def old(values):
        return pltpu.roll(values, 96, 1)

    proj_old = old(projs)
    solved_old = old(solved)
    spread_old = old(spread)
    removed_old = jnp.sum(proj_old * solved_old, axis=0, keepdims=True)

    ez_left()
    ez_arrive()
    curvature = jnp.sum(e_z[...], axis=0)
    cross = pltpu.roll(jnp.broadcast_to(curvature, (8, 128)), 96, 1)[0:1]
    square = pltpu.roll(jnp.broadcast_to(curvature, (8, 128)), 64, 1)[0:1]
    square_old = pltpu.roll(jnp.broadcast_to(curvature, (8, 128)), 32, 1)[0:1]
    norm_old = (square_old - removed_old) / noise_var
    step = norm_old / curvature
    residual_new = res_t - step * image
    proj_new = proj_old - step * projs
    solved_new = solved_old - step * solved
    square_new = square_old - 2.0 * step * cross + step * step * square
    norm_new = (square_new - jnp.sum(proj_new * solved_new, axis=0, keepdims=True)) / noise_var
    precond_new = (residual_new - (spread_old - step * spread)) / noise_var
    direction_new = precond_new + (norm_new / norm_old) * dir_t
    solution_new = sol_t + step * dir_t
    result[...] = jnp.where(
        lane < 32,
        solution_new,
        jnp.where(
            lane < 64,
            pltpu.roll(residual_new, 32, 1),
            jnp.where(lane < 96, pltpu.roll(direction_new, 64, 1), slope),
        ),
    )


def turn_kernel(result, sol_out, res_out, dir_out, slope_out, stage):
    stage[0:64, :] = result[...]
    stage[64:128, :] = jnp.zeros((64, 128), f32)
    turned = stage[...].T
    sol_out[...] = turned[0:32, 0:64]
    res_out[...] = turned[32:64, 0:64]
    dir_out[...] = turned[64:96, 0:64]
    slope_out[...] = turned[96:128, 0:64]


def local(features, inv_scale, pivots, solution, residual, direction):
    vmem = pltpu.VMEM
    dma = pltpu.SemaphoreType.DMA
    one = dma(())
    fold16 = vmem((16, 16, 128), f32)
    flat32 = vmem((32, 128), f32)
    flat16 = vmem((16, 128), f32)
    flat1 = vmem((1, 128), f32)
    scratch = [
        vmem((64, 64), bf16), vmem((1, 64), f32), vmem((1, 64), jnp.int32),
        vmem((32, 64), f32), vmem((32, 64), f32), vmem((32, 64), f32),
        vmem((128, 128), f32), vmem((128, 128), f32),
        vmem((2, 16, 48, 128), bf16), vmem((16, 64, 128), bf16),
        vmem((2, 1024, 128), bf16), vmem((1024, 128), f32),
        fold16, fold16, fold16, fold16,
        vmem((16, 1, 128), f32), vmem((8, 128), f32), vmem((8, 128), f32), vmem((16, 8, 128), f32),
        flat32, flat16, flat16, fold16, flat16, flat16,
        flat32, flat16, flat16, fold16, fold16, flat16, flat16,
        flat1, flat1, flat1, vmem((16, 1, 128), f32), vmem((16, 1, 128), f32),
        dma((6,)), one, dma((4,)), one, one, dma((3,)), dma((3,)), *[one] * 30,
    ]
    result = pl.pallas_call(
        step_kernel,
        name="cg_step",
        out_shape=jax.ShapeDtypeStruct((64, 128), f32),
        in_specs=[pl.BlockSpec(memory_space=pltpu.HBM)] * 6,
        out_specs=pl.BlockSpec(memory_space=vmem),
        scratch_shapes=scratch,
        compiler_params=pltpu.CompilerParams(
            collective_id=0, has_side_effects=True, vmem_limit_bytes=60 * 1024 * 1024
        ),
    )(features, inv_scale[None, :], pivots[None, :], solution, residual, direction)
    return pl.pallas_call(
        turn_kernel,
        name="turn",
        out_shape=(jax.ShapeDtypeStruct((32, 64), f32),) * 4,
        in_specs=[pl.BlockSpec(memory_space=vmem)],
        out_specs=(pl.BlockSpec(memory_space=vmem),) * 4,
        scratch_shapes=[vmem((128, 128), f32)],
    )(result)


def solution(mesh):
    split = P(None, ("row", "col"))
    return jax.shard_map(
        local,
        mesh=mesh,
        in_specs=(split, P(), P(), split, split, split),
        out_specs=(split,) * 4,
        check_vma=False,
    )
```

```python
import jax
import jax.numpy as jnp
from jax import lax
from jax.experimental import pallas as pl
from jax.experimental.pallas import tpu as pltpu
from jax.sharding import PartitionSpec as P

noise_var = 1.0
MESH = pl.DeviceIdType.MESH
highest = lax.Precision.HIGHEST
f32 = jnp.float32
bf16 = jnp.bfloat16
NT = (((1,), (1,)), ((), ()))
NN = (((1,), (0,)), ((), ()))


def iota(shape, dim):
    return lax.broadcasted_iota(jnp.int32, shape, dim)


def loop(low, high, body):
    def step(k, carry):
        body(k)
        return carry

    lax.fori_loop(low, high, step, 0)


def each(low, high, body):
    for k in range(low, high):
        body(jnp.int32(k))


def exact(left, right, numbers=NN):
    return lax.dot_general(left, right, numbers, precision=highest, preferred_element_type=f32)


def kernel_of(left, right):
    return jnp.exp(lax.dot_general(left, right, NT, preferred_element_type=f32))


def forms(scaled, lane):
    norm = jnp.sum(scaled * scaled, axis=1, keepdims=True)
    high = norm.astype(bf16).astype(f32)
    rest = norm - high
    mid = rest.astype(bf16).astype(f32)
    low = (rest - mid).astype(bf16).astype(f32)
    place = lane - 32
    first = jnp.where(place == 0, high, jnp.where(place == 1, mid, jnp.where(place == 2, low, 0.0)))
    place = lane - 35
    second = jnp.where(place == 0, high, jnp.where(place == 1, mid, jnp.where(place == 2, low, 0.0)))
    in_first = (lane >= 32) & (lane < 35)
    in_second = (lane >= 35) & (lane < 38)
    row_form = scaled + second + jnp.where(in_first, -0.5, 0.0)
    col_form = scaled + first + jnp.where(in_second, -0.5, 0.0)
    return row_form, col_form


def unfold_block(blocks):
    count = blocks.shape[0]
    wide = blocks.astype(f32)
    lane = iota((count * 64, 128), 1)
    near = wide[:, 0:32]
    far = pltpu.roll(near.reshape(count * 32, 128), 64, 1).reshape(count, 32, 128)
    scaled = jnp.concatenate([near, far], axis=1).reshape(count * 64, 128)
    column = forms(jnp.where(lane >= 64, scaled, 0.0), lane)[1].astype(bf16)
    packed = wide[:, 32:48].reshape(count * 16, 128)

    def at(first):
        turned = [pltpu.roll(packed, (first - 32 * q) % 128, 1).reshape(count, 16, 128) for q in range(4)]
        return jnp.concatenate(turned, axis=1).reshape(count * 64, 128)

    plain = jnp.where(lane < 32, at(0), 0.0).astype(bf16)
    slope = jnp.where((lane >= 32) & (lane < 64), -2.0 * at(32), 0.0).astype(bf16)
    return column, plain, slope


def unfold(packed):
    return jnp.concatenate([packed, pltpu.roll(packed, 64, 1)], axis=0)


def step_kernel(
    feat_hbm, inv_hbm, piv_hbm, sol_hbm, res_hbm, dir_hbm,
    result,
    feat_in, inv_in, piv_in, sol_in, res_in, dir_in,
    stage_a, stage_b,
    zall, xbuf, colm, acc,
    part, part_xy, slopes, slopes_xy,
    q_z, q_own, q_sib, q_xy,
    g_own, g_sib, g_sum, g_xy, g_half, g_other,
    l_own, l_sib, l_sum, l_xy, l_z, l_half, l_other,
    e_own, e_sib, e_sum, e_xy, e_z,
    in_sem, zs, zr, xs, xr, ws, wr, ps, pr, ds, dr, qs, qr, qcs, qcr, qxs, qxr,
    gs, gr, gxs, gxr, vs, vr, ls, lr, lxs, lxr, lzs, lzr, us, ur, es, er, exs, exr, ezs, ezr,
):
    zbuf = zall.at[0]
    zsib = zall.at[1]
    row = lax.axis_index("row")
    col = lax.axis_index("col")
    xy = lax.rem(row, 16)
    core = lax.rem(col, 2)
    z = (col // 2) * 4 + row // 16

    def dev(z_at, xy_at, core_at):
        return (lax.rem(z_at, 4) * 16 + xy_at, (z_at // 4) * 2 + core_at)

    def z_shift(k):
        far = 8 - (k + 1) // 2
        return jnp.where(lax.rem(k, 2) == 1, far, 16 - far)

    def z_peer(k):
        return lax.rem(z + z_shift(k), 16)

    def xy_peer(k):
        return lax.rem(xy + k, 16)

    sibling = dev(z, xy, 1 - core)
    kept = pl.ds(pl.multiple_of(core * 16, 16), 16)
    given = pl.ds(pl.multiple_of((1 - core) * 16, 16), 16)

    def remote(src, dst, send, recv, where=sibling):
        return pltpu.make_async_remote_copy(
            src_ref=src, dst_ref=dst, send_sem=send, recv_sem=recv, device_id=where, device_id_type=MESH
        )

    def halves(mine, other):
        first = jnp.where(core == 0, mine, other)
        second = jnp.where(core == 0, other, mine)
        return unfold(jnp.concatenate([first, second], axis=0))

    def exchange(count, copy, buf, send, recv):
        whole = remote(buf.at[0:count], buf.at[0:count], send, recv)
        return (lambda: each(0, count, lambda k: copy(k).start())), whole.wait_recv, whole.wait_send

    def along_z(src, buf, send, recv):
        return exchange(15, lambda k: remote(src, buf.at[z], send, recv, dev(z_peer(k), xy, core)), buf, send, recv)

    def over_xy(src_of, buf, send, recv):
        def copy(k):
            p = xy_peer(k + 1)
            return remote(src_of(p), buf.at[xy], send, recv, dev(z, p, core))

        return exchange(15, copy, buf, send, recv)

    barrier = pltpu.get_barrier_semaphore()

    def greet(where):
        pl.semaphore_signal(barrier, inc=1, device_id=where, device_id_type=MESH)

    loop(0, 15, lambda k: greet(dev(z_peer(k), xy, core)))
    loop(1, 16, lambda k: greet(dev(z, xy_peer(k), core)))
    greet(sibling)

    loads = [
        pltpu.make_async_copy(src, dst, in_sem.at[n])
        for n, (src, dst) in enumerate(
            (
                (feat_hbm, feat_in), (inv_hbm, inv_in), (piv_hbm, piv_in),
                (sol_hbm, sol_in), (res_hbm, res_in), (dir_hbm, dir_in),
            )
        )
    ]
    for load in loads:
        load.start()
    stage_a[...] = jnp.zeros((128, 128), f32)
    stage_b[...] = jnp.zeros((128, 128), f32)
    for load in loads:
        load.wait()

    lane = iota((64, 128), 1)
    line = iota((64, 128), 0)
    stage_a[0:32, 0:64] = dir_in[...]
    stage_a[64:128, 0:64] = feat_in[...].astype(f32)
    stage_b[0:32, 0:64] = res_in[...]
    stage_b[32:64, 0:64] = sol_in[...]
    turned = stage_a[...].T[0:64]
    others = stage_b[...].T[0:64]
    dir_t = jnp.where(lane < 32, turned, 0.0)
    res_t = jnp.where(lane < 32, others, 0.0)
    sol_t = jnp.where(lane < 32, pltpu.roll(others, 96, 1), 0.0)
    stage_a[0:1, 0:64] = inv_in[...]
    stage_a[0:1, 64:128] = jnp.zeros((1, 64), f32)
    inv_row = pltpu.roll(stage_a[0:8, :], 64, 1)[0:1]
    scaled = jnp.where(lane >= 64, (turned * inv_row).astype(bf16).astype(f32), 0.0)

    offset = (row * 8 + col) * 64
    hits = piv_in[...] == iota((64, 64), 0) + offset
    picked = jnp.max(jnp.where(hits, 1.0, 0.0), axis=1, keepdims=True)
    q_z[z] = jnp.sum(picked * scaled, axis=0, keepdims=True)
    row_form, col_form = forms(scaled, lane)
    own_row = row_form.astype(bf16)
    own_col = col_form.astype(bf16)
    zbuf[0, 0:32, :] = (scaled[0:32] + pltpu.roll(scaled[32:64], 64, 1)).astype(bf16)
    zbuf[0, 32:48, :] = sum(
        (pltpu.roll(dir_t[16 * q : 16 * q + 16], 32 * q, 1) for q in range(1, 4)), dir_t[0:16]
    ).astype(bf16)
    xbuf[xy] = own_row

    pl.semaphore_wait(barrier, 31)

    q_start, q_arrive, q_left = along_z(q_z.at[z], q_z, qs, qr)

    def z_near(k):
        far = 4 - k // 2
        return dev(lax.rem(z + jnp.where(lax.rem(k, 2) == 0, far, 16 - far), 16), xy, core)

    def z_copy(k):
        at = min(k, 2)
        return remote(zbuf.at[0], zbuf.at[k + 1], zs, zr.at[at], z_near(jnp.int32(k)))

    def relay_up(k):
        return remote(zbuf.at[1], zbuf.at[k + 9], zs, zr.at[3], dev(lax.rem(z + 4 - k, 16), xy, core))

    def relay_down(k):
        return remote(zbuf.at[2], zbuf.at[k + 13], zs, zr.at[3], dev(lax.rem(z + 13 + k, 16), xy, core))

    def z_arrival(slots, at):
        remote(zbuf.at[slots], zbuf.at[slots], zs, zr.at[at]).wait_recv()

    def z_left():
        remote(zbuf.at[0:15], zbuf.at[0:15], zs, zr.at[0]).wait_send()

    shared = [
        remote(zbuf.at[slots], zsib.at[slots], ws.at[n], wr.at[n])
        for n, slots in enumerate((pl.ds(0, 3), pl.ds(3, 6), pl.ds(9, 7)))
    ]

    x_start, x_arrive, x_left = over_xy(lambda p: xbuf.at[xy], xbuf, xs, xr)
    for k in range(2):
        z_copy(k).start()
    q_start()
    for k in range(2, 8):
        z_copy(k).start()
    x_start()

    z_arrival(pl.ds(1, 1), 0)
    for k in range(4):
        relay_up(k).start()
    z_arrival(pl.ds(2, 1), 1)
    for k in range(3):
        relay_down(k).start()
    shared[0].start()
    z_arrival(pl.ds(3, 6), 2)
    shared[1].start()
    x_arrive()
    acc[...] = jnp.zeros((1024, 128), f32)
    qc_copy = remote(q_own, q_sib, qcs, qcr)
    qx_start, qx_arrive, qx_left = over_xy(lambda p: q_xy.at[xy], q_xy, qxs, qxr)

    def tile(step):
        @pl.when(step == 1)
        def _():
            q_arrive()
            line8 = iota((8, 128), 0)
            found = jnp.zeros((8, 128), f32)
            for low in range(4):
                lot = q_z[low] + q_z[4 + low] + q_z[8 + low] + q_z[12 + low]
                found = found + jnp.where(line8 == lax.rem(xy, 2) * 4 + low, lot, 0.0)
            q_own[...] = found
            qc_copy.start()
            shared[0].wait_recv()
            shared[1].wait_recv()

        @pl.when(step == 2)
        def _():
            qc_copy.wait()
            q_xy[xy] = q_own[...] + q_sib[...]
            qx_start()
            z_arrival(pl.ds(9, 7), 3)
            shared[2].start()

        @pl.when(step == 3)
        def _():
            shared[2].wait_recv()

        side = lax.rem(step, 2)
        group = step // 2
        cols, plain, slope = unfold_block(zall[side, pl.ds(pl.multiple_of(group * 8, 8), 8)])
        colm[side, pl.ds(pl.multiple_of(group * 512, 512), 512), :] = cols
        half = lax.dot_general(xbuf[...].reshape(1024, 128), cols, NT, preferred_element_type=f32)
        value = jnp.exp(half)
        images = jnp.dot(value.astype(bf16), plain, preferred_element_type=f32)
        acc[...] += images + jnp.dot((value * half).astype(bf16), slope, preferred_element_type=f32)

    loop(0, 4, tile)
    total = acc[...]

    quarters = total.reshape(16, 4, 16, 128)
    lane_q = iota((256, 128), 1)

    def pack(first):
        packed = jnp.zeros((256, 128), f32)
        for q in range(4):
            turned = pltpu.roll(quarters[:, q].reshape(256, 128), (32 * q - first) % 128, 1)
            packed = jnp.where((lane_q >= 32 * q) & (lane_q < 32 * q + 32), turned, packed)
        return packed.reshape(16, 16, 128)

    def unpack(packed, first):
        return jnp.concatenate([pltpu.roll(packed, (first - 32 * q) % 128, 1) for q in range(4)], axis=0)

    part[...] = pack(0)
    part_xy[xy] = part[xy]
    s_start, s_arrive, s_left = over_xy(lambda p: part.at[p], part_xy, ps, pr)
    s_start()
    d_start, d_arrive, d_left = over_xy(lambda p: slopes.at[p], slopes_xy, ds, dr)

    qx_arrive()
    lots = [q_xy[2 * pair] + q_xy[2 * pair + 1] for pair in range(8)]
    pivot_row, pivot_col = forms(jnp.concatenate(lots, axis=0), lane)
    pivot_row = pivot_row.astype(bf16)
    pivot_col = pivot_col.astype(bf16)
    own_kernel = kernel_of(pivot_row, own_col)
    plane_kernel = kernel_of(pivot_col, xbuf[...].reshape(1024, 128))
    proj = exact(plane_kernel, acc[...])
    proj = jnp.where(lane < 32, proj, 0.0) + exact(own_kernel, noise_var * dir_t + pltpu.roll(res_t, 32, 1))
    l_own[...] = proj[0:32] + pltpu.roll(proj[32:64], 64, 1)
    l_copy = remote(l_own.at[given], l_sib, ls, lr)
    l_copy.start()

    line_kernel = kernel_of(pivot_row, colm[0])
    gram_part = exact(line_kernel, line_kernel, NT)
    wide = jnp.concatenate([gram_part, jnp.zeros((64, 64), f32)], axis=1)
    g_own[...] = wide[0:32] + pltpu.roll(wide[32:64], 64, 1)
    g_copy = remote(g_own.at[given], g_sib, gs, gr)
    g_copy.start()
    slopes[...] = pack(32)
    slopes_xy[xy] = slopes[xy]
    l_copy.wait()
    l_sum[...] = l_own[kept, :] + l_sib[...]
    l_xy[xy] = l_sum[...]
    l_start, l_arrive, l_left = over_xy(lambda p: l_sum, l_xy, lxs, lxr)
    l_start()
    own_kernel_t = kernel_of(own_row, pivot_col)
    pivot_self = kernel_of(pivot_row, pivot_col)
    g_copy.wait()
    g_sum[...] = g_own[kept, :] + g_sib[...]
    g_xy[xy] = g_sum[...]
    g_start, g_arrive, g_left = over_xy(lambda p: g_sum, g_xy, gxs, gxr)
    g_start()

    s_arrive()
    images = unpack(jnp.sum(part_xy[...], axis=0), 0)
    image = jnp.where(lane < 32, images + noise_var * dir_t, 0.0)
    sums = jnp.sum(
        dir_t * image
        + pltpu.roll(res_t * image, 32, 1)
        + pltpu.roll(image * image, 64, 1)
        + pltpu.roll(res_t * res_t, 96, 1),
        axis=0,
        keepdims=True,
    )
    e_own[...] = sums
    e_copy = remote(e_own, e_sib, es, er)
    e_copy.start()
    z_left()
    for copy in shared:
        copy.wait_send()
    x_left()
    q_left()
    qx_left()
    s_left()
    e_copy.wait()
    e_sum[...] = e_own[...] + e_sib[...]
    e_xy[xy] = e_sum[...]
    e_start, e_arrive, e_left = over_xy(lambda p: e_sum, e_xy, exs, exr)
    e_start()

    l_arrive()
    l_z[z] = jnp.sum(l_xy[...], axis=0)
    lz_start, lz_arrive, lz_left = along_z(l_z.at[z], l_z, lzs, lzr)
    lz_start()
    e_arrive()
    e_z[z] = jnp.sum(e_xy[...], axis=0)
    ez_start, ez_arrive, ez_left = along_z(e_z.at[z], e_z, ezs, ezr)
    ez_start()
    d_start()

    g_arrive()
    g_half[...] = jnp.sum(g_xy[...], axis=0)
    v_copy = remote(g_half, g_other, vs, vr)
    v_copy.start()
    g_left()
    l_left()
    v_copy.wait()
    gram = halves(g_half[...], g_other[...])
    own_self = jnp.concatenate([noise_var * pivot_self, jnp.zeros((64, 64), f32)], axis=1)
    work = jnp.where(lane < 64, gram + own_self, jnp.where(lane == line + 64, 1.0, 0.0))

    done = []
    for panel in range(8):
        count = 64 - 8 * panel
        below = iota((count, 128), 0)
        cols = [jnp.broadcast_to(work[:, 8 * panel + j : 8 * panel + j + 1], (count, 128)) for j in range(8)]
        for k in range(8):
            factor = jnp.where(below > k, cols[k] * (1.0 / cols[k][k : k + 1]), 0.0)
            work = work - factor * work[k : k + 1]
            for j in range(k + 1, 8):
                cols[j] = cols[j] - factor * cols[j][k : k + 1]
        done.append(work[0:8])
        work = work[8:]
    work = jnp.concatenate(done, axis=0)
    diagonal = jnp.sum(jnp.where(lane == line, work, 0.0), axis=1, keepdims=True)
    lower_inv = pltpu.roll(work, 64, 1)[:, 0:64] * lax.rsqrt(diagonal)
    gram_inv = exact(lower_inv.T, lower_inv)
    mapped = exact(own_kernel_t, gram_inv)

    e_left()
    d_arrive()
    d_left()
    slope = unpack(jnp.sum(slopes_xy[...], axis=0), 96)

    lz_arrive()
    l_half[...] = jnp.sum(l_z[...], axis=0)
    u_copy = remote(l_half, l_other, us, ur)
    u_copy.start()
    lz_left()
    u_copy.wait()
    projs = halves(l_half[...], l_other[...])
    solved = exact(gram_inv, projs)
    spread = exact(mapped, projs)

    def old(values):
        return pltpu.roll(values, 96, 1)

    proj_old = old(projs)
    solved_old = old(solved)
    spread_old = old(spread)
    removed_old = jnp.sum(proj_old * solved_old, axis=0, keepdims=True)

    ez_left()
    ez_arrive()
    curvature = jnp.sum(e_z[...], axis=0)
    cross = pltpu.roll(jnp.broadcast_to(curvature, (8, 128)), 96, 1)[0:1]
    square = pltpu.roll(jnp.broadcast_to(curvature, (8, 128)), 64, 1)[0:1]
    square_old = pltpu.roll(jnp.broadcast_to(curvature, (8, 128)), 32, 1)[0:1]
    norm_old = (square_old - removed_old) / noise_var
    step = norm_old / curvature
    residual_new = res_t - step * image
    proj_new = proj_old - step * projs
    solved_new = solved_old - step * solved
    square_new = square_old - 2.0 * step * cross + step * step * square
    norm_new = (square_new - jnp.sum(proj_new * solved_new, axis=0, keepdims=True)) / noise_var
    precond_new = (residual_new - (spread_old - step * spread)) / noise_var
    direction_new = precond_new + (norm_new / norm_old) * dir_t
    solution_new = sol_t + step * dir_t
    result[...] = jnp.where(
        lane < 32,
        solution_new,
        jnp.where(
            lane < 64,
            pltpu.roll(residual_new, 32, 1),
            jnp.where(lane < 96, pltpu.roll(direction_new, 64, 1), slope),
        ),
    )


def turn_kernel(result, sol_out, res_out, dir_out, slope_out, stage):
    stage[0:64, :] = result[...]
    stage[64:128, :] = jnp.zeros((64, 128), f32)
    turned = stage[...].T
    sol_out[...] = turned[0:32, 0:64]
    res_out[...] = turned[32:64, 0:64]
    dir_out[...] = turned[64:96, 0:64]
    slope_out[...] = turned[96:128, 0:64]


def local(features, inv_scale, pivots, solution, residual, direction):
    vmem = pltpu.VMEM
    dma = pltpu.SemaphoreType.DMA
    one = dma(())
    fold16 = vmem((16, 16, 128), f32)
    flat32 = vmem((32, 128), f32)
    flat16 = vmem((16, 128), f32)
    flat1 = vmem((1, 128), f32)
    scratch = [
        vmem((64, 64), bf16), vmem((1, 64), f32), vmem((1, 64), jnp.int32),
        vmem((32, 64), f32), vmem((32, 64), f32), vmem((32, 64), f32),
        vmem((128, 128), f32), vmem((128, 128), f32),
        vmem((2, 16, 48, 128), bf16), vmem((16, 64, 128), bf16),
        vmem((2, 1024, 128), bf16), vmem((1024, 128), f32),
        fold16, fold16, fold16, fold16,
        vmem((16, 1, 128), f32), vmem((8, 128), f32), vmem((8, 128), f32), vmem((16, 8, 128), f32),
        flat32, flat16, flat16, fold16, flat16, flat16,
        flat32, flat16, flat16, fold16, fold16, flat16, flat16,
        flat1, flat1, flat1, vmem((16, 1, 128), f32), vmem((16, 1, 128), f32),
        dma((6,)), one, dma((4,)), one, one, dma((3,)), dma((3,)), *[one] * 30,
    ]
    result = pl.pallas_call(
        step_kernel,
        name="cg_step",
        out_shape=jax.ShapeDtypeStruct((64, 128), f32),
        in_specs=[pl.BlockSpec(memory_space=pltpu.HBM)] * 6,
        out_specs=pl.BlockSpec(memory_space=vmem),
        scratch_shapes=scratch,
        compiler_params=pltpu.CompilerParams(
            collective_id=0, has_side_effects=True, vmem_limit_bytes=60 * 1024 * 1024
        ),
    )(features, inv_scale[None, :], pivots[None, :], solution, residual, direction)
    return pl.pallas_call(
        turn_kernel,
        name="turn",
        out_shape=(jax.ShapeDtypeStruct((32, 64), f32),) * 4,
        in_specs=[pl.BlockSpec(memory_space=vmem)],
        out_specs=(pl.BlockSpec(memory_space=vmem),) * 4,
        scratch_shapes=[vmem((128, 128), f32)],
    )(result)


def solution(mesh):
    split = P(None, ("row", "col"))
    return jax.shard_map(
        local,
        mesh=mesh,
        in_specs=(split, P(), P(), split, split, split),
        out_specs=(split,) * 4,
        check_vma=False,
    )
```
